32 devices in a mesh: gx: 4 (over x, core), gy: 8 (over z, y).
Axes of the slice: x: 2, y: 2, z: 4, core: 2. Of those that a mesh axis runs over, the one named last changes fastest.
Arguments:
- flux: float32 [8, 256, 2048], P(None, 'gx', 'gy'), may hold values from -6 to 6
- diffusivity: float32 [128, 1024], P('gx', 'gy'), may hold values from 0.08 to 0.24
- remap_bank: bfloat16 [16, 3, 256, 128], replicated, may hold values from -0.21875 to 0.21875
- rec_owner: int32 [4096], P(('gx', 'gy')), may hold values from 0 to 31, as said below
- rec_source: int32 [4096], P(('gx', 'gy')), may hold values from 0 to 63
- rec_target: int32 [4096], P(('gx', 'gy')), may hold values from 0 to 31
- rec_weight: int32 [4096], P(('gx', 'gy')), may hold values from 0 to 15
Outputs:
- ocean_state: float32 [8, 128, 1024], P(None, 'gx', 'gy')
The draws below stay inside these ranges and needn't reach their ends.
Inputs may be any that keep to these rules, and one draw needn't show every extreme that they name: `rec_owner`: among the records of one atmosphere block each owner appears at most 8 times; in every draw some owner appears exactly 8 times in every block's records.
All inputs are finite; a program needn't handle non-finite values.
Results may differ from the reference program's by a relative error of at most 0.0029.
Values may be sent and summed in bfloat16 or wider, within the bound.
A program may use at most 64 MiB of HBM per device.

```python
import math
import jax
import jax.numpy as jnp
from jax import lax

F = 8
TILE_X = 16
TILE_Y = 16
OTILE_X = 8
OTILE_Y = 16
NWB = 16
SWEEPS = 4
AXD = 64
AYD = 256
TC = 256
OC = 128
OXD = 32
OYD = 128
AX = 256
AY = 2048
OX = 128
OY = 1024
ST = 64
OT = 32
RECS = 128
OWNERS = 32
CAP = 8
RECORDS = 4096
N_GY = 8


def draw_rec_owner(key, part):
    slot_count = OWNERS * CAP
    bias_key, hot_key, source_key = jax.random.split(jax.random.fold_in(key, 11), 3)
    bias = jax.random.randint(bias_key, (OWNERS,), 0, 4)
    hot_owner = jax.random.randint(hot_key, (), 0, OWNERS)
    owner_of = jnp.arange(slot_count, dtype=jnp.int32) // CAP

    def one_source(index):
        noise_key, order_key = jax.random.split(jax.random.fold_in(source_key, index))
        noise = jax.random.randint(noise_key, (slot_count,), 0, 4096)
        lifted = jnp.where(owner_of == hot_owner, 65536, 0)
        score = (bias[owner_of] * 1024 + noise + lifted) * slot_count + jnp.arange(slot_count, dtype=jnp.int32)
        chosen = jnp.argsort(-score)[:RECS]
        picked = owner_of[chosen]
        return picked[jax.random.permutation(order_key, RECS)]
    return jax.vmap(one_source)(jnp.arange(OWNERS)).reshape(-1).astype(jnp.int32)


def plant(result, key, least, largest):
    longest = result.shape.index(max(result.shape))
    spots = []
    for shift in (0, 1):
        where = [jax.random.randint(jax.random.fold_in(key, axis), (), 0, length) for axis, length in enumerate(result.shape)]
        where[longest] = (where[longest] + shift) % result.shape[longest]
        spots.append(tuple(where))
    return result.at[spots[0]].set(least).at[spots[1]].set(largest)


def levels(own_key, extent, cuts, low, largest):
    loudness = 1.0
    for axis_at, blocks in cuts:
        draws = jax.random.uniform(jax.random.fold_in(jax.random.fold_in(own_key, 6), axis_at), (blocks,), jnp.float32, low / len(cuts), largest / len(cuts))
        loudness = loudness * jnp.repeat(jnp.exp(draws), extent[axis_at] // blocks).reshape((-1,) + (1,) * (len(extent) - 1 - axis_at))
    return loudness


def normal_values(key, shape, spread, limit, cuts=(), kind=jnp.bfloat16):
    array = jax.random.normal(key, shape, jnp.float32) * spread
    if len(cuts) > 0:
        array = levels(key, shape, cuts, -0.22, 0.18) * array
    return jnp.clip(array, min=-limit, max=limit).astype(kind)


def setup_inputs(seed: int = 0) -> dict:
    splits = jax.random.split(jax.random.key(seed), 8)
    return {
        "flux": normal_values(splits[0], (F, AX, AY), 1.0, 6.0, ((1, 4), (2, 8)), jnp.float32),
        "diffusivity": jnp.clip(jnp.exp(math.log(0.24) - 1.0986123 * jax.random.uniform(splits[1], (OX, OY), jnp.float32) ** levels(splits[1], (OX, OY), ((0, 4), (1, 8)), -0.2, 0.2)), 0.08, 0.24),
        "remap_bank": normal_values(splits[2], (NWB, 3, TC, OC), (3 * TC) ** -0.5, 0.21875),
        "rec_owner": draw_rec_owner(jax.random.fold_in(splits[7], 71), 0),
        "rec_source": plant(jax.random.randint(splits[4], (RECORDS,), 0, ST), jax.random.fold_in(splits[4], 1), 0, ST - 1).astype(jnp.int32),
        "rec_target": plant(jax.random.randint(splits[5], (RECORDS,), 0, OT), jax.random.fold_in(splits[5], 1), 0, OT - 1).astype(jnp.int32),
        "rec_weight": plant(jax.random.randint(splits[6], (RECORDS,), 0, NWB), jax.random.fold_in(splits[6], 1), 0, NWB - 1).astype(jnp.int32),
    }


def reference(flux, diffusivity, remap_bank, rec_owner, rec_source, rec_target, rec_weight):
    slope_x = (jnp.roll(flux, -1, 1) - jnp.roll(flux, 1, 1)) * 0.5
    slope_y = (jnp.roll(flux, -1, 2) - jnp.roll(flux, 1, 2)) * 0.5
    coeffs = jnp.stack([flux, slope_x, slope_y]).astype(jnp.bfloat16)
    grid_tx = AX // TILE_X
    grid_ty = AY // TILE_Y
    all_tiles = coeffs.reshape(3, F, grid_tx, TILE_X, grid_ty, TILE_Y)
    all_tiles = all_tiles.transpose(2, 4, 0, 1, 3, 5).reshape(grid_tx * grid_ty, 3, F, TC)
    source_block = jnp.arange(RECORDS, dtype=jnp.int32) // RECS
    per_row = AYD // TILE_Y
    tile_i = (source_block // N_GY) * (AXD // TILE_X) + rec_source // per_row
    tile_j = (source_block % N_GY) * per_row + rec_source % per_row
    source_id = (tile_i * grid_ty + tile_j).astype(jnp.int32)
    ocean_tx = OX // OTILE_X
    ocean_ty = OY // OTILE_Y
    ocean_row = OYD // OTILE_Y
    target_i = (rec_owner // N_GY) * (OXD // OTILE_X) + rec_target // ocean_row
    target_j = (rec_owner % N_GY) * ocean_row + rec_target % ocean_row
    target_id = (target_i * ocean_ty + target_j).astype(jnp.int32)
    group_size = math.gcd(RECORDS, 64)
    block_count = RECORDS // group_size

    def accumulate(total, pieces):
        src_ids, weight_ids, dest_ids = pieces
        source_part = all_tiles[src_ids].astype(jnp.float32)
        bank_part = remap_bank[weight_ids].astype(jnp.float32)
        contribution = jnp.einsum("gkfc,gkco->gfo", source_part, bank_part, precision=lax.Precision.HIGHEST)
        return total.at[dest_ids].add(contribution), None

    start_total = jnp.zeros((ocean_tx * ocean_ty, F, OC), jnp.float32)
    forcing_tiles, unused = lax.scan(accumulate, start_total, (source_id.reshape(block_count, group_size), rec_weight.reshape(block_count, group_size), target_id.reshape(block_count, group_size)))
    forcing = forcing_tiles.reshape(ocean_tx, ocean_ty, F, OTILE_X, OTILE_Y)
    ocean = forcing.transpose(2, 0, 3, 1, 4).reshape(F, OX, OY)
    for sweep in range(SWEEPS):
        padded = jnp.pad(ocean, ((0, 0), (1, 1), (1, 1)))
        beside_all = padded[:, 2:, 1:-1] + padded[:, :-2, 1:-1] + padded[:, 1:-1, 2:] + padded[:, 1:-1, :-2]
        ocean = ocean + diffusivity * (beside_all - 4.0 * ocean)
    return ocean
```

```python
import functools

import jax
import jax.numpy as jnp
from jax import lax
from jax.experimental import pallas as pl
from jax.experimental.pallas import tpu as pltpu
from jax.sharding import PartitionSpec as P

TILE_X = 16
TILE_Y = 16
OTILE_X = 8
OTILE_Y = 16
SWEEPS = 4
LANES = 128
MESH = pl.DeviceIdType.MESH


def lane_of(shape):
    return lax.broadcasted_iota(jnp.int32, shape, len(shape) - 1)


def block_transpose(parts, width):
    parts = list(parts)
    block = lane_of(parts[0].shape) // width
    step = 1
    while step < len(parts):
        keep = (block & step) == 0
        for i in range(len(parts)):
            if i & step == 0:
                j = i | step
                low, high = parts[i], parts[j]
                parts[i] = jnp.where(keep, low, pltpu.roll(high, step * width, 1))
                parts[j] = jnp.where(keep, pltpu.roll(low, LANES - step * width, 1), high)
        step *= 2
    return parts


def kernel(
    nx, ny, cap,
    flux, diff, bank, own, src, tgt, wgt,
    out,
    bank_v, xs, xmat, prod, table_v, table_s, meta_s, meta_r, sent, got,
    row_s, row_r, col_s, col_r, d_edge, d_corner, d_row, u, pack_s, u_edge, u_corner, u_row,
    bank_sem, table_sem, a_send, a_recv, m_send, m_recv, h_send, h_recv,
):
    n = nx * ny
    fields, rows, cols = flux.shape
    nwb = bank.shape[0]
    tiles_x, tiles_y = rows // TILE_X, cols // TILE_Y
    tiles = tiles_x * tiles_y
    orows = diff.shape[0]
    oty = diff.shape[1] // OTILE_Y
    otx = orows // OTILE_X
    span = cap * fields
    gx, gy = lax.axis_index("gx"), lax.axis_index("gy")
    me = gx * ny + gy
    up, down = lax.rem(gx + nx - 1, nx), lax.rem(gx + 1, nx)
    left, right = lax.rem(gy + ny - 1, ny), lax.rem(gy + 1, ny)

    barrier = pltpu.get_barrier_semaphore()

    def greet(k, c):
        d = lax.rem(me + k, n)
        pl.semaphore_signal(barrier, inc=1, device_id=(d // ny, lax.rem(d, ny)), device_id_type=MESH)
        return c

    lax.fori_loop(1, n, greet, 0)
    bank_copy = pltpu.make_async_copy(bank, bank_v, bank_sem)
    bank_copy.start()

    records = own.shape[1]
    owner_i = lax.broadcasted_iota(jnp.int32, (n, records), 0)
    member = own[...] == owner_i
    lower = lax.broadcasted_iota(jnp.int32, (records, records), 0) < lane_of((records, records))
    before = jnp.dot(
        member.astype(jnp.bfloat16), lower.astype(jnp.bfloat16), preferred_element_type=jnp.float32
    )
    source, target = src[...], tgt[...]
    code = (wgt[...] * tiles + lax.rem(source, tiles_y) * tiles_x + source // tiles_y).astype(jnp.float32)
    aim = (lax.rem(target, oty) * (fields * otx) + target // oty).astype(jnp.float32)
    lane = lane_of((n, LANES))
    slot_lane = lax.rem(lane, span) // fields
    field_lane = (lax.rem(lane, fields) * otx).astype(jnp.float32)
    table = jnp.zeros((n, LANES), jnp.float32)
    meta = jnp.full((n, LANES), -1.0, jnp.float32)
    for k in range(cap):
        hit = jnp.logical_and(member, before == k)
        code_k = jnp.sum(jnp.where(hit, code, 0.0), axis=1, keepdims=True)
        aim_k = jnp.sum(jnp.where(hit, aim + 1.0, 0.0), axis=1, keepdims=True) - 1.0
        table = jnp.where(lane == k, code_k, table)
        filled = jnp.where(aim_k >= 0.0, aim_k + field_lane, -1.0)
        meta = jnp.where(slot_lane == k, filled, meta)
    table_v[...] = table.astype(jnp.int32)
    table_copy = pltpu.make_async_copy(table_v, table_s, table_sem)
    table_copy.start()
    for o in range(n):
        meta_s[o] = meta[o : o + 1, :]
    meta_r[me] = meta_s[me]

    for f in range(fields):
        for h in range(2):
            xs[0, h, f * rows : (f + 1) * rows, :] = flux[f, :, h * LANES : (h + 1) * LANES]
    lane_c = lane_of((rows, LANES))
    first = jnp.zeros((rows, LANES), jnp.float32)
    last = jnp.zeros((rows, LANES), jnp.float32)
    for f in range(fields):
        a = flux[f, :, 0:LANES]
        b = flux[f, :, cols - LANES : cols]
        first = jnp.where(lane_c == f, pltpu.roll(a, f, 1) if f else a, first)
        last = jnp.where(lane_c == f, pltpu.roll(b, f + 1, 1), last)
    col_s[0] = first
    col_s[1] = last
    for h in range(2):
        row_s[0, h] = xs[0, h, pl.ds(0, fields, stride=rows), :]
        row_s[1, h] = xs[0, h, pl.ds(rows - 1, fields, stride=rows), :]

    pl.semaphore_wait(barrier, n - 1)

    def remote(a, b, k, x, y):
        return pltpu.make_async_remote_copy(
            src_ref=a, dst_ref=b, send_sem=h_send.at[k], recv_sem=h_recv.at[k],
            device_id=(x, y), device_id_type=MESH,
        )

    flux_copies = [
        remote(row_s.at[0], row_r.at[1], 0, up, gy),
        remote(row_s.at[1], row_r.at[0], 1, down, gy),
        remote(col_s.at[0], col_r.at[1], 2, gx, left),
        remote(col_s.at[1], col_r.at[0], 3, gx, right),
    ]
    for c in flux_copies:
        c.start()

    def halo_copies(base, edge0, edge1, row0, row1, edge, corner, row):
        low = pl.ds(0, 8)
        high = pl.ds(orows - 8, 8)
        return [
            remote(edge0, edge.at[1], base, gx, left),
            remote(edge1, edge.at[0], base + 1, gx, right),
            remote(row0, row.at[1], base + 2, up, gy),
            remote(row1, row.at[0], base + 3, down, gy),
            remote(edge0.at[low], corner.at[1, 1], base + 4, up, left),
            remote(edge0.at[high], corner.at[0, 1], base + 5, down, left),
            remote(edge1.at[low], corner.at[1, 0], base + 6, up, right),
            remote(edge1.at[high], corner.at[0, 0], base + 7, down, right),
        ]

    diff_copies = halo_copies(
        4, diff, diff, diff.at[pl.ds(0, 8)], diff.at[pl.ds(orows - 8, 8)], d_edge, d_corner, d_row
    )
    for c in diff_copies:
        c.start()

    def meta_to(d):
        return pltpu.make_async_remote_copy(
            src_ref=meta_s.at[d], dst_ref=meta_r.at[me], send_sem=m_send.at[d], recv_sem=m_recv.at[me],
            device_id=(d // ny, lax.rem(d, ny)), device_id_type=MESH,
        )

    def data_to(d):
        return pltpu.make_async_remote_copy(
            src_ref=sent.at[d], dst_ref=got.at[me], send_sem=a_send.at[d], recv_sem=a_recv.at[me],
            device_id=(d // ny, lax.rem(d, ny)), device_id_type=MESH,
        )

    def send_meta(k, c):
        meta_to(lax.rem(me + k, n)).start()
        return c

    lax.fori_loop(1, n, send_meta, 0)

    for c in flux_copies:
        c.wait()
    row_i = lax.broadcasted_iota(jnp.int32, (rows, LANES), 0)
    for f in range(fields):
        halves = [flux[f, :, h * LANES : (h + 1) * LANES] for h in range(2)]
        ends = (
            pltpu.roll(col_r[0], LANES - f, 1) if f else col_r[0],
            pltpu.roll(col_r[1], LANES - 1 - f, 1),
        )
        to_right = [pltpu.roll(x, 1, 1) for x in halves]
        to_left = [pltpu.roll(x, LANES - 1, 1) for x in halves]
        at_first, at_last = lane_c == 0, lane_c == LANES - 1
        before_y = [jnp.where(at_first, ends[0], to_right[0]), jnp.where(at_first, to_right[0], to_right[1])]
        after_y = [jnp.where(at_last, to_left[1], to_left[0]), jnp.where(at_last, ends[1], to_left[1])]
        for h in range(2):
            x = halves[h]
            above = jnp.where(row_i == 0, row_r[0, h, f : f + 1, :], pltpu.roll(x, 1, 0))
            below = jnp.where(row_i == rows - 1, row_r[1, h, f : f + 1, :], pltpu.roll(x, rows - 1, 0))
            xs[1, h, f * rows : (f + 1) * rows, :] = (below - above) * 0.5
            xs[2, h, f * rows : (f + 1) * rows, :] = (after_y[h] - before_y[h]) * 0.5

    per = LANES // TILE_Y
    halfx = TILE_X // per
    tile_rows = tiles_x * fields
    for c in range(3):
        for h in range(2):
            for g in range(halfx):
                parts = [
                    jnp.concatenate(
                        [
                            xs[c, h, pl.ds(t * TILE_X + g * per + a, fields, stride=rows), :]
                            for t in range(tiles_x)
                        ],
                        axis=0,
                    )
                    for a in range(per)
                ]
                parts = block_transpose(parts, TILE_Y)
                at = (c * halfx + g) * LANES
                for t in range(per):
                    j = h * per + t
                    xmat[j * tile_rows : (j + 1) * tile_rows, at : at + LANES] = parts[t].astype(jnp.bfloat16)

    bank_copy.wait()

    def products(p, c):
        pair = jnp.concatenate([bank_v[2 * p], bank_v[2 * p + 1]], axis=1)
        got_pair = jnp.dot(xmat[...], pair, preferred_element_type=jnp.float32)
        prod[pl.ds(2 * p * tiles, tiles)] = got_pair[:, :LANES].reshape(tiles, fields, LANES)
        prod[pl.ds((2 * p + 1) * tiles, tiles)] = got_pair[:, LANES:].reshape(tiles, fields, LANES)
        return c

    lax.fori_loop(0, nwb // 2, products, 0)
    table_copy.wait()

    def record(d, s):
        return prod[jnp.clip(table_s[d, s], 0, nwb * tiles - 1)]

    def fill(d, ref):
        for s in range(0, cap, 2):
            pair = jnp.concatenate([record(d, s), record(d, s + 1)], axis=0)
            ref[d, s * fields : (s + 2) * fields, :] = pair.astype(jnp.bfloat16)

    def send_data(k, c):
        d = lax.rem(me + k, n)
        fill(d, sent)
        data_to(d).start()
        return c

    lax.fori_loop(1, n, send_data, 0)
    fill(me, got)

    group = max(1, 2 * LANES // span)
    cells = fields * otx * oty
    shares = LANES // span
    cell_i = lax.broadcasted_iota(jnp.int32, (cells, LANES), 0).astype(jnp.float32)
    part_lane = lane_of((1, LANES)) // span

    def collect(q, total):
        def arrive(i, c):
            s = q * group + i

            @pl.when(s != me)
            def _():
                pltpu.make_async_remote_copy(
                    src_ref=meta_s.at[s], dst_ref=meta_r.at[s], send_sem=m_send.at[s], recv_sem=m_recv.at[s],
                    device_id=(s // ny, lax.rem(s, ny)), device_id_type=MESH,
                ).wait_recv()
                pltpu.make_async_remote_copy(
                    src_ref=sent.at[s], dst_ref=got.at[s], send_sem=a_send.at[s], recv_sem=a_recv.at[s],
                    device_id=(s // ny, lax.rem(s, ny)), device_id_type=MESH,
                ).wait_recv()

            return c

        lax.fori_loop(0, group, arrive, 0)
        hots = []
        for b in range(group // shares):
            aims = meta_r[q * group + b * shares]
            for i in range(1, shares):
                aims = jnp.where(part_lane == i, meta_r[q * group + b * shares + i], aims)
            hots.append(jnp.where(cell_i == aims, 1.0, 0.0).astype(jnp.bfloat16))
        hot = jnp.concatenate(hots, axis=1)
        data = got[pl.ds(q * group, group)].reshape(group * span, LANES)
        return total + jnp.dot(hot, data, preferred_element_type=jnp.float32)

    total = lax.fori_loop(0, n // group, collect, jnp.zeros((cells, LANES), jnp.float32))
    high = fields * otx
    parts = block_transpose([total[t * high : (t + 1) * high, :] for t in range(oty)], OTILE_Y)
    for a in range(OTILE_X):
        u[pl.ds(a, high, stride=OTILE_X), :] = parts[a]

    lane_o = lane_of((orows, LANES))
    packed = [jnp.zeros((orows, LANES), jnp.float32) for _ in range(2)]
    for f in range(fields):
        block = u[f * orows : (f + 1) * orows, :]
        shift = f * SWEEPS
        rolled = (pltpu.roll(block, shift, 1), pltpu.roll(block, LANES - shift, 1)) if f else (block, block)
        mine = (lane_o // SWEEPS == f, (LANES - 1 - lane_o) // SWEEPS == f)
        packed = [jnp.where(mine[e], rolled[e], packed[e]) for e in range(2)]
        pack_s[2, f * 8 : f * 8 + 8, :] = block[0:8]
        pack_s[3, f * 8 : f * 8 + 8, :] = block[orows - 8 : orows]
    pack_s[0, 0:orows, :] = packed[0]
    pack_s[1, 0:orows, :] = packed[1]
    ocean_copies = halo_copies(
        12,
        pack_s.at[0, pl.ds(0, orows)],
        pack_s.at[1, pl.ds(0, orows)],
        pack_s.at[2, pl.ds(0, fields * 8)],
        pack_s.at[3, pl.ds(0, fields * 8)],
        u_edge, u_corner, u_row,
    )
    for c in ocean_copies:
        c.start()

    for c in diff_copies:
        c.wait()

    has = (gx > 0, gx < nx - 1, gy > 0, gy < ny - 1)
    tail_lane = lane_of((8, LANES)) < LANES // 2
    tail_row = lax.broadcasted_iota(jnp.int32, (8, LANES), 0) < 4
    wide_lane = lane_o < LANES // 2
    row_ok = jnp.where(tail_row, has[1].astype(jnp.float32), has[0].astype(jnp.float32))
    col_ok = jnp.where(wide_lane, has[3].astype(jnp.float32), has[2].astype(jnp.float32))
    both_ok = row_ok * col_ok[0:8]
    d_tail = jnp.where(tail_row, d_row[1], d_row[0]) * row_ok
    d_side = jnp.where(wide_lane, d_edge[1], d_edge[0]) * col_ok
    d_both = (
        jnp.where(
            tail_lane,
            jnp.where(tail_row, d_corner[1, 1], d_corner[0, 1]),
            jnp.where(tail_row, d_corner[1, 0], d_corner[0, 0]),
        )
        * both_ok
    )
    d = [
        jnp.concatenate([diff[...], d_tail], axis=0),
        jnp.concatenate([d_side, d_both], axis=0),
    ]
    for c in ocean_copies:
        c.wait()
    side = [
        jnp.concatenate([u_edge[e], jnp.where(tail_row, u_corner[1, e], u_corner[0, e])], axis=0)
        for e in range(2)
    ]
    ext = orows + 8
    lane_e = lane_of((ext, LANES))
    side_ok = jnp.concatenate([col_ok, both_ok], axis=0)
    at_first, at_last = lane_e == 0, lane_e == LANES - 1
    for f in range(fields):
        shift = f * SWEEPS
        tail = jnp.where(tail_row, u_row[1, f * 8 : f * 8 + 8, :], u_row[0, f * 8 : f * 8 + 8, :]) * row_ok
        rolled = (
            (pltpu.roll(side[1], LANES - shift, 1), pltpu.roll(side[0], shift, 1)) if f else (side[1], side[0])
        )
        x = [
            jnp.concatenate([u[f * orows : (f + 1) * orows, :], tail], axis=0),
            jnp.where(lane_e < LANES // 2, rolled[0], rolled[1]) * side_ok,
        ]
        for sweep in range(SWEEPS):
            to_right = [pltpu.roll(v, 1, 1) for v in x]
            to_left = [pltpu.roll(v, LANES - 1, 1) for v in x]
            beside = [
                jnp.where(at_first, to_right[1 - h], to_right[h])
                + jnp.where(at_last, to_left[1 - h], to_left[h])
                + pltpu.roll(x[h], 1, 0)
                + pltpu.roll(x[h], ext - 1, 0)
                for h in range(2)
            ]
            x = [x[h] + d[h] * (beside[h] - 4.0 * x[h]) for h in range(2)]
        out[f] = x[0][0:orows, :]

    def settle(k, c):
        t = lax.rem(me + k, n)
        meta_to(t).wait_send()
        data_to(t).wait_send()
        return c

    lax.fori_loop(1, n, settle, 0)


def local(nx, ny, flux, diffusivity, remap_bank, rec_owner, rec_source, rec_target, rec_weight):
    n = nx * ny
    fields, rows, cols = flux.shape
    orows, ocols = diffusivity.shape
    records = rec_owner.shape[0]
    cap = max(2, 2 * records // n)
    nwb = remap_bank.shape[0]
    depth = 3 * TILE_X * TILE_Y
    tiles = rows // TILE_X * (cols // TILE_Y)
    span = cap * fields
    f32, bf16 = jnp.float32, jnp.bfloat16
    v = pltpu.VMEM
    dma = pltpu.SemaphoreType.DMA
    vm = pl.BlockSpec(memory_space=pltpu.VMEM)
    flat = [x.reshape(1, records) for x in (rec_owner, rec_source, rec_target, rec_weight)]
    return pl.pallas_call(
        functools.partial(kernel, nx, ny, cap),
        out_shape=jax.ShapeDtypeStruct((fields, orows, ocols), f32),
        in_specs=[vm, vm, pl.BlockSpec(memory_space=pl.ANY)] + [vm] * 4,
        out_specs=vm,
        scratch_shapes=[
            v((nwb, depth, LANES), bf16),
            v((3, 2, (fields + 1) * rows, LANES), f32),
            v((tiles * fields, depth), bf16),
            v((nwb * tiles, fields, LANES), f32),
            v((n, LANES), jnp.int32),
            pltpu.SMEM((n, LANES), jnp.int32),
            v((n, 1, LANES), f32),
            v((n, 1, LANES), f32),
            v((n, span, LANES), bf16),
            v((n, span, LANES), bf16),
            v((2, 2, fields, LANES), f32),
            v((2, 2, fields, LANES), f32),
            v((2, rows, LANES), f32),
            v((2, rows, LANES), f32),
            v((2, orows, LANES), f32),
            v((2, 2, 8, LANES), f32),
            v((2, 8, LANES), f32),
            v((fields * orows + OTILE_X, LANES), f32),
            v((4, max(orows, fields * 8), LANES), f32),
            v((2, orows, LANES), f32),
            v((2, 2, 8, LANES), f32),
            v((2, fields * 8, LANES), f32),
            dma, dma,
            dma((n,)), dma((n,)), dma((n,)), dma((n,)),
            dma((20,)), dma((20,)),
        ],
        compiler_params=pltpu.CompilerParams(
            collective_id=0, has_side_effects=True, vmem_limit_bytes=40 * 1024 * 1024
        ),
    )(flux, diffusivity, remap_bank.reshape(nwb, depth, LANES), *flat)


def solution(mesh):
    in_specs = (
        P(None, "gx", "gy"),
        P("gx", "gy"),
        P(),
        P(("gx", "gy")),
        P(("gx", "gy")),
        P(("gx", "gy")),
        P(("gx", "gy")),
    )
    out_specs = P(None, "gx", "gy")
    body = functools.partial(local, mesh.shape["gx"], mesh.shape["gy"])
    return jax.shard_map(body, mesh=mesh, in_specs=in_specs, out_specs=out_specs, check_vma=False)
```

```python
import functools

import jax
import jax.numpy as jnp
from jax import lax
from jax.experimental import pallas as pl
from jax.experimental.pallas import tpu as pltpu
from jax.sharding import PartitionSpec as P

TILE_X = 16
TILE_Y = 16
OTILE_X = 8
OTILE_Y = 16
SWEEPS = 4
LANES = 128
MESH = pl.DeviceIdType.MESH


def lane_of(shape):
    return lax.broadcasted_iota(jnp.int32, shape, len(shape) - 1)


def block_transpose(parts, width):
    parts = list(parts)
    block = lane_of(parts[0].shape) // width
    step = 1
    while step < len(parts):
        keep = (block & step) == 0
        for i in range(len(parts)):
            if i & step == 0:
                j = i | step
                low, high = parts[i], parts[j]
                parts[i] = jnp.where(keep, low, pltpu.roll(high, step * width, 1))
                parts[j] = jnp.where(keep, pltpu.roll(low, LANES - step * width, 1), high)
        step *= 2
    return parts


def kernel(
    nx, ny, cap,
    flux_h, diff_h, bank, own_h, src_h, tgt_h, wgt_h,
    out,
    flux, diff, recs, in_sem,
    bank_v, xs, xmat, prod, table_v, table_s, meta_s, meta_r, sent, got,
    row_s, row_r, col_s, col_r, d_edge, d_corner, d_row, u, pack_s, u_edge, u_corner, u_row,
    bank_sem, table_sem, a_send, a_recv, m_send, m_recv, h_send, h_recv,
):
    n = nx * ny
    fields, rows, cols = flux.shape
    nwb = bank.shape[0]
    tiles_x, tiles_y = rows // TILE_X, cols // TILE_Y
    tiles = tiles_x * tiles_y
    orows = diff.shape[0]
    oty = diff.shape[1] // OTILE_Y
    otx = orows // OTILE_X
    span = cap * fields
    gx, gy = lax.axis_index("gx"), lax.axis_index("gy")
    me = gx * ny + gy
    up, down = lax.rem(gx + nx - 1, nx), lax.rem(gx + 1, nx)
    left, right = lax.rem(gy + ny - 1, ny), lax.rem(gy + 1, ny)

    barrier = pltpu.get_barrier_semaphore()

    y_order = [o for k in range(ny // 2 + 1) for o in sorted({ny // 2 - k, ny // 2 + k}) if o < ny]
    y_at = [gy if o == 0 else lax.rem(gy + o, ny) for o in y_order]

    def each_other(act):
        def one_row(i, c):
            x = lax.rem(gx + i, nx)
            for o, y in zip(y_order, y_at):
                if o:
                    act(x, y)
                else:
                    pl.when(i != 0)(functools.partial(act, x, y))
            return c

        lax.fori_loop(0, nx, one_row, 0)

    ins = [pltpu.make_async_copy(flux_h, flux, in_sem.at[0]), pltpu.make_async_copy(diff_h, diff, in_sem.at[1])]
    ins += [
        pltpu.make_async_copy(r, recs.at[i], in_sem.at[2 + i]) for i, r in enumerate((own_h, src_h, tgt_h, wgt_h))
    ]
    for c in ins:
        c.start()
    bank_copy = pltpu.make_async_copy(bank, bank_v, bank_sem)
    bank_copy.start()

    def greet(x, y):
        pl.semaphore_signal(barrier, inc=1, device_id=(x, y), device_id_type=MESH)

    each_other(greet)

    ins[0].wait()
    for f in range(fields):
        for h in range(2):
            xs[0, h, f * rows : (f + 1) * rows, :] = flux[f, :, h * LANES : (h + 1) * LANES]
    lane_c = lane_of((rows, LANES))
    first = jnp.zeros((rows, LANES), jnp.float32)
    last = jnp.zeros((rows, LANES), jnp.float32)
    for f in range(fields):
        a = flux[f, :, 0:LANES]
        b = flux[f, :, cols - LANES : cols]
        first = jnp.where(lane_c == f, pltpu.roll(a, f, 1) if f else a, first)
        last = jnp.where(lane_c == f, pltpu.roll(b, f + 1, 1), last)
    col_s[0] = first
    col_s[1] = last
    for h in range(2):
        row_s[0, h] = xs[0, h, pl.ds(0, fields, stride=rows), :]
        row_s[1, h] = xs[0, h, pl.ds(rows - 1, fields, stride=rows), :]

    ins[1].wait()
    pl.semaphore_wait(barrier, n - 1)

    def remote(a, b, k, x, y):
        return pltpu.make_async_remote_copy(
            src_ref=a, dst_ref=b, send_sem=h_send.at[k], recv_sem=h_recv.at[k],
            device_id=(x, y), device_id_type=MESH,
        )

    flux_copies = [
        remote(row_s.at[0], row_r.at[1], 0, up, gy),
        remote(row_s.at[1], row_r.at[0], 1, down, gy),
        remote(col_s.at[0], col_r.at[1], 2, gx, left),
        remote(col_s.at[1], col_r.at[0], 3, gx, right),
    ]
    for c in flux_copies:
        c.start()

    def halo_copies(base, edge0, edge1, row0, row1, edge, corner, row):
        low = pl.ds(0, 8)
        high = pl.ds(orows - 8, 8)
        return [
            remote(edge0, edge.at[1], base, gx, left),
            remote(edge1, edge.at[0], base + 1, gx, right),
            remote(row0, row.at[1], base + 2, up, gy),
            remote(row1, row.at[0], base + 3, down, gy),
            remote(edge0.at[low], corner.at[1, 1], base + 4, up, left),
            remote(edge0.at[high], corner.at[0, 1], base + 5, down, left),
            remote(edge1.at[low], corner.at[1, 0], base + 6, up, right),
            remote(edge1.at[high], corner.at[0, 0], base + 7, down, right),
        ]

    diff_copies = halo_copies(
        4, diff, diff, diff.at[pl.ds(0, 8)], diff.at[pl.ds(orows - 8, 8)], d_edge, d_corner, d_row
    )
    for c in diff_copies:
        c.start()

    for c in ins[2:]:
        c.wait()
    records = recs.shape[2]
    owner_i = lax.broadcasted_iota(jnp.int32, (n, records), 0)
    member = recs[0] == owner_i
    lower = lax.broadcasted_iota(jnp.int32, (records, records), 0) < lane_of((records, records))
    before = jnp.dot(
        member.astype(jnp.bfloat16), lower.astype(jnp.bfloat16), preferred_element_type=jnp.float32
    )
    source, target = recs[1], recs[2]
    code = (recs[3] * tiles + lax.rem(source, tiles_y) * tiles_x + source // tiles_y).astype(jnp.float32)
    aim = (lax.rem(target, oty) * (fields * otx) + target // oty).astype(jnp.float32)
    lane = lane_of((n, LANES))
    slot_lane = lax.rem(lane, span) // fields
    field_lane = (lax.rem(lane, fields) * otx).astype(jnp.float32)
    table = jnp.zeros((n, LANES), jnp.float32)
    meta = jnp.full((n, LANES), -1.0, jnp.float32)
    for k in range(cap):
        hit = jnp.logical_and(member, before == k)
        code_k = jnp.sum(jnp.where(hit, code, 0.0), axis=1, keepdims=True)
        aim_k = jnp.sum(jnp.where(hit, aim + 1.0, 0.0), axis=1, keepdims=True) - 1.0
        table = jnp.where(lane == k, code_k, table)
        filled = jnp.where(aim_k >= 0.0, aim_k + field_lane, -1.0)
        meta = jnp.where(slot_lane == k, filled, meta)
    table_v[...] = table.astype(jnp.int32)
    table_copy = pltpu.make_async_copy(table_v, table_s, table_sem)
    table_copy.start()
    for o in range(n):
        meta_s[o] = meta[o : o + 1, :]
    meta_r[me] = meta_s[me]

    def meta_to(x, y):
        d = x * ny + y
        return pltpu.make_async_remote_copy(
            src_ref=meta_s.at[d], dst_ref=meta_r.at[me], send_sem=m_send.at[d], recv_sem=m_recv.at[me],
            device_id=(x, y), device_id_type=MESH,
        )

    def data_to(x, y):
        d = x * ny + y
        return pltpu.make_async_remote_copy(
            src_ref=sent.at[d], dst_ref=got.at[me], send_sem=a_send.at[d], recv_sem=a_recv.at[me],
            device_id=(x, y), device_id_type=MESH,
        )

    each_other(lambda x, y: meta_to(x, y).start())

    per = LANES // TILE_Y
    halfx = TILE_X // per
    tile_rows = tiles_x * fields
    def spread(c):
        for h in range(2):
            for g in range(halfx):
                parts = [
                    jnp.concatenate(
                        [
                            xs[c, h, pl.ds(t * TILE_X + g * per + a, fields, stride=rows), :]
                            for t in range(tiles_x)
                        ],
                        axis=0,
                    )
                    for a in range(per)
                ]
                parts = block_transpose(parts, TILE_Y)
                at = (c * halfx + g) * LANES
                for t in range(per):
                    j = h * per + t
                    xmat[j * tile_rows : (j + 1) * tile_rows, at : at + LANES] = parts[t].astype(jnp.bfloat16)

    spread(0)

    for c in flux_copies:
        c.wait()
    row_i = lax.broadcasted_iota(jnp.int32, (rows, LANES), 0)
    for f in range(fields):
        halves = [flux[f, :, h * LANES : (h + 1) * LANES] for h in range(2)]
        ends = (
            pltpu.roll(col_r[0], LANES - f, 1) if f else col_r[0],
            pltpu.roll(col_r[1], LANES - 1 - f, 1),
        )
        to_right = [pltpu.roll(x, 1, 1) for x in halves]
        to_left = [pltpu.roll(x, LANES - 1, 1) for x in halves]
        at_first, at_last = lane_c == 0, lane_c == LANES - 1
        before_y = [jnp.where(at_first, ends[0], to_right[0]), jnp.where(at_first, to_right[0], to_right[1])]
        after_y = [jnp.where(at_last, to_left[1], to_left[0]), jnp.where(at_last, ends[1], to_left[1])]
        for h in range(2):
            x = halves[h]
            above = jnp.where(row_i == 0, row_r[0, h, f : f + 1, :], pltpu.roll(x, 1, 0))
            below = jnp.where(row_i == rows - 1, row_r[1, h, f : f + 1, :], pltpu.roll(x, rows - 1, 0))
            xs[1, h, f * rows : (f + 1) * rows, :] = (below - above) * 0.5
            xs[2, h, f * rows : (f + 1) * rows, :] = (after_y[h] - before_y[h]) * 0.5

    spread(1)
    spread(2)
    bank_copy.wait()

    def products(p, c):
        pair = jnp.concatenate([bank_v[2 * p], bank_v[2 * p + 1]], axis=1)
        got_pair = jnp.dot(xmat[...], pair, preferred_element_type=jnp.float32)
        prod[pl.ds(2 * p * tiles, tiles)] = got_pair[:, :LANES].reshape(tiles, fields, LANES)
        prod[pl.ds((2 * p + 1) * tiles, tiles)] = got_pair[:, LANES:].reshape(tiles, fields, LANES)
        return c

    lax.fori_loop(0, nwb // 2, products, 0)
    table_copy.wait()

    def record(d, s):
        return prod[jnp.clip(table_s[d, s], 0, nwb * tiles - 1)]

    def fill(d, ref):
        for s in range(0, cap, 2):
            pair = jnp.concatenate([record(d, s), record(d, s + 1)], axis=0)
            ref[d, s * fields : (s + 2) * fields, :] = pair.astype(jnp.bfloat16)

    def send_data(x, y):
        fill(x * ny + y, sent)
        data_to(x, y).start()

    each_other(send_data)
    fill(me, got)

    group = max(1, 2 * LANES // span)
    cells = fields * otx * oty
    shares = LANES // span
    cell_i = lax.broadcasted_iota(jnp.int32, (cells, LANES), 0).astype(jnp.float32)
    part_lane = lane_of((1, LANES)) // span

    def collect(q, total):
        def arrive(i, c):
            s = q * group + i

            @pl.when(s != me)
            def _():
                pltpu.make_async_remote_copy(
                    src_ref=meta_s.at[s], dst_ref=meta_r.at[s], send_sem=m_send.at[s], recv_sem=m_recv.at[s],
                    device_id=(s // ny, lax.rem(s, ny)), device_id_type=MESH,
                ).wait_recv()
                pltpu.make_async_remote_copy(
                    src_ref=sent.at[s], dst_ref=got.at[s], send_sem=a_send.at[s], recv_sem=a_recv.at[s],
                    device_id=(s // ny, lax.rem(s, ny)), device_id_type=MESH,
                ).wait_recv()

            return c

        lax.fori_loop(0, group, arrive, 0)
        hots = []
        for b in range(group // shares):
            aims = meta_r[q * group + b * shares]
            for i in range(1, shares):
                aims = jnp.where(part_lane == i, meta_r[q * group + b * shares + i], aims)
            hots.append(jnp.where(cell_i == aims, 1.0, 0.0).astype(jnp.bfloat16))
        hot = jnp.concatenate(hots, axis=1)
        data = got[pl.ds(q * group, group)].reshape(group * span, LANES)
        return total + jnp.dot(hot, data, preferred_element_type=jnp.float32)

    total = lax.fori_loop(0, n // group, collect, jnp.zeros((cells, LANES), jnp.float32))
    high = fields * otx
    parts = block_transpose([total[t * high : (t + 1) * high, :] for t in range(oty)], OTILE_Y)
    for a in range(OTILE_X):
        u[pl.ds(a, high, stride=OTILE_X), :] = parts[a]

    lane_o = lane_of((orows, LANES))
    packed = [jnp.zeros((orows, LANES), jnp.float32) for _ in range(2)]
    for f in range(fields):
        block = u[f * orows : (f + 1) * orows, :]
        shift = f * SWEEPS
        rolled = (pltpu.roll(block, shift, 1), pltpu.roll(block, LANES - shift, 1)) if f else (block, block)
        mine = (lane_o // SWEEPS == f, (LANES - 1 - lane_o) // SWEEPS == f)
        packed = [jnp.where(mine[e], rolled[e], packed[e]) for e in range(2)]
        pack_s[2, f * 8 : f * 8 + 8, :] = block[0:8]
        pack_s[3, f * 8 : f * 8 + 8, :] = block[orows - 8 : orows]
    pack_s[0, 0:orows, :] = packed[0]
    pack_s[1, 0:orows, :] = packed[1]
    ocean_copies = halo_copies(
        12,
        pack_s.at[0, pl.ds(0, orows)],
        pack_s.at[1, pl.ds(0, orows)],
        pack_s.at[2, pl.ds(0, fields * 8)],
        pack_s.at[3, pl.ds(0, fields * 8)],
        u_edge, u_corner, u_row,
    )
    for c in ocean_copies:
        c.start()

    def settle(x, y):
        meta_to(x, y).wait_send()
        data_to(x, y).wait_send()

    each_other(settle)
    for c in diff_copies:
        c.wait()

    has = (gx > 0, gx < nx - 1, gy > 0, gy < ny - 1)
    tail_lane = lane_of((8, LANES)) < LANES // 2
    tail_row = lax.broadcasted_iota(jnp.int32, (8, LANES), 0) < 4
    wide_lane = lane_o < LANES // 2
    row_ok = jnp.where(tail_row, has[1].astype(jnp.float32), has[0].astype(jnp.float32))
    col_ok = jnp.where(wide_lane, has[3].astype(jnp.float32), has[2].astype(jnp.float32))
    both_ok = row_ok * col_ok[0:8]
    d_tail = jnp.where(tail_row, d_row[1], d_row[0]) * row_ok
    d_side = jnp.where(wide_lane, d_edge[1], d_edge[0]) * col_ok
    d_both = (
        jnp.where(
            tail_lane,
            jnp.where(tail_row, d_corner[1, 1], d_corner[0, 1]),
            jnp.where(tail_row, d_corner[1, 0], d_corner[0, 0]),
        )
        * both_ok
    )
    d = [
        jnp.concatenate([diff[...], d_tail], axis=0),
        jnp.concatenate([d_side, d_both], axis=0),
    ]
    for c in ocean_copies:
        c.wait()
    side = [
        jnp.concatenate([u_edge[e], jnp.where(tail_row, u_corner[1, e], u_corner[0, e])], axis=0)
        for e in range(2)
    ]
    ext = orows + 8
    lane_e = lane_of((ext, LANES))
    side_ok = jnp.concatenate([col_ok, both_ok], axis=0)
    at_first, at_last = lane_e == 0, lane_e == LANES - 1
    for f in range(fields):
        shift = f * SWEEPS
        tail = jnp.where(tail_row, u_row[1, f * 8 : f * 8 + 8, :], u_row[0, f * 8 : f * 8 + 8, :]) * row_ok
        rolled = (
            (pltpu.roll(side[1], LANES - shift, 1), pltpu.roll(side[0], shift, 1)) if f else (side[1], side[0])
        )
        x = [
            jnp.concatenate([u[f * orows : (f + 1) * orows, :], tail], axis=0),
            jnp.where(lane_e < LANES // 2, rolled[0], rolled[1]) * side_ok,
        ]
        for sweep in range(SWEEPS):
            to_right = [pltpu.roll(v, 1, 1) for v in x]
            to_left = [pltpu.roll(v, LANES - 1, 1) for v in x]
            beside = [
                jnp.where(at_first, to_right[1 - h], to_right[h])
                + jnp.where(at_last, to_left[1 - h], to_left[h])
                + pltpu.roll(x[h], 1, 0)
                + pltpu.roll(x[h], ext - 1, 0)
                for h in range(2)
            ]
            x = [x[h] + d[h] * (beside[h] - 4.0 * x[h]) for h in range(2)]
        out[f] = x[0][0:orows, :]


def local(nx, ny, flux, diffusivity, remap_bank, rec_owner, rec_source, rec_target, rec_weight):
    n = nx * ny
    fields, rows, cols = flux.shape
    orows, ocols = diffusivity.shape
    records = rec_owner.shape[0]
    cap = max(2, 2 * records // n)
    nwb = remap_bank.shape[0]
    depth = 3 * TILE_X * TILE_Y
    tiles = rows // TILE_X * (cols // TILE_Y)
    span = cap * fields
    f32, bf16 = jnp.float32, jnp.bfloat16
    v = pltpu.VMEM
    dma = pltpu.SemaphoreType.DMA
    vm = pl.BlockSpec(memory_space=pltpu.VMEM)
    flat = [x.reshape(1, records) for x in (rec_owner, rec_source, rec_target, rec_weight)]
    return pl.pallas_call(
        functools.partial(kernel, nx, ny, cap),
        out_shape=jax.ShapeDtypeStruct((fields, orows, ocols), f32),
        in_specs=[pl.BlockSpec(memory_space=pl.ANY)] * 7,
        out_specs=vm,
        scratch_shapes=[
            v((fields, rows, cols), f32),
            v((orows, ocols), f32),
            v((4, 1, records), jnp.int32),
            dma((6,)),
            v((nwb, depth, LANES), bf16),
            v((3, 2, (fields + 1) * rows, LANES), f32),
            v((tiles * fields, depth), bf16),
            v((nwb * tiles, fields, LANES), f32),
            v((n, LANES), jnp.int32),
            pltpu.SMEM((n, LANES), jnp.int32),
            v((n, 1, LANES), f32),
            v((n, 1, LANES), f32),
            v((n, span, LANES), bf16),
            v((n, span, LANES), bf16),
            v((2, 2, fields, LANES), f32),
            v((2, 2, fields, LANES), f32),
            v((2, rows, LANES), f32),
            v((2, rows, LANES), f32),
            v((2, orows, LANES), f32),
            v((2, 2, 8, LANES), f32),
            v((2, 8, LANES), f32),
            v((fields * orows + OTILE_X, LANES), f32),
            v((4, max(orows, fields * 8), LANES), f32),
            v((2, orows, LANES), f32),
            v((2, 2, 8, LANES), f32),
            v((2, fields * 8, LANES), f32),
            dma, dma,
            dma((n,)), dma((n,)), dma((n,)), dma((n,)),
            dma((20,)), dma((20,)),
        ],
        compiler_params=pltpu.CompilerParams(
            collective_id=0, has_side_effects=True, vmem_limit_bytes=64 * 1024 * 1024 - 128 * 1024
        ),
    )(flux, diffusivity, remap_bank.reshape(nwb, depth, LANES), *flat)


def solution(mesh):
    in_specs = (
        P(None, "gx", "gy"),
        P("gx", "gy"),
        P(),
        P(("gx", "gy")),
        P(("gx", "gy")),
        P(("gx", "gy")),
        P(("gx", "gy")),
    )
    out_specs = P(None, "gx", "gy")
    body = functools.partial(local, mesh.shape["gx"], mesh.shape["gy"])
    return jax.shard_map(body, mesh=mesh, in_specs=in_specs, out_specs=out_specs, check_vma=False)
```

```python
import functools

import jax
import jax.numpy as jnp
from jax import lax
from jax.experimental import pallas as pl
from jax.experimental.pallas import tpu as pltpu
from jax.sharding import PartitionSpec as P

TILE_X = 16
TILE_Y = 16
OTILE_X = 8
OTILE_Y = 16
SWEEPS = 4
LANES = 128
MESH = pl.DeviceIdType.MESH


def lane_of(shape):
    return lax.broadcasted_iota(jnp.int32, shape, len(shape) - 1)


def block_transpose(parts, width):
    parts = list(parts)
    block = lane_of(parts[0].shape) // width
    step = 1
    while step < len(parts):
        keep = (block & step) == 0
        for i in range(len(parts)):
            if i & step == 0:
                j = i | step
                low, high = parts[i], parts[j]
                parts[i] = jnp.where(keep, low, pltpu.roll(high, step * width, 1))
                parts[j] = jnp.where(keep, pltpu.roll(low, LANES - step * width, 1), high)
        step *= 2
    return parts


def kernel(
    nx, ny, cap,
    flux_h, diff_h, bank, own_h, src_h, tgt_h, wgt_h,
    out,
    flux, diff, recs, in_sem,
    bank_v, xs, xmat, prod, table_v, table_s, meta_s, meta_r, sent, got,
    row_s, row_r, col_s, col_r, d_edge, d_corner, d_row, u, pack_s, u_edge, u_corner, u_row, part_s, part_r,
    bank_sem, table_sem, a_send, a_recv, m_send, m_recv, h_send, h_recv,
):
    n = nx * ny
    fields, rows, cols = flux.shape
    nwb = bank.shape[0]
    tiles_x, tiles_y = rows // TILE_X, cols // TILE_Y
    tiles = tiles_x * tiles_y
    orows = diff.shape[0]
    oty = diff.shape[1] // OTILE_Y
    otx = orows // OTILE_X
    span = cap * fields
    gx, gy = lax.axis_index("gx"), lax.axis_index("gy")
    me = gx * ny + gy
    up, down = lax.rem(gx + nx - 1, nx), lax.rem(gx + 1, nx)
    left, right = lax.rem(gy + ny - 1, ny), lax.rem(gy + 1, ny)

    barrier = pltpu.get_barrier_semaphore()

    y_order = [o for k in range(ny // 2 + 1) for o in sorted({ny // 2 - k, ny // 2 + k}) if o < ny]
    y_at = [gy if o == 0 else lax.rem(gy + o, ny) for o in y_order]

    def each_other(act):
        def one_row(i, c):
            x = lax.rem(gx + i, nx)
            for o, y in zip(y_order, y_at):
                if o:
                    act(x, y)
                else:
                    pl.when(i != 0)(functools.partial(act, x, y))
            return c

        lax.fori_loop(0, nx, one_row, 0)

    hy = ny // 2
    hn = n // 2
    base = gy // hy * hy
    other = hy - base
    mine_j = gy - base
    place = gx * hy + mine_j
    j_order = [o for k in range(hy // 2 + 1) for o in sorted({hy // 2 - k, hy // 2 + k}) if o < hy]
    j_at = [mine_j if o == 0 else lax.rem(mine_j + o, hy) for o in j_order]

    ins = [pltpu.make_async_copy(flux_h, flux, in_sem.at[0]), pltpu.make_async_copy(diff_h, diff, in_sem.at[1])]
    ins += [
        pltpu.make_async_copy(r, recs.at[i], in_sem.at[2 + i]) for i, r in enumerate((own_h, src_h, tgt_h, wgt_h))
    ]
    for c in ins:
        c.start()
    bank_copy = pltpu.make_async_copy(bank, bank_v, bank_sem)
    bank_copy.start()

    def greet(x, y):
        pl.semaphore_signal(barrier, inc=1, device_id=(x, y), device_id_type=MESH)

    each_other(greet)

    ins[0].wait()
    for f in range(fields):
        for h in range(2):
            xs[0, h, f * rows : (f + 1) * rows, :] = flux[f, :, h * LANES : (h + 1) * LANES]
    lane_c = lane_of((rows, LANES))
    first = jnp.zeros((rows, LANES), jnp.float32)
    last = jnp.zeros((rows, LANES), jnp.float32)
    for f in range(fields):
        a = flux[f, :, 0:LANES]
        b = flux[f, :, cols - LANES : cols]
        first = jnp.where(lane_c == f, pltpu.roll(a, f, 1) if f else a, first)
        last = jnp.where(lane_c == f, pltpu.roll(b, f + 1, 1), last)
    col_s[0] = first
    col_s[1] = last
    for h in range(2):
        row_s[0, h] = xs[0, h, pl.ds(0, fields, stride=rows), :]
        row_s[1, h] = xs[0, h, pl.ds(rows - 1, fields, stride=rows), :]

    ins[1].wait()
    pl.semaphore_wait(barrier, n - 1)

    def remote(a, b, k, x, y):
        return pltpu.make_async_remote_copy(
            src_ref=a, dst_ref=b, send_sem=h_send.at[k], recv_sem=h_recv.at[k],
            device_id=(x, y), device_id_type=MESH,
        )

    flux_copies = [
        remote(row_s.at[0], row_r.at[1], 0, up, gy),
        remote(row_s.at[1], row_r.at[0], 1, down, gy),
        remote(col_s.at[0], col_r.at[1], 2, gx, left),
        remote(col_s.at[1], col_r.at[0], 3, gx, right),
    ]
    for c in flux_copies:
        c.start()

    def halo_copies(base, edge0, edge1, row0, row1, edge, corner, row):
        low = pl.ds(0, 8)
        high = pl.ds(orows - 8, 8)
        return [
            remote(edge0, edge.at[1], base, gx, left),
            remote(edge1, edge.at[0], base + 1, gx, right),
            remote(row0, row.at[1], base + 2, up, gy),
            remote(row1, row.at[0], base + 3, down, gy),
            remote(edge0.at[low], corner.at[1, 1], base + 4, up, left),
            remote(edge0.at[high], corner.at[0, 1], base + 5, down, left),
            remote(edge1.at[low], corner.at[1, 0], base + 6, up, right),
            remote(edge1.at[high], corner.at[0, 0], base + 7, down, right),
        ]

    diff_copies = halo_copies(
        4, diff, diff, diff.at[pl.ds(0, 8)], diff.at[pl.ds(orows - 8, 8)], d_edge, d_corner, d_row
    )
    for c in diff_copies:
        c.start()

    for c in ins[2:]:
        c.wait()
    records = recs.shape[2]
    owner_i = lax.broadcasted_iota(jnp.int32, (n, records), 0)
    member = recs[0] == owner_i
    lower = lax.broadcasted_iota(jnp.int32, (records, records), 0) < lane_of((records, records))
    before = jnp.dot(
        member.astype(jnp.bfloat16), lower.astype(jnp.bfloat16), preferred_element_type=jnp.float32
    )
    source, target = recs[1], recs[2]
    code = (recs[3] * tiles + lax.rem(source, tiles_y) * tiles_x + source // tiles_y).astype(jnp.float32)
    aim = (lax.rem(target, oty) * (fields * otx) + target // oty).astype(jnp.float32)
    lane = lane_of((n, LANES))
    slot_lane = lax.rem(lane, span) // fields
    field_lane = (lax.rem(lane, fields) * otx).astype(jnp.float32)
    table = jnp.zeros((n, LANES), jnp.float32)
    meta = jnp.full((n, LANES), -1.0, jnp.float32)
    for k in range(cap):
        hit = jnp.logical_and(member, before == k)
        code_k = jnp.sum(jnp.where(hit, code, 0.0), axis=1, keepdims=True)
        aim_k = jnp.sum(jnp.where(hit, aim + 1.0, 0.0), axis=1, keepdims=True) - 1.0
        table = jnp.where(lane == k, code_k, table)
        filled = jnp.where(aim_k >= 0.0, aim_k + field_lane, -1.0)
        meta = jnp.where(slot_lane == k, filled, meta)
    table_v[...] = table.astype(jnp.int32)
    table_copy = pltpu.make_async_copy(table_v, table_s, table_sem)
    table_copy.start()
    for o in range(n):
        meta_s[o] = meta[o : o + 1, :]

    def parties(kind, x, j):
        owner = x * ny + (base if kind else other) + j
        return owner, kind * hn + place, (x, base + j)

    def meta_to(kind, x, j):
        owner, slot, device = parties(kind, x, j)
        return pltpu.make_async_remote_copy(
            src_ref=meta_s.at[owner], dst_ref=meta_r.at[slot], send_sem=m_send.at[owner], recv_sem=m_recv.at[slot],
            device_id=device, device_id_type=MESH,
        )

    def data_to(kind, x, j):
        owner, slot, device = parties(kind, x, j)
        return pltpu.make_async_remote_copy(
            src_ref=sent.at[owner], dst_ref=got.at[slot], send_sem=a_send.at[owner], recv_sem=a_recv.at[slot],
            device_id=device, device_id_type=MESH,
        )

    def half_others(act):
        def one_row(i, c):
            x = lax.rem(gx + i, nx)
            for k, j in zip(j_order, j_at):
                if k:
                    act(x, j)
                else:
                    pl.when(i != 0)(functools.partial(act, x, j))
            return c

        lax.fori_loop(0, nx, one_row, 0)

    for kind in range(2):
        meta_r[kind * hn + place] = meta_s[gx * ny + (base if kind else other) + mine_j]
        half_others(lambda x, j: meta_to(kind, x, j).start())

    per = LANES // TILE_Y
    halfx = TILE_X // per
    tile_rows = tiles_x * fields
    def spread(c):
        for h in range(2):
            for g in range(halfx):
                parts = [
                    jnp.concatenate(
                        [
                            xs[c, h, pl.ds(t * TILE_X + g * per + a, fields, stride=rows), :]
                            for t in range(tiles_x)
                        ],
                        axis=0,
                    )
                    for a in range(per)
                ]
                parts = block_transpose(parts, TILE_Y)
                at = (c * halfx + g) * LANES
                for t in range(per):
                    j = h * per + t
                    xmat[j * tile_rows : (j + 1) * tile_rows, at : at + LANES] = parts[t].astype(jnp.bfloat16)

    spread(0)

    for c in flux_copies:
        c.wait()
    row_i = lax.broadcasted_iota(jnp.int32, (rows, LANES), 0)
    for f in range(fields):
        halves = [flux[f, :, h * LANES : (h + 1) * LANES] for h in range(2)]
        ends = (
            pltpu.roll(col_r[0], LANES - f, 1) if f else col_r[0],
            pltpu.roll(col_r[1], LANES - 1 - f, 1),
        )
        to_right = [pltpu.roll(x, 1, 1) for x in halves]
        to_left = [pltpu.roll(x, LANES - 1, 1) for x in halves]
        at_first, at_last = lane_c == 0, lane_c == LANES - 1
        before_y = [jnp.where(at_first, ends[0], to_right[0]), jnp.where(at_first, to_right[0], to_right[1])]
        after_y = [jnp.where(at_last, to_left[1], to_left[0]), jnp.where(at_last, ends[1], to_left[1])]
        for h in range(2):
            x = halves[h]
            above = jnp.where(row_i == 0, row_r[0, h, f : f + 1, :], pltpu.roll(x, 1, 0))
            below = jnp.where(row_i == rows - 1, row_r[1, h, f : f + 1, :], pltpu.roll(x, rows - 1, 0))
            xs[1, h, f * rows : (f + 1) * rows, :] = (below - above) * 0.5
            xs[2, h, f * rows : (f + 1) * rows, :] = (after_y[h] - before_y[h]) * 0.5

    spread(1)
    spread(2)
    bank_copy.wait()

    def products(p, c):
        pair = jnp.concatenate([bank_v[2 * p], bank_v[2 * p + 1]], axis=1)
        got_pair = jnp.dot(xmat[...], pair, preferred_element_type=jnp.float32)
        prod[pl.ds(2 * p * tiles, tiles)] = got_pair[:, :LANES].reshape(tiles, fields, LANES)
        prod[pl.ds((2 * p + 1) * tiles, tiles)] = got_pair[:, LANES:].reshape(tiles, fields, LANES)
        return c

    lax.fori_loop(0, nwb // 2, products, 0)
    table_copy.wait()

    def record(d, s):
        return prod[jnp.clip(table_s[d, s], 0, nwb * tiles - 1)]

    def fill(d, ref, at):
        for s in range(0, cap, 2):
            pair = jnp.concatenate([record(d, s), record(d, s + 1)], axis=0)
            ref[at, s * fields : (s + 2) * fields, :] = pair.astype(jnp.bfloat16)

    for kind in range(2):

        def send_data(x, j):
            d = parties(kind, x, j)[0]
            fill(d, sent, d)
            data_to(kind, x, j).start()

        half_others(send_data)
        fill(gx * ny + (base if kind else other) + mine_j, got, kind * hn + place)

    group = min(hn, max(1, 2 * LANES // span))
    cells = fields * otx * oty
    shares = LANES // span
    cell_i = lax.broadcasted_iota(jnp.int32, (cells, LANES), 0).astype(jnp.float32)
    part_lane = lane_of((1, LANES)) // span

    def collect(q, total):
        def arrive(i, c):
            s = q * group + i

            @pl.when(lax.rem(s, hn) != place)
            def _():
                device = (lax.rem(s, hn) // hy, base + lax.rem(s, hy))
                pltpu.make_async_remote_copy(
                    src_ref=meta_s.at[s], dst_ref=meta_r.at[s], send_sem=m_send.at[s], recv_sem=m_recv.at[s],
                    device_id=device, device_id_type=MESH,
                ).wait_recv()
                pltpu.make_async_remote_copy(
                    src_ref=sent.at[s], dst_ref=got.at[s], send_sem=a_send.at[s], recv_sem=a_recv.at[s],
                    device_id=device, device_id_type=MESH,
                ).wait_recv()

            return c

        lax.fori_loop(0, group, arrive, 0)
        hots = []
        for b in range(group // shares):
            aims = meta_r[q * group + b * shares]
            for i in range(1, shares):
                aims = jnp.where(part_lane == i, meta_r[q * group + b * shares + i], aims)
            hots.append(jnp.where(cell_i == aims, 1.0, 0.0).astype(jnp.bfloat16))
        hot = jnp.concatenate(hots, axis=1)
        data = got[pl.ds(q * group, group)].reshape(group * span, LANES)
        return total + jnp.dot(hot, data, preferred_element_type=jnp.float32)

    empty = jnp.zeros((cells, LANES), jnp.float32)
    part_s[...] = lax.fori_loop(0, hn // group, collect, empty).astype(jnp.bfloat16)
    cross = remote(part_s, part_r, 20, gx, other + mine_j)
    cross.start()
    total = lax.fori_loop(hn // group, n // group, collect, empty)
    cross.wait()
    total = total + part_r[...].astype(jnp.float32)
    high = fields * otx
    parts = block_transpose([total[t * high : (t + 1) * high, :] for t in range(oty)], OTILE_Y)
    for a in range(OTILE_X):
        u[pl.ds(a, high, stride=OTILE_X), :] = parts[a]

    lane_o = lane_of((orows, LANES))
    packed = [jnp.zeros((orows, LANES), jnp.float32) for _ in range(2)]
    for f in range(fields):
        block = u[f * orows : (f + 1) * orows, :]
        shift = f * SWEEPS
        rolled = (pltpu.roll(block, shift, 1), pltpu.roll(block, LANES - shift, 1)) if f else (block, block)
        mine = (lane_o // SWEEPS == f, (LANES - 1 - lane_o) // SWEEPS == f)
        packed = [jnp.where(mine[e], rolled[e], packed[e]) for e in range(2)]
        pack_s[2, f * 8 : f * 8 + 8, :] = block[0:8]
        pack_s[3, f * 8 : f * 8 + 8, :] = block[orows - 8 : orows]
    pack_s[0, 0:orows, :] = packed[0]
    pack_s[1, 0:orows, :] = packed[1]
    ocean_copies = halo_copies(
        12,
        pack_s.at[0, pl.ds(0, orows)],
        pack_s.at[1, pl.ds(0, orows)],
        pack_s.at[2, pl.ds(0, fields * 8)],
        pack_s.at[3, pl.ds(0, fields * 8)],
        u_edge, u_corner, u_row,
    )
    for c in ocean_copies:
        c.start()

    for kind in range(2):

        def settle(x, j):
            meta_to(kind, x, j).wait_send()
            data_to(kind, x, j).wait_send()

        half_others(settle)
    for c in diff_copies:
        c.wait()

    has = (gx > 0, gx < nx - 1, gy > 0, gy < ny - 1)
    tail_lane = lane_of((8, LANES)) < LANES // 2
    tail_row = lax.broadcasted_iota(jnp.int32, (8, LANES), 0) < 4
    wide_lane = lane_o < LANES // 2
    row_ok = jnp.where(tail_row, has[1].astype(jnp.float32), has[0].astype(jnp.float32))
    col_ok = jnp.where(wide_lane, has[3].astype(jnp.float32), has[2].astype(jnp.float32))
    both_ok = row_ok * col_ok[0:8]
    d_tail = jnp.where(tail_row, d_row[1], d_row[0]) * row_ok
    d_side = jnp.where(wide_lane, d_edge[1], d_edge[0]) * col_ok
    d_both = (
        jnp.where(
            tail_lane,
            jnp.where(tail_row, d_corner[1, 1], d_corner[0, 1]),
            jnp.where(tail_row, d_corner[1, 0], d_corner[0, 0]),
        )
        * both_ok
    )
    d = [
        jnp.concatenate([diff[...], d_tail], axis=0),
        jnp.concatenate([d_side, d_both], axis=0),
    ]
    for c in ocean_copies:
        c.wait()
    side = [
        jnp.concatenate([u_edge[e], jnp.where(tail_row, u_corner[1, e], u_corner[0, e])], axis=0)
        for e in range(2)
    ]
    ext = orows + 8
    lane_e = lane_of((ext, LANES))
    side_ok = jnp.concatenate([col_ok, both_ok], axis=0)
    at_first, at_last = lane_e == 0, lane_e == LANES - 1
    for f in range(fields):
        shift = f * SWEEPS
        tail = jnp.where(tail_row, u_row[1, f * 8 : f * 8 + 8, :], u_row[0, f * 8 : f * 8 + 8, :]) * row_ok
        rolled = (
            (pltpu.roll(side[1], LANES - shift, 1), pltpu.roll(side[0], shift, 1)) if f else (side[1], side[0])
        )
        x = [
            jnp.concatenate([u[f * orows : (f + 1) * orows, :], tail], axis=0),
            jnp.where(lane_e < LANES // 2, rolled[0], rolled[1]) * side_ok,
        ]
        for sweep in range(SWEEPS):
            to_right = [pltpu.roll(v, 1, 1) for v in x]
            to_left = [pltpu.roll(v, LANES - 1, 1) for v in x]
            beside = [
                jnp.where(at_first, to_right[1 - h], to_right[h])
                + jnp.where(at_last, to_left[1 - h], to_left[h])
                + pltpu.roll(x[h], 1, 0)
                + pltpu.roll(x[h], ext - 1, 0)
                for h in range(2)
            ]
            x = [x[h] + d[h] * (beside[h] - 4.0 * x[h]) for h in range(2)]
        out[f] = x[0][0:orows, :]


def local(nx, ny, flux, diffusivity, remap_bank, rec_owner, rec_source, rec_target, rec_weight):
    n = nx * ny
    fields, rows, cols = flux.shape
    orows, ocols = diffusivity.shape
    records = rec_owner.shape[0]
    cap = max(2, 2 * records // n)
    nwb = remap_bank.shape[0]
    depth = 3 * TILE_X * TILE_Y
    tiles = rows // TILE_X * (cols // TILE_Y)
    span = cap * fields
    f32, bf16 = jnp.float32, jnp.bfloat16
    v = pltpu.VMEM
    dma = pltpu.SemaphoreType.DMA
    vm = pl.BlockSpec(memory_space=pltpu.VMEM)
    flat = [x.reshape(1, records) for x in (rec_owner, rec_source, rec_target, rec_weight)]
    return pl.pallas_call(
        functools.partial(kernel, nx, ny, cap),
        out_shape=jax.ShapeDtypeStruct((fields, orows, ocols), f32),
        in_specs=[pl.BlockSpec(memory_space=pl.ANY)] * 7,
        out_specs=vm,
        scratch_shapes=[
            v((fields, rows, cols), f32),
            v((orows, ocols), f32),
            v((4, 1, records), jnp.int32),
            dma((6,)),
            v((nwb, depth, LANES), bf16),
            v((3, 2, (fields + 1) * rows, LANES), f32),
            v((tiles * fields, depth), bf16),
            v((nwb * tiles, fields, LANES), f32),
            v((n, LANES), jnp.int32),
            pltpu.SMEM((n, LANES), jnp.int32),
            v((n, 1, LANES), f32),
            v((n, 1, LANES), f32),
            v((n, span, LANES), bf16),
            v((n, span, LANES), bf16),
            v((2, 2, fields, LANES), f32),
            v((2, 2, fields, LANES), f32),
            v((2, rows, LANES), f32),
            v((2, rows, LANES), f32),
            v((2, orows, LANES), f32),
            v((2, 2, 8, LANES), f32),
            v((2, 8, LANES), f32),
            v((fields * orows + OTILE_X, LANES), f32),
            v((4, max(orows, fields * 8), LANES), f32),
            v((2, orows, LANES), f32),
            v((2, 2, 8, LANES), f32),
            v((2, fields * 8, LANES), f32),
            v((fields * orows * ocols // LANES, LANES), bf16),
            v((fields * orows * ocols // LANES, LANES), bf16),
            dma, dma,
            dma((n,)), dma((n,)), dma((n,)), dma((n,)),
            dma((21,)), dma((21,)),
        ],
        compiler_params=pltpu.CompilerParams(
            collective_id=0, has_side_effects=True, vmem_limit_bytes=64 * 1024 * 1024 - 128 * 1024
        ),
    )(flux, diffusivity, remap_bank.reshape(nwb, depth, LANES), *flat)


def solution(mesh):
    in_specs = (
        P(None, "gx", "gy"),
        P("gx", "gy"),
        P(),
        P(("gx", "gy")),
        P(("gx", "gy")),
        P(("gx", "gy")),
        P(("gx", "gy")),
    )
    out_specs = P(None, "gx", "gy")
    body = functools.partial(local, mesh.shape["gx"], mesh.shape["gy"])
    return jax.shard_map(body, mesh=mesh, in_specs=in_specs, out_specs=out_specs, check_vma=False)
```

```python
import functools

import jax
import jax.numpy as jnp
from jax import lax
from jax.experimental import pallas as pl
from jax.experimental.pallas import tpu as pltpu
from jax.sharding import PartitionSpec as P

TILE_X = 16
TILE_Y = 16
OTILE_X = 8
OTILE_Y = 16
SWEEPS = 4
LANES = 128
MESH = pl.DeviceIdType.MESH


def lane_of(shape):
    return lax.broadcasted_iota(jnp.int32, shape, len(shape) - 1)


def block_transpose(parts, width):
    parts = list(parts)
    block = lane_of(parts[0].shape) // width
    step = 1
    while step < len(parts):
        keep = (block & step) == 0
        for i in range(len(parts)):
            if i & step == 0:
                j = i | step
                low, high = parts[i], parts[j]
                parts[i] = jnp.where(keep, low, pltpu.roll(high, step * width, 1))
                parts[j] = jnp.where(keep, pltpu.roll(low, LANES - step * width, 1), high)
        step *= 2
    return parts


def kernel(
    nx, ny, cap,
    flux_h, diff_h, bank, own_h, src_h, tgt_h, wgt_h,
    out,
    flux, diff, recs, in_sem,
    bank_v, xs, xmat, prod, table_v, table_s, meta_s, meta_r, sent, got,
    row_s, row_r, col_s, col_r, d_edge, d_corner, d_row, u, pack_s, u_edge, u_corner, u_row, part_s, part_r, hot,
    bank_sem, table_sem, a_send, a_recv, m_send, m_recv, h_send, h_recv,
):
    n = nx * ny
    fields, rows, cols = flux.shape
    nwb = bank.shape[0]
    tiles_x, tiles_y = rows // TILE_X, cols // TILE_Y
    tiles = tiles_x * tiles_y
    orows = diff.shape[0]
    oty = diff.shape[1] // OTILE_Y
    otx = orows // OTILE_X
    span = cap * fields
    gx, gy = lax.axis_index("gx"), lax.axis_index("gy")
    me = gx * ny + gy
    up, down = lax.rem(gx + nx - 1, nx), lax.rem(gx + 1, nx)
    left, right = lax.rem(gy + ny - 1, ny), lax.rem(gy + 1, ny)

    barrier = pltpu.get_barrier_semaphore()

    y_order = [o for k in range(ny // 2 + 1) for o in sorted({ny // 2 - k, ny // 2 + k}) if o < ny]
    y_at = [gy if o == 0 else lax.rem(gy + o, ny) for o in y_order]

    def each_other(act):
        def one_row(i, c):
            x = lax.rem(gx + i, nx)
            for o, y in zip(y_order, y_at):
                if o:
                    act(x, y)
                else:
                    pl.when(i != 0)(functools.partial(act, x, y))
            return c

        lax.fori_loop(0, nx, one_row, 0)

    hy = ny // 2
    hn = n // 2
    base = gy // hy * hy
    other = hy - base
    mine_j = gy - base
    place = gx * hy + mine_j
    j_order = [o for k in range(hy // 2 + 1) for o in sorted({hy // 2 - k, hy // 2 + k}) if o < hy]
    j_at = [mine_j if o == 0 else lax.rem(mine_j + o, hy) for o in j_order]

    ins = [pltpu.make_async_copy(flux_h, flux, in_sem.at[0]), pltpu.make_async_copy(diff_h, diff, in_sem.at[1])]
    ins += [
        pltpu.make_async_copy(r, recs.at[i], in_sem.at[2 + i]) for i, r in enumerate((own_h, src_h, tgt_h, wgt_h))
    ]
    for c in ins:
        c.start()
    bank_copy = pltpu.make_async_copy(bank, bank_v, bank_sem)
    bank_copy.start()

    def greet(x, y):
        pl.semaphore_signal(barrier, inc=1, device_id=(x, y), device_id_type=MESH)

    each_other(greet)

    ins[0].wait()
    for f in range(fields):
        for h in range(2):
            xs[0, h, f * rows : (f + 1) * rows, :] = flux[f, :, h * LANES : (h + 1) * LANES]
    lane_c = lane_of((rows, LANES))
    first = jnp.zeros((rows, LANES), jnp.float32)
    last = jnp.zeros((rows, LANES), jnp.float32)
    for f in range(fields):
        a = flux[f, :, 0:LANES]
        b = flux[f, :, cols - LANES : cols]
        first = jnp.where(lane_c == f, pltpu.roll(a, f, 1) if f else a, first)
        last = jnp.where(lane_c == f, pltpu.roll(b, f + 1, 1), last)
    col_s[0] = first
    col_s[1] = last
    for h in range(2):
        row_s[0, h] = xs[0, h, pl.ds(0, fields, stride=rows), :]
        row_s[1, h] = xs[0, h, pl.ds(rows - 1, fields, stride=rows), :]

    ins[1].wait()
    pl.semaphore_wait(barrier, n - 1)

    def remote(a, b, k, x, y):
        return pltpu.make_async_remote_copy(
            src_ref=a, dst_ref=b, send_sem=h_send.at[k], recv_sem=h_recv.at[k],
            device_id=(x, y), device_id_type=MESH,
        )

    flux_copies = [
        remote(row_s.at[0], row_r.at[1], 0, up, gy),
        remote(row_s.at[1], row_r.at[0], 1, down, gy),
        remote(col_s.at[0], col_r.at[1], 2, gx, left),
        remote(col_s.at[1], col_r.at[0], 3, gx, right),
    ]
    for c in flux_copies:
        c.start()

    def halo_copies(base, edge0, edge1, row0, row1, edge, corner, row):
        low = pl.ds(0, 8)
        high = pl.ds(orows - 8, 8)
        return [
            remote(edge0, edge.at[1], base, gx, left),
            remote(edge1, edge.at[0], base + 1, gx, right),
            remote(row0, row.at[1], base + 2, up, gy),
            remote(row1, row.at[0], base + 3, down, gy),
            remote(edge0.at[low], corner.at[1, 1], base + 4, up, left),
            remote(edge0.at[high], corner.at[0, 1], base + 5, down, left),
            remote(edge1.at[low], corner.at[1, 0], base + 6, up, right),
            remote(edge1.at[high], corner.at[0, 0], base + 7, down, right),
        ]

    diff_copies = halo_copies(
        4, diff, diff, diff.at[pl.ds(0, 8)], diff.at[pl.ds(orows - 8, 8)], d_edge, d_corner, d_row
    )
    for c in diff_copies:
        c.start()

    for c in ins[2:]:
        c.wait()
    records = recs.shape[2]
    owner_i = lax.broadcasted_iota(jnp.int32, (n, records), 0)
    member = recs[0] == owner_i
    lower = lax.broadcasted_iota(jnp.int32, (records, records), 0) < lane_of((records, records))
    before = jnp.dot(
        member.astype(jnp.bfloat16), lower.astype(jnp.bfloat16), preferred_element_type=jnp.float32
    )
    source, target = recs[1], recs[2]
    code = (recs[3] * tiles + lax.rem(source, tiles_y) * tiles_x + source // tiles_y).astype(jnp.float32)
    aim = (lax.rem(target, oty) * (fields * otx) + target // oty).astype(jnp.float32)
    lane = lane_of((n, LANES))
    slot_lane = lax.rem(lane, span) // fields
    field_lane = (lax.rem(lane, fields) * otx).astype(jnp.float32)
    table = jnp.zeros((n, LANES), jnp.float32)
    meta = jnp.full((n, LANES), -1.0, jnp.float32)
    for k in range(cap):
        hit = jnp.logical_and(member, before == k)
        code_k = jnp.sum(jnp.where(hit, code, 0.0), axis=1, keepdims=True)
        aim_k = jnp.sum(jnp.where(hit, aim + 1.0, 0.0), axis=1, keepdims=True) - 1.0
        table = jnp.where(lane == k, code_k, table)
        filled = jnp.where(aim_k >= 0.0, aim_k + field_lane, -1.0)
        meta = jnp.where(slot_lane == k, filled, meta)
    table_v[...] = table.astype(jnp.int32)
    table_copy = pltpu.make_async_copy(table_v, table_s, table_sem)
    table_copy.start()
    for o in range(n):
        meta_s[o // ny * hy + o % hy, o % ny // hy] = meta[o : o + 1, :]
    meta_r[place] = meta_s[place]

    def parties(kind, x, j):
        owner = x * ny + (base if kind else other) + j
        return owner, kind * hn + place, (x, base + j)

    def meta_to(x, j):
        return pltpu.make_async_remote_copy(
            src_ref=meta_s.at[x * hy + j], dst_ref=meta_r.at[place], send_sem=m_send, recv_sem=m_recv,
            device_id=(x, base + j), device_id_type=MESH,
        )

    def data_to(kind, x, j):
        owner, slot, device = parties(kind, x, j)
        return pltpu.make_async_remote_copy(
            src_ref=sent.at[owner], dst_ref=got.at[slot], send_sem=a_send, recv_sem=a_recv.at[kind],
            device_id=device, device_id_type=MESH,
        )

    def half_others(act):
        def one_row(i, c):
            x = lax.rem(gx + i, nx)
            for k, j in zip(j_order, j_at):
                if k:
                    act(x, j)
                else:
                    pl.when(i != 0)(functools.partial(act, x, j))
            return c

        lax.fori_loop(0, nx, one_row, 0)

    half_others(lambda x, j: meta_to(x, j).start())

    per = LANES // TILE_Y
    halfx = TILE_X // per
    tile_rows = tiles_x * fields
    def spread(c):
        for h in range(2):
            for g in range(halfx):
                parts = [
                    jnp.concatenate(
                        [
                            xs[c, h, pl.ds(t * TILE_X + g * per + a, fields, stride=rows), :]
                            for t in range(tiles_x)
                        ],
                        axis=0,
                    )
                    for a in range(per)
                ]
                parts = block_transpose(parts, TILE_Y)
                at = (c * halfx + g) * LANES
                for t in range(per):
                    j = h * per + t
                    xmat[j * tile_rows : (j + 1) * tile_rows, at : at + LANES] = parts[t].astype(jnp.bfloat16)

    spread(0)

    for c in flux_copies:
        c.wait()
    row_i = lax.broadcasted_iota(jnp.int32, (rows, LANES), 0)
    for f in range(fields):
        halves = [flux[f, :, h * LANES : (h + 1) * LANES] for h in range(2)]
        ends = (
            pltpu.roll(col_r[0], LANES - f, 1) if f else col_r[0],
            pltpu.roll(col_r[1], LANES - 1 - f, 1),
        )
        to_right = [pltpu.roll(x, 1, 1) for x in halves]
        to_left = [pltpu.roll(x, LANES - 1, 1) for x in halves]
        at_first, at_last = lane_c == 0, lane_c == LANES - 1
        before_y = [jnp.where(at_first, ends[0], to_right[0]), jnp.where(at_first, to_right[0], to_right[1])]
        after_y = [jnp.where(at_last, to_left[1], to_left[0]), jnp.where(at_last, ends[1], to_left[1])]
        for h in range(2):
            x = halves[h]
            above = jnp.where(row_i == 0, row_r[0, h, f : f + 1, :], pltpu.roll(x, 1, 0))
            below = jnp.where(row_i == rows - 1, row_r[1, h, f : f + 1, :], pltpu.roll(x, rows - 1, 0))
            xs[1, h, f * rows : (f + 1) * rows, :] = (below - above) * 0.5
            xs[2, h, f * rows : (f + 1) * rows, :] = (after_y[h] - before_y[h]) * 0.5

    spread(1)
    spread(2)
    bank_copy.wait()

    def products(p, c):
        pair = jnp.concatenate([bank_v[2 * p], bank_v[2 * p + 1]], axis=1)
        got_pair = jnp.dot(xmat[...], pair, preferred_element_type=jnp.float32)
        prod[pl.ds(2 * p * tiles, tiles)] = got_pair[:, :LANES].reshape(tiles, fields, LANES)
        prod[pl.ds((2 * p + 1) * tiles, tiles)] = got_pair[:, LANES:].reshape(tiles, fields, LANES)
        return c

    lax.fori_loop(0, nwb // 2, products, 0)
    table_copy.wait()

    def record(d, s):
        return prod[jnp.clip(table_s[d, s], 0, nwb * tiles - 1)]

    def fill(d, ref, at):
        for s in range(0, cap, 2):
            pair = jnp.concatenate([record(d, s), record(d, s + 1)], axis=0)
            ref[at, s * fields : (s + 2) * fields, :] = pair.astype(jnp.bfloat16)

    for kind in range(2):

        def send_data(x, j):
            d = parties(kind, x, j)[0]
            fill(d, sent, d)
            data_to(kind, x, j).start()

        half_others(send_data)
        fill(gx * ny + (base if kind else other) + mine_j, got, kind * hn + place)

    cells = fields * otx * oty
    shares = LANES // span
    depth = hn * span
    cell_i = lax.broadcasted_iota(jnp.int32, (cells, LANES), 0).astype(jnp.float32)
    part_lane = lane_of((1, LANES)) // span
    mine_half = gy // hy

    def whole(src_ref, dst_ref, send_sem, recv_sem):
        return pltpu.make_async_remote_copy(
            src_ref=src_ref, dst_ref=dst_ref, send_sem=send_sem, recv_sem=recv_sem,
            device_id=(gx, other + mine_j), device_id_type=MESH,
        )

    meta_all = whole(meta_s.at[pl.ds(0, hn - 1)], meta_r.at[pl.ds(0, hn - 1)], m_send, m_recv)
    meta_all.wait_recv()
    for kind in range(2):
        row = mine_half if kind else 1 - mine_half
        for b in range(depth // LANES):
            aims = meta_r[b * shares, row]
            for i in range(1, shares):
                aims = jnp.where(part_lane == i, meta_r[b * shares + i, row], aims)
            at = kind * depth + b * LANES
            hot[:, at : at + LANES] = jnp.where(cell_i == aims, 1.0, 0.0).astype(jnp.bfloat16)

    def collect(kind):
        ref = got.at[pl.ds(kind * hn, hn - 1)]
        whole(ref, ref, a_send, a_recv.at[kind]).wait_recv()
        data = got[kind * hn : (kind + 1) * hn].reshape(depth, LANES)
        return jnp.dot(hot[:, kind * depth : (kind + 1) * depth], data, preferred_element_type=jnp.float32)

    part_s[...] = collect(0).astype(jnp.bfloat16)
    cross = remote(part_s, part_r, 20, gx, other + mine_j)
    cross.start()
    total = collect(1)
    cross.wait()
    total = total + part_r[...].astype(jnp.float32)
    high = fields * otx
    parts = block_transpose([total[t * high : (t + 1) * high, :] for t in range(oty)], OTILE_Y)
    for a in range(OTILE_X):
        u[pl.ds(a, high, stride=OTILE_X), :] = parts[a]

    lane_o = lane_of((orows, LANES))
    packed = [jnp.zeros((orows, LANES), jnp.float32) for _ in range(2)]
    for f in range(fields):
        block = u[f * orows : (f + 1) * orows, :]
        shift = f * SWEEPS
        rolled = (pltpu.roll(block, shift, 1), pltpu.roll(block, LANES - shift, 1)) if f else (block, block)
        mine = (lane_o // SWEEPS == f, (LANES - 1 - lane_o) // SWEEPS == f)
        packed = [jnp.where(mine[e], rolled[e], packed[e]) for e in range(2)]
        pack_s[2, f * 8 : f * 8 + 8, :] = block[0:8]
        pack_s[3, f * 8 : f * 8 + 8, :] = block[orows - 8 : orows]
    pack_s[0, 0:orows, :] = packed[0]
    pack_s[1, 0:orows, :] = packed[1]
    ocean_copies = halo_copies(
        12,
        pack_s.at[0, pl.ds(0, orows)],
        pack_s.at[1, pl.ds(0, orows)],
        pack_s.at[2, pl.ds(0, fields * 8)],
        pack_s.at[3, pl.ds(0, fields * 8)],
        u_edge, u_corner, u_row,
    )
    for c in ocean_copies:
        c.start()

    meta_all.wait_send()
    ref = sent.at[pl.ds(0, 2 * (hn - 1))]
    whole(ref, ref, a_send, a_recv.at[0]).wait_send()
    for c in diff_copies:
        c.wait()

    has = (gx > 0, gx < nx - 1, gy > 0, gy < ny - 1)
    tail_lane = lane_of((8, LANES)) < LANES // 2
    tail_row = lax.broadcasted_iota(jnp.int32, (8, LANES), 0) < 4
    wide_lane = lane_o < LANES // 2
    row_ok = jnp.where(tail_row, has[1].astype(jnp.float32), has[0].astype(jnp.float32))
    col_ok = jnp.where(wide_lane, has[3].astype(jnp.float32), has[2].astype(jnp.float32))
    both_ok = row_ok * col_ok[0:8]
    d_tail = jnp.where(tail_row, d_row[1], d_row[0]) * row_ok
    d_side = jnp.where(wide_lane, d_edge[1], d_edge[0]) * col_ok
    d_both = (
        jnp.where(
            tail_lane,
            jnp.where(tail_row, d_corner[1, 1], d_corner[0, 1]),
            jnp.where(tail_row, d_corner[1, 0], d_corner[0, 0]),
        )
        * both_ok
    )
    d = [
        jnp.concatenate([diff[...], d_tail], axis=0),
        jnp.concatenate([d_side, d_both], axis=0),
    ]
    for c in ocean_copies:
        c.wait()
    side = [
        jnp.concatenate([u_edge[e], jnp.where(tail_row, u_corner[1, e], u_corner[0, e])], axis=0)
        for e in range(2)
    ]
    ext = orows + 8
    lane_e = lane_of((ext, LANES))
    side_ok = jnp.concatenate([col_ok, both_ok], axis=0)
    at_first, at_last = lane_e == 0, lane_e == LANES - 1
    def opened(f):
        shift = f * SWEEPS
        tail = jnp.where(tail_row, u_row[1, f * 8 : f * 8 + 8, :], u_row[0, f * 8 : f * 8 + 8, :]) * row_ok
        rolled = (
            (pltpu.roll(side[1], LANES - shift, 1), pltpu.roll(side[0], shift, 1)) if f else (side[1], side[0])
        )
        return [
            jnp.concatenate([u[f * orows : (f + 1) * orows, :], tail], axis=0),
            jnp.where(lane_e < LANES // 2, rolled[0], rolled[1]) * side_ok,
        ]

    def swept(x):
        to_right = [pltpu.roll(v, 1, 1) for v in x]
        to_left = [pltpu.roll(v, LANES - 1, 1) for v in x]
        beside = [
            jnp.where(at_first, to_right[1 - h], to_right[h])
            + jnp.where(at_last, to_left[1 - h], to_left[h])
            + pltpu.roll(x[h], 1, 0)
            + pltpu.roll(x[h], ext - 1, 0)
            for h in range(2)
        ]
        return [x[h] + d[h] * (beside[h] - 4.0 * x[h]) for h in range(2)]

    for f in range(0, fields, 2):
        pair = [opened(f), opened(f + 1)]
        for sweep in range(SWEEPS):
            pair = [swept(x) for x in pair]
        for i, x in enumerate(pair):
            out[f + i] = x[0][0:orows, :]


def local(nx, ny, flux, diffusivity, remap_bank, rec_owner, rec_source, rec_target, rec_weight):
    n = nx * ny
    fields, rows, cols = flux.shape
    orows, ocols = diffusivity.shape
    records = rec_owner.shape[0]
    cap = max(2, 2 * records // n)
    nwb = remap_bank.shape[0]
    depth = 3 * TILE_X * TILE_Y
    tiles = rows // TILE_X * (cols // TILE_Y)
    span = cap * fields
    f32, bf16 = jnp.float32, jnp.bfloat16
    v = pltpu.VMEM
    dma = pltpu.SemaphoreType.DMA
    vm = pl.BlockSpec(memory_space=pltpu.VMEM)
    flat = [x.reshape(1, records) for x in (rec_owner, rec_source, rec_target, rec_weight)]
    return pl.pallas_call(
        functools.partial(kernel, nx, ny, cap),
        out_shape=jax.ShapeDtypeStruct((fields, orows, ocols), f32),
        in_specs=[pl.BlockSpec(memory_space=pl.ANY)] * 7,
        out_specs=vm,
        scratch_shapes=[
            v((fields, rows, cols), f32),
            v((orows, ocols), f32),
            v((4, 1, records), jnp.int32),
            dma((6,)),
            v((nwb, depth, LANES), bf16),
            v((3, 2, (fields + 1) * rows, LANES), f32),
            v((tiles * fields, depth), bf16),
            v((nwb * tiles, fields, LANES), f32),
            v((n, LANES), jnp.int32),
            pltpu.SMEM((n, LANES), jnp.int32),
            v((n // 2, 2, 1, LANES), f32),
            v((n // 2, 2, 1, LANES), f32),
            v((n, span, LANES), bf16),
            v((n, span, LANES), bf16),
            v((2, 2, fields, LANES), f32),
            v((2, 2, fields, LANES), f32),
            v((2, rows, LANES), f32),
            v((2, rows, LANES), f32),
            v((2, orows, LANES), f32),
            v((2, 2, 8, LANES), f32),
            v((2, 8, LANES), f32),
            v((fields * orows + OTILE_X, LANES), f32),
            v((4, max(orows, fields * 8), LANES), f32),
            v((2, orows, LANES), f32),
            v((2, 2, 8, LANES), f32),
            v((2, fields * 8, LANES), f32),
            v((fields * orows * ocols // LANES, LANES), bf16),
            v((fields * orows * ocols // LANES, LANES), bf16),
            v((fields * orows * ocols // LANES, n * span), bf16),
            dma, dma,
            dma, dma((2,)), dma, dma,
            dma((21,)), dma((21,)),
        ],
        compiler_params=pltpu.CompilerParams(
            collective_id=0, has_side_effects=True, vmem_limit_bytes=64 * 1024 * 1024 - 128 * 1024
        ),
    )(flux, diffusivity, remap_bank.reshape(nwb, depth, LANES), *flat)


def solution(mesh):
    in_specs = (
        P(None, "gx", "gy"),
        P("gx", "gy"),
        P(),
        P(("gx", "gy")),
        P(("gx", "gy")),
        P(("gx", "gy")),
        P(("gx", "gy")),
    )
    out_specs = P(None, "gx", "gy")
    body = functools.partial(local, mesh.shape["gx"], mesh.shape["gy"])
    return jax.shard_map(body, mesh=mesh, in_specs=in_specs, out_specs=out_specs, check_vma=False)
```

```python
import functools

import jax
import jax.numpy as jnp
from jax import lax
from jax.experimental import pallas as pl
from jax.experimental.pallas import tpu as pltpu
from jax.sharding import PartitionSpec as P

TILE_X = 16
TILE_Y = 16
OTILE_X = 8
OTILE_Y = 16
SWEEPS = 4
LANES = 128
MESH = pl.DeviceIdType.MESH


def lane_of(shape):
    return lax.broadcasted_iota(jnp.int32, shape, len(shape) - 1)


def block_transpose(parts, width):
    parts = list(parts)
    block = lane_of(parts[0].shape) // width
    step = 1
    while step < len(parts):
        keep = (block & step) == 0
        for i in range(len(parts)):
            if i & step == 0:
                j = i | step
                low, high = parts[i], parts[j]
                parts[i] = jnp.where(keep, low, pltpu.roll(high, step * width, 1))
                parts[j] = jnp.where(keep, pltpu.roll(low, LANES - step * width, 1), high)
        step *= 2
    return parts


def kernel(
    nx, ny, cap,
    flux_h, diff_h, bank, own_h, src_h, tgt_h, wgt_h,
    out, last_step,
    flux, diff, recs, in_sem,
    bank_v, xs, xmat, prod, table_v, table_s, meta_s, meta_r, sent, got,
    row_s, row_r, col_s, col_r, d_edge, d_corner, d_row, u, pack_s, u_edge, u_corner, u_row, part_s, part_r, hot,
    bank_sem, table_sem, a_send, a_recv, m_send, m_recv, h_send, h_recv,
):
    n = nx * ny
    fields, rows, cols = flux.shape
    nwb = bank.shape[0]
    tiles_x, tiles_y = rows // TILE_X, cols // TILE_Y
    tiles = tiles_x * tiles_y
    orows = diff.shape[0]
    oty = diff.shape[1] // OTILE_Y
    otx = orows // OTILE_X
    span = cap * fields
    gx, gy = lax.axis_index("gx"), lax.axis_index("gy")
    me = gx * ny + gy
    up, down = lax.rem(gx + nx - 1, nx), lax.rem(gx + 1, nx)
    left, right = lax.rem(gy + ny - 1, ny), lax.rem(gy + 1, ny)

    barrier = pltpu.get_barrier_semaphore()

    y_order = [o for k in range(ny // 2 + 1) for o in sorted({ny // 2 - k, ny // 2 + k}) if o < ny]
    y_at = [gy if o == 0 else lax.rem(gy + o, ny) for o in y_order]

    def each_other(act):
        def one_row(i, c):
            x = lax.rem(gx + i, nx)
            for o, y in zip(y_order, y_at):
                if o:
                    act(x, y)
                else:
                    pl.when(i != 0)(functools.partial(act, x, y))
            return c

        lax.fori_loop(0, nx, one_row, 0)

    hy = ny // 2
    hn = n // 2
    base = gy // hy * hy
    other = hy - base
    mine_j = gy - base
    place = gx * hy + mine_j
    j_order = [o for k in range(hy // 2 + 1) for o in sorted({hy // 2 - k, hy // 2 + k}) if o < hy]
    j_at = [mine_j if o == 0 else lax.rem(mine_j + o, hy) for o in j_order]

    ins = [pltpu.make_async_copy(flux_h, flux, in_sem.at[0]), pltpu.make_async_copy(diff_h, diff, in_sem.at[1])]
    ins += [
        pltpu.make_async_copy(r, recs.at[i], in_sem.at[2 + i]) for i, r in enumerate((own_h, src_h, tgt_h, wgt_h))
    ]
    for c in ins:
        c.start()
    bank_copy = pltpu.make_async_copy(bank, bank_v, bank_sem)
    bank_copy.start()

    def greet(x, y):
        pl.semaphore_signal(barrier, inc=1, device_id=(x, y), device_id_type=MESH)

    each_other(greet)

    ins[0].wait()
    for f in range(fields):
        for h in range(2):
            xs[0, h, f * rows : (f + 1) * rows, :] = flux[f, :, h * LANES : (h + 1) * LANES]
    lane_c = lane_of((rows, LANES))
    first = jnp.zeros((rows, LANES), jnp.float32)
    last = jnp.zeros((rows, LANES), jnp.float32)
    for f in range(fields):
        a = flux[f, :, 0:LANES]
        b = flux[f, :, cols - LANES : cols]
        first = jnp.where(lane_c == f, pltpu.roll(a, f, 1) if f else a, first)
        last = jnp.where(lane_c == f, pltpu.roll(b, f + 1, 1), last)
    col_s[0] = first
    col_s[1] = last
    for h in range(2):
        row_s[0, h] = xs[0, h, pl.ds(0, fields, stride=rows), :]
        row_s[1, h] = xs[0, h, pl.ds(rows - 1, fields, stride=rows), :]

    ins[1].wait()
    pl.semaphore_wait(barrier, n - 1)

    def remote(a, b, k, x, y):
        return pltpu.make_async_remote_copy(
            src_ref=a, dst_ref=b, send_sem=h_send.at[k], recv_sem=h_recv.at[k],
            device_id=(x, y), device_id_type=MESH,
        )

    flux_copies = [
        remote(row_s.at[0], row_r.at[1], 0, up, gy),
        remote(row_s.at[1], row_r.at[0], 1, down, gy),
        remote(col_s.at[0], col_r.at[1], 2, gx, left),
        remote(col_s.at[1], col_r.at[0], 3, gx, right),
    ]
    for c in flux_copies:
        c.start()

    def halo_copies(base, edge0, edge1, row0, row1, edge, corner, row):
        low = pl.ds(0, 8)
        high = pl.ds(orows - 8, 8)
        return [
            remote(edge0, edge.at[1], base, gx, left),
            remote(edge1, edge.at[0], base + 1, gx, right),
            remote(row0, row.at[1], base + 2, up, gy),
            remote(row1, row.at[0], base + 3, down, gy),
            remote(edge0.at[low], corner.at[1, 1], base + 4, up, left),
            remote(edge0.at[high], corner.at[0, 1], base + 5, down, left),
            remote(edge1.at[low], corner.at[1, 0], base + 6, up, right),
            remote(edge1.at[high], corner.at[0, 0], base + 7, down, right),
        ]

    diff_copies = halo_copies(
        4, diff, diff, diff.at[pl.ds(0, 8)], diff.at[pl.ds(orows - 8, 8)], d_edge, d_corner, d_row
    )
    for c in diff_copies:
        c.start()

    for c in ins[2:]:
        c.wait()
    records = recs.shape[2]
    owner_i = lax.broadcasted_iota(jnp.int32, (n, records), 0)
    member = recs[0] == owner_i
    lower = lax.broadcasted_iota(jnp.int32, (records, records), 0) < lane_of((records, records))
    before = jnp.dot(
        member.astype(jnp.bfloat16), lower.astype(jnp.bfloat16), preferred_element_type=jnp.float32
    )
    source, target = recs[1], recs[2]
    code = (recs[3] * tiles + lax.rem(source, tiles_y) * tiles_x + source // tiles_y).astype(jnp.float32)
    aim = (lax.rem(target, oty) * (fields * otx) + target // oty).astype(jnp.float32)
    lane = lane_of((n, LANES))
    slot_lane = lax.rem(lane, span) // fields
    field_lane = (lax.rem(lane, fields) * otx).astype(jnp.float32)
    table = jnp.zeros((n, LANES), jnp.float32)
    meta = jnp.full((n, LANES), -1.0, jnp.float32)
    for k in range(cap):
        hit = jnp.logical_and(member, before == k)
        code_k = jnp.sum(jnp.where(hit, code, 0.0), axis=1, keepdims=True)
        aim_k = jnp.sum(jnp.where(hit, aim + 1.0, 0.0), axis=1, keepdims=True) - 1.0
        table = jnp.where(lane == k, code_k, table)
        filled = jnp.where(aim_k >= 0.0, aim_k + field_lane, -1.0)
        meta = jnp.where(slot_lane == k, filled, meta)
    table_v[...] = table.astype(jnp.int32)
    table_copy = pltpu.make_async_copy(table_v, table_s, table_sem)
    table_copy.start()
    for o in range(n):
        meta_s[o // ny * hy + o % hy, o % ny // hy] = meta[o : o + 1, :]
    meta_r[place] = meta_s[place]

    def parties(kind, x, j):
        owner = x * ny + (base if kind else other) + j
        return owner, kind * hn + place, (x, base + j)

    def meta_to(x, j):
        return pltpu.make_async_remote_copy(
            src_ref=meta_s.at[x * hy + j], dst_ref=meta_r.at[place], send_sem=m_send, recv_sem=m_recv,
            device_id=(x, base + j), device_id_type=MESH,
        )

    def data_to(kind, x, j):
        owner, slot, device = parties(kind, x, j)
        return pltpu.make_async_remote_copy(
            src_ref=sent.at[owner], dst_ref=got.at[slot], send_sem=a_send, recv_sem=a_recv.at[kind],
            device_id=device, device_id_type=MESH,
        )

    def half_others(act):
        def one_row(i, c):
            x = lax.rem(gx + i, nx)
            for k, j in zip(j_order, j_at):
                if k:
                    act(x, j)
                else:
                    pl.when(i != 0)(functools.partial(act, x, j))
            return c

        lax.fori_loop(0, nx, one_row, 0)

    half_others(lambda x, j: meta_to(x, j).start())

    per = LANES // TILE_Y
    halfx = TILE_X // per
    tile_rows = tiles_x * fields

    def spread(ch, carry):
        c, h = ch // 2, lax.rem(ch, 2)
        for g in range(halfx):
            parts = [
                jnp.concatenate(
                    [
                        xs[c, h, pl.ds(t * TILE_X + g * per + a, fields, stride=rows), :]
                        for t in range(tiles_x)
                    ],
                    axis=0,
                )
                for a in range(per)
            ]
            parts = block_transpose(parts, TILE_Y)
            at = pl.ds(pl.multiple_of((c * halfx + g) * LANES, LANES), LANES)
            for t in range(per):
                row = pl.ds(pl.multiple_of((h * per + t) * tile_rows, tile_rows), tile_rows)
                xmat[row, at] = parts[t].astype(jnp.bfloat16)
        return carry

    lax.fori_loop(0, 2, spread, 0)

    for c in flux_copies:
        c.wait()
    row_i = lax.broadcasted_iota(jnp.int32, (rows, LANES), 0)
    at_first, at_last = lane_c == 0, lane_c == LANES - 1

    def slopes(f, carry):
        halves = [flux[f, :, h * LANES : (h + 1) * LANES] for h in range(2)]
        ends = (pltpu.roll(col_r[0], lax.rem(LANES - f, LANES), 1), pltpu.roll(col_r[1], LANES - 1 - f, 1))
        to_right = [pltpu.roll(x, 1, 1) for x in halves]
        to_left = [pltpu.roll(x, LANES - 1, 1) for x in halves]
        before_y = [jnp.where(at_first, ends[0], to_right[0]), jnp.where(at_first, to_right[0], to_right[1])]
        after_y = [jnp.where(at_last, to_left[1], to_left[0]), jnp.where(at_last, ends[1], to_left[1])]
        at = pl.ds(pl.multiple_of(f * rows, rows), rows)
        for h in range(2):
            x = halves[h]
            above = jnp.where(row_i == 0, row_r[0, h, pl.ds(f, 1), :], pltpu.roll(x, 1, 0))
            below = jnp.where(row_i == rows - 1, row_r[1, h, pl.ds(f, 1), :], pltpu.roll(x, rows - 1, 0))
            xs[1, h, at, :] = (below - above) * 0.5
            xs[2, h, at, :] = (after_y[h] - before_y[h]) * 0.5
        return carry

    lax.fori_loop(0, fields, slopes, 0)
    lax.fori_loop(2, 6, spread, 0)
    bank_copy.wait()

    def products(p, c):
        pair = jnp.concatenate([bank_v[2 * p], bank_v[2 * p + 1]], axis=1)
        got_pair = jnp.dot(xmat[...], pair, preferred_element_type=jnp.float32)
        prod[pl.ds(2 * p * tiles, tiles)] = got_pair[:, :LANES].reshape(tiles, fields, LANES)
        prod[pl.ds((2 * p + 1) * tiles, tiles)] = got_pair[:, LANES:].reshape(tiles, fields, LANES)
        return c

    lax.fori_loop(0, nwb // 2, products, 0)
    table_copy.wait()

    def record(d, s):
        return prod[jnp.clip(table_s[d, s], 0, nwb * tiles - 1)]

    def fill(d, ref, at):
        for s in range(0, cap, 2):
            pair = jnp.concatenate([record(d, s), record(d, s + 1)], axis=0)
            ref[at, s * fields : (s + 2) * fields, :] = pair.astype(jnp.bfloat16)

    for kind in range(2):

        def send_data(x, j):
            d = parties(kind, x, j)[0]
            fill(d, sent, d)
            data_to(kind, x, j).start()

        half_others(send_data)
        fill(gx * ny + (base if kind else other) + mine_j, got, kind * hn + place)

    cells = fields * otx * oty
    shares = LANES // span
    depth = hn * span
    cell_i = lax.broadcasted_iota(jnp.int32, (cells, LANES), 0).astype(jnp.float32)
    part_lane = lane_of((1, LANES)) // span
    mine_half = gy // hy

    def whole(src_ref, dst_ref, send_sem, recv_sem):
        return pltpu.make_async_remote_copy(
            src_ref=src_ref, dst_ref=dst_ref, send_sem=send_sem, recv_sem=recv_sem,
            device_id=(gx, other + mine_j), device_id_type=MESH,
        )

    meta_all = whole(meta_s.at[pl.ds(0, hn - 1)], meta_r.at[pl.ds(0, hn - 1)], m_send, m_recv)
    meta_all.wait_recv()
    for kind in range(2):
        row = mine_half if kind else 1 - mine_half
        for b in range(depth // LANES):
            aims = meta_r[b * shares, row]
            for i in range(1, shares):
                aims = jnp.where(part_lane == i, meta_r[b * shares + i, row], aims)
            at = kind * depth + b * LANES
            hot[:, at : at + LANES] = jnp.where(cell_i == aims, 1.0, 0.0).astype(jnp.bfloat16)

    def collect(kind):
        ref = got.at[pl.ds(kind * hn, hn - 1)]
        whole(ref, ref, a_send, a_recv.at[kind]).wait_recv()
        data = got[kind * hn : (kind + 1) * hn].reshape(depth, LANES)
        return jnp.dot(hot[:, kind * depth : (kind + 1) * depth], data, preferred_element_type=jnp.float32)

    part_s[...] = collect(0).astype(jnp.bfloat16)
    cross = remote(part_s, part_r, 20, gx, other + mine_j)
    cross.start()
    total = collect(1)
    cross.wait()
    total = total + part_r[...].astype(jnp.float32)
    high = fields * otx
    parts = block_transpose([total[t * high : (t + 1) * high, :] for t in range(oty)], OTILE_Y)
    for a in range(OTILE_X):
        u[pl.ds(a, high, stride=OTILE_X), :] = parts[a]

    lane_o = lane_of((orows, LANES))
    packed = [jnp.zeros((orows, LANES), jnp.float32) for _ in range(2)]
    for f in range(fields):
        block = u[f * orows : (f + 1) * orows, :]
        shift = f * SWEEPS
        rolled = (pltpu.roll(block, shift, 1), pltpu.roll(block, LANES - shift, 1)) if f else (block, block)
        mine = (lane_o // SWEEPS == f, (LANES - 1 - lane_o) // SWEEPS == f)
        packed = [jnp.where(mine[e], rolled[e], packed[e]) for e in range(2)]
        pack_s[2, f * 8 : f * 8 + 8, :] = block[0:8]
        pack_s[3, f * 8 : f * 8 + 8, :] = block[orows - 8 : orows]
    pack_s[0, 0:orows, :] = packed[0]
    pack_s[1, 0:orows, :] = packed[1]
    ocean_copies = halo_copies(
        12,
        pack_s.at[0, pl.ds(0, orows)],
        pack_s.at[1, pl.ds(0, orows)],
        pack_s.at[2, pl.ds(0, fields * 8)],
        pack_s.at[3, pl.ds(0, fields * 8)],
        u_edge, u_corner, u_row,
    )
    for c in ocean_copies:
        c.start()

    meta_all.wait_send()
    ref = sent.at[pl.ds(0, 2 * (hn - 1))]
    whole(ref, ref, a_send, a_recv.at[0]).wait_send()
    for c in diff_copies:
        c.wait()

    has = (gx > 0, gx < nx - 1, gy > 0, gy < ny - 1)
    tail_lane = lane_of((8, LANES)) < LANES // 2
    tail_row = lax.broadcasted_iota(jnp.int32, (8, LANES), 0) < 4
    wide_lane = lane_o < LANES // 2
    row_ok = jnp.where(tail_row, has[1].astype(jnp.float32), has[0].astype(jnp.float32))
    col_ok = jnp.where(wide_lane, has[3].astype(jnp.float32), has[2].astype(jnp.float32))
    both_ok = row_ok * col_ok[0:8]
    d_tail = jnp.where(tail_row, d_row[1], d_row[0]) * row_ok
    d_side = jnp.where(wide_lane, d_edge[1], d_edge[0]) * col_ok
    d_both = (
        jnp.where(
            tail_lane,
            jnp.where(tail_row, d_corner[1, 1], d_corner[0, 1]),
            jnp.where(tail_row, d_corner[1, 0], d_corner[0, 0]),
        )
        * both_ok
    )
    d = [
        jnp.concatenate([diff[...], d_tail], axis=0),
        jnp.concatenate([d_side, d_both], axis=0),
    ]
    for c in ocean_copies:
        c.wait()
    side = [
        jnp.concatenate([u_edge[e], jnp.where(tail_row, u_corner[1, e], u_corner[0, e])], axis=0)
        for e in range(2)
    ]
    ext = orows + 8
    lane_e = lane_of((ext, LANES))
    side_ok = jnp.concatenate([col_ok, both_ok], axis=0)
    at_first, at_last = lane_e == 0, lane_e == LANES - 1
    def opened(f):
        at = pl.ds(pl.multiple_of(f * 8, 8), 8)
        tail = jnp.where(tail_row, u_row[1, at, :], u_row[0, at, :]) * row_ok
        shift = f * SWEEPS
        rolled = (pltpu.roll(side[1], lax.rem(LANES - shift, LANES), 1), pltpu.roll(side[0], shift, 1))
        return [
            jnp.concatenate([u[pl.ds(pl.multiple_of(f * orows, orows), orows), :], tail], axis=0),
            jnp.where(lane_e < LANES // 2, rolled[0], rolled[1]) * side_ok,
        ]

    def change(x):
        to_right = [pltpu.roll(v, 1, 1) for v in x]
        to_left = [pltpu.roll(v, LANES - 1, 1) for v in x]
        beside = [
            jnp.where(at_first, to_right[1 - h], to_right[h])
            + jnp.where(at_last, to_left[1 - h], to_left[h])
            + pltpu.roll(x[h], 1, 0)
            + pltpu.roll(x[h], ext - 1, 0)
            for h in range(2)
        ]
        return [d[h] * (beside[h] - 4.0 * x[h]) for h in range(2)]

    def sweeps(k, carry):
        pair = [opened(2 * k), opened(2 * k + 1)]
        for sweep in range(SWEEPS - 1):
            steps = [change(x) for x in pair]
            pair = [[x[h] + y[h] for h in range(2)] for x, y in zip(pair, steps)]
        for i, x in enumerate(pair):
            out[2 * k + i] = x[0][0:orows, :]
            last_step[2 * k + i] = change(x)[0][0:orows, :]
        return carry

    lax.fori_loop(0, fields // 2, sweeps, 0)


def local(nx, ny, flux, diffusivity, remap_bank, rec_owner, rec_source, rec_target, rec_weight):
    n = nx * ny
    fields, rows, cols = flux.shape
    orows, ocols = diffusivity.shape
    records = rec_owner.shape[0]
    cap = max(2, 2 * records // n)
    nwb = remap_bank.shape[0]
    depth = 3 * TILE_X * TILE_Y
    tiles = rows // TILE_X * (cols // TILE_Y)
    span = cap * fields
    f32, bf16 = jnp.float32, jnp.bfloat16
    v = pltpu.VMEM
    dma = pltpu.SemaphoreType.DMA
    vm = pl.BlockSpec(memory_space=pltpu.VMEM)
    flat = [x.reshape(1, records) for x in (rec_owner, rec_source, rec_target, rec_weight)]
    state, last_step = pl.pallas_call(
        functools.partial(kernel, nx, ny, cap),
        out_shape=[jax.ShapeDtypeStruct((fields, orows, ocols), f32)] * 2,
        in_specs=[pl.BlockSpec(memory_space=pl.ANY)] * 7,
        out_specs=[vm, vm],
        scratch_shapes=[
            v((fields, rows, cols), f32),
            v((orows, ocols), f32),
            v((4, 1, records), jnp.int32),
            dma((6,)),
            v((nwb, depth, LANES), bf16),
            v((3, 2, (fields + 1) * rows, LANES), f32),
            v((tiles * fields, depth), bf16),
            v((nwb * tiles, fields, LANES), f32),
            v((n, LANES), jnp.int32),
            pltpu.SMEM((n, LANES), jnp.int32),
            v((n // 2, 2, 1, LANES), f32),
            v((n // 2, 2, 1, LANES), f32),
            v((n, span, LANES), bf16),
            v((n, span, LANES), bf16),
            v((2, 2, fields, LANES), f32),
            v((2, 2, fields, LANES), f32),
            v((2, rows, LANES), f32),
            v((2, rows, LANES), f32),
            v((2, orows, LANES), f32),
            v((2, 2, 8, LANES), f32),
            v((2, 8, LANES), f32),
            v((fields * orows + OTILE_X, LANES), f32),
            v((4, max(orows, fields * 8), LANES), f32),
            v((2, orows, LANES), f32),
            v((2, 2, 8, LANES), f32),
            v((2, fields * 8, LANES), f32),
            v((fields * orows * ocols // LANES, LANES), bf16),
            v((fields * orows * ocols // LANES, LANES), bf16),
            v((fields * orows * ocols // LANES, n * span), bf16),
            dma, dma,
            dma, dma((2,)), dma, dma,
            dma((21,)), dma((21,)),
        ],
        compiler_params=pltpu.CompilerParams(
            collective_id=0, has_side_effects=True, vmem_limit_bytes=64 * 1024 * 1024 - 128 * 1024
        ),
    )(flux, diffusivity, remap_bank.reshape(nwb, depth, LANES), *flat)
    return state + last_step


def solution(mesh):
    in_specs = (
        P(None, "gx", "gy"),
        P("gx", "gy"),
        P(),
        P(("gx", "gy")),
        P(("gx", "gy")),
        P(("gx", "gy")),
        P(("gx", "gy")),
    )
    out_specs = P(None, "gx", "gy")
    body = functools.partial(local, mesh.shape["gx"], mesh.shape["gy"])
    return jax.shard_map(body, mesh=mesh, in_specs=in_specs, out_specs=out_specs, check_vma=False)
```

```python
import functools

import jax
import jax.numpy as jnp
from jax import lax
from jax.experimental import pallas as pl
from jax.experimental.pallas import tpu as pltpu
from jax.sharding import PartitionSpec as P

TILE_X = 16
TILE_Y = 16
OTILE_X = 8
OTILE_Y = 16
SWEEPS = 4
LANES = 128
MESH = pl.DeviceIdType.MESH


def lane_of(shape):
    return lax.broadcasted_iota(jnp.int32, shape, len(shape) - 1)


def block_transpose(parts, width):
    parts = list(parts)
    block = lane_of(parts[0].shape) // width
    step = 1
    while step < len(parts):
        keep = (block & step) == 0
        for i in range(len(parts)):
            if i & step == 0:
                j = i | step
                low, high = parts[i], parts[j]
                parts[i] = jnp.where(keep, low, pltpu.roll(high, step * width, 1))
                parts[j] = jnp.where(keep, pltpu.roll(low, LANES - step * width, 1), high)
        step *= 2
    return parts


def kernel(
    nx, ny, cap,
    flux_h, diff_h, bank, own_h, src_h, tgt_h, wgt_h,
    out,
    flux, diff, recs, in_sem,
    bank_v, xs, xmat, prod, table_v, table_s, meta_s, meta_r, sent, got,
    row_s, row_r, col_s, col_r, d_edge, d_corner, d_row, u, pack_s, u_edge, u_corner, u_row, part_s, part_r, hot,
    bank_sem, table_sem, a_send, a_recv, m_send, m_recv, h_send, h_recv,
):
    n = nx * ny
    fields, rows, cols = flux.shape
    nwb = bank.shape[0]
    tiles_x, tiles_y = rows // TILE_X, cols // TILE_Y
    tiles = tiles_x * tiles_y
    orows = diff.shape[0]
    oty = diff.shape[1] // OTILE_Y
    otx = orows // OTILE_X
    span = cap * fields
    gx, gy = lax.axis_index("gx"), lax.axis_index("gy")
    me = gx * ny + gy
    up, down = lax.rem(gx + nx - 1, nx), lax.rem(gx + 1, nx)
    left, right = lax.rem(gy + ny - 1, ny), lax.rem(gy + 1, ny)

    barrier = pltpu.get_barrier_semaphore()

    hy = ny // 2
    hn = n // 2
    base = gy // hy * hy
    other = hy - base
    mine_j = gy - base
    place = gx * hy + mine_j
    j_order = [o for k in range(hy // 2 + 1) for o in sorted({hy // 2 - k, hy // 2 + k}) if o < hy]
    j_at = [mine_j if o == 0 else lax.rem(mine_j + o, hy) for o in j_order]

    def half_others(act):
        def one_row(i, c):
            x = lax.rem(gx + i, nx)
            for k, j in zip(j_order, j_at):
                if k:
                    act(x, j)
                else:
                    pl.when(i != 0)(functools.partial(act, x, j))
            return c

        lax.fori_loop(0, nx, one_row, 0)

    quarter = fields // 4
    flux_ins = [
        pltpu.make_async_copy(flux_h.at[pl.ds(i * quarter, quarter)], flux.at[pl.ds(i * quarter, quarter)], in_sem.at[5 + i])
        for i in range(4)
    ]
    ins = [
        pltpu.make_async_copy(r, recs.at[i], in_sem.at[i]) for i, r in enumerate((own_h, src_h, tgt_h, wgt_h))
    ]
    diff_in = pltpu.make_async_copy(diff_h, diff, in_sem.at[4])
    for c in flux_ins + ins + [diff_in]:
        c.start()
    bank_copy = pltpu.make_async_copy(bank, bank_v, bank_sem)

    def greet(x, y):
        pl.semaphore_signal(barrier, inc=1, device_id=(x, y), device_id_type=MESH)

    greet(gx, other + mine_j)
    for y, edge in ((left, 0), (right, hy - 1)):

        @pl.when(mine_j == edge)
        def _():
            for x in (up, gx, down):
                greet(x, y)

    half_others(lambda x, j: greet(x, base + j))
    beside_others = 3 * (mine_j == 0).astype(jnp.int32) + 3 * (mine_j == hy - 1).astype(jnp.int32)

    for c in flux_ins:
        c.wait()
    bank_copy.start()
    for f in range(fields):
        for h in range(2):
            xs[0, h, f * rows : (f + 1) * rows, :] = flux[f, :, h * LANES : (h + 1) * LANES]
    lane_c = lane_of((rows, LANES))
    first = jnp.zeros((rows, LANES), jnp.float32)
    last = jnp.zeros((rows, LANES), jnp.float32)
    for f in range(fields):
        a = flux[f, :, 0:LANES]
        b = flux[f, :, cols - LANES : cols]
        first = jnp.where(lane_c == f, pltpu.roll(a, f, 1) if f else a, first)
        last = jnp.where(lane_c == f, pltpu.roll(b, f + 1, 1), last)
    col_s[0] = first
    col_s[1] = last
    for h in range(2):
        row_s[0, h] = xs[0, h, pl.ds(0, fields, stride=rows), :]
        row_s[1, h] = xs[0, h, pl.ds(rows - 1, fields, stride=rows), :]

    pl.semaphore_wait(barrier, hn + beside_others)

    def remote(a, b, k, x, y):
        return pltpu.make_async_remote_copy(
            src_ref=a, dst_ref=b, send_sem=h_send.at[k], recv_sem=h_recv.at[k],
            device_id=(x, y), device_id_type=MESH,
        )

    flux_copies = [
        remote(row_s.at[0], row_r.at[1], 0, up, gy),
        remote(row_s.at[1], row_r.at[0], 1, down, gy),
        remote(col_s.at[0], col_r.at[1], 2, gx, left),
        remote(col_s.at[1], col_r.at[0], 3, gx, right),
    ]
    for c in flux_copies:
        c.start()

    def halo_copies(base, edge0, edge1, row0, row1, edge, corner, row):
        low = pl.ds(0, 8)
        high = pl.ds(orows - 8, 8)
        return [
            remote(edge0, edge.at[1], base, gx, left),
            remote(edge1, edge.at[0], base + 1, gx, right),
            remote(row0, row.at[1], base + 2, up, gy),
            remote(row1, row.at[0], base + 3, down, gy),
            remote(edge0.at[low], corner.at[1, 1], base + 4, up, left),
            remote(edge0.at[high], corner.at[0, 1], base + 5, down, left),
            remote(edge1.at[low], corner.at[1, 0], base + 6, up, right),
            remote(edge1.at[high], corner.at[0, 0], base + 7, down, right),
        ]

    for c in ins:
        c.wait()
    records = recs.shape[2]
    owner_i = lax.broadcasted_iota(jnp.int32, (n, records), 0)
    member = recs[0] == owner_i
    lower = lax.broadcasted_iota(jnp.int32, (records, records), 0) < lane_of((records, records))
    before = jnp.dot(
        member.astype(jnp.bfloat16), lower.astype(jnp.bfloat16), preferred_element_type=jnp.float32
    )
    source, target = recs[1], recs[2]
    code = (recs[3] * tiles + lax.rem(source, tiles_y) * tiles_x + source // tiles_y).astype(jnp.float32)
    aim = (lax.rem(target, oty) * (fields * otx) + target // oty).astype(jnp.float32)
    lane = lane_of((n, LANES))
    slot_lane = lax.rem(lane, span) // fields
    field_lane = (lax.rem(lane, fields) * otx).astype(jnp.float32)
    table = jnp.zeros((n, LANES), jnp.float32)
    meta = jnp.full((n, LANES), -1.0, jnp.float32)
    for k in range(cap):
        hit = jnp.logical_and(member, before == k)
        code_k = jnp.sum(jnp.where(hit, code, 0.0), axis=1, keepdims=True)
        aim_k = jnp.sum(jnp.where(hit, aim + 1.0, 0.0), axis=1, keepdims=True) - 1.0
        table = jnp.where(lane == k, code_k, table)
        filled = jnp.where(aim_k >= 0.0, aim_k + field_lane, -1.0)
        meta = jnp.where(slot_lane == k, filled, meta)
    table_v[...] = table.astype(jnp.int32)
    table_copy = pltpu.make_async_copy(table_v, table_s, table_sem)
    table_copy.start()
    for o in range(n):
        meta_s[o // ny * hy + o % hy, o % ny // hy] = meta[o : o + 1, :]
    meta_r[place] = meta_s[place]

    def parties(kind, x, j):
        owner = x * ny + (base if kind else other) + j
        return owner, kind * hn + place, (x, base + j)

    def meta_to(x, j):
        return pltpu.make_async_remote_copy(
            src_ref=meta_s.at[x * hy + j], dst_ref=meta_r.at[place], send_sem=m_send, recv_sem=m_recv,
            device_id=(x, base + j), device_id_type=MESH,
        )

    def data_to(kind, x, j):
        owner, slot, device = parties(kind, x, j)
        return pltpu.make_async_remote_copy(
            src_ref=sent.at[owner], dst_ref=got.at[slot], send_sem=a_send, recv_sem=a_recv.at[kind],
            device_id=device, device_id_type=MESH,
        )

    half_others(lambda x, j: meta_to(x, j).start())

    per = LANES // TILE_Y
    halfx = TILE_X // per
    tile_rows = tiles_x * fields
    def spread(c):
        for h in range(2):
            for g in range(halfx):
                parts = [
                    jnp.concatenate(
                        [
                            xs[c, h, pl.ds(t * TILE_X + g * per + a, fields, stride=rows), :]
                            for t in range(tiles_x)
                        ],
                        axis=0,
                    )
                    for a in range(per)
                ]
                parts = block_transpose(parts, TILE_Y)
                at = (c * halfx + g) * LANES
                for t in range(per):
                    j = h * per + t
                    xmat[j * tile_rows : (j + 1) * tile_rows, at : at + LANES] = parts[t].astype(jnp.bfloat16)

    spread(0)

    for c in flux_copies:
        c.wait()
    row_i = lax.broadcasted_iota(jnp.int32, (rows, LANES), 0)
    for f in range(fields):
        halves = [flux[f, :, h * LANES : (h + 1) * LANES] for h in range(2)]
        ends = (
            pltpu.roll(col_r[0], LANES - f, 1) if f else col_r[0],
            pltpu.roll(col_r[1], LANES - 1 - f, 1),
        )
        to_right = [pltpu.roll(x, 1, 1) for x in halves]
        to_left = [pltpu.roll(x, LANES - 1, 1) for x in halves]
        at_first, at_last = lane_c == 0, lane_c == LANES - 1
        before_y = [jnp.where(at_first, ends[0], to_right[0]), jnp.where(at_first, to_right[0], to_right[1])]
        after_y = [jnp.where(at_last, to_left[1], to_left[0]), jnp.where(at_last, ends[1], to_left[1])]
        for h in range(2):
            x = halves[h]
            above = jnp.where(row_i == 0, row_r[0, h, f : f + 1, :], pltpu.roll(x, 1, 0))
            below = jnp.where(row_i == rows - 1, row_r[1, h, f : f + 1, :], pltpu.roll(x, rows - 1, 0))
            xs[1, h, f * rows : (f + 1) * rows, :] = (below - above) * 0.5
            xs[2, h, f * rows : (f + 1) * rows, :] = (after_y[h] - before_y[h]) * 0.5

    spread(1)
    spread(2)
    bank_copy.wait()

    def products(p, c):
        pair = jnp.concatenate([bank_v[2 * p], bank_v[2 * p + 1]], axis=1)
        got_pair = jnp.dot(xmat[...], pair, preferred_element_type=jnp.float32)
        prod[pl.ds(2 * p * tiles, tiles)] = got_pair[:, :LANES].reshape(tiles, fields, LANES)
        prod[pl.ds((2 * p + 1) * tiles, tiles)] = got_pair[:, LANES:].reshape(tiles, fields, LANES)
        return c

    lax.fori_loop(0, nwb // 2, products, 0)
    table_copy.wait()

    def record(d, s):
        return prod[jnp.clip(table_s[d, s], 0, nwb * tiles - 1)]

    def fill(d, ref, at):
        for s in range(0, cap, 2):
            pair = jnp.concatenate([record(d, s), record(d, s + 1)], axis=0)
            ref[at, s * fields : (s + 2) * fields, :] = pair.astype(jnp.bfloat16)

    for kind in range(2):

        def send_data(x, j):
            d = parties(kind, x, j)[0]
            fill(d, sent, d)
            data_to(kind, x, j).start()

        half_others(send_data)
        fill(gx * ny + (base if kind else other) + mine_j, got, kind * hn + place)

    diff_in.wait()
    diff_copies = halo_copies(
        4, diff, diff, diff.at[pl.ds(0, 8)], diff.at[pl.ds(orows - 8, 8)], d_edge, d_corner, d_row
    )
    for c in diff_copies:
        c.start()

    cells = fields * otx * oty
    shares = LANES // span
    depth = hn * span
    cell_i = lax.broadcasted_iota(jnp.int32, (cells, LANES), 0).astype(jnp.float32)
    part_lane = lane_of((1, LANES)) // span
    mine_half = gy // hy

    def whole(src_ref, dst_ref, send_sem, recv_sem):
        return pltpu.make_async_remote_copy(
            src_ref=src_ref, dst_ref=dst_ref, send_sem=send_sem, recv_sem=recv_sem,
            device_id=(gx, other + mine_j), device_id_type=MESH,
        )

    meta_all = whole(meta_s.at[pl.ds(0, hn - 1)], meta_r.at[pl.ds(0, hn - 1)], m_send, m_recv)
    meta_all.wait_recv()
    for kind in range(2):
        row = mine_half if kind else 1 - mine_half
        for b in range(depth // LANES):
            aims = meta_r[b * shares, row]
            for i in range(1, shares):
                aims = jnp.where(part_lane == i, meta_r[b * shares + i, row], aims)
            at = kind * depth + b * LANES
            hot[:, at : at + LANES] = jnp.where(cell_i == aims, 1.0, 0.0).astype(jnp.bfloat16)

    def collect(kind):
        ref = got.at[pl.ds(kind * hn, hn - 1)]
        whole(ref, ref, a_send, a_recv.at[kind]).wait_recv()
        data = got[kind * hn : (kind + 1) * hn].reshape(depth, LANES)
        return jnp.dot(hot[:, kind * depth : (kind + 1) * depth], data, preferred_element_type=jnp.float32)

    part_s[...] = collect(0).astype(jnp.bfloat16)
    cross = remote(part_s, part_r, 20, gx, other + mine_j)
    cross.start()
    total = collect(1)
    cross.wait()
    total = total + part_r[...].astype(jnp.float32)
    high = fields * otx
    parts = block_transpose([total[t * high : (t + 1) * high, :] for t in range(oty)], OTILE_Y)
    for a in range(OTILE_X):
        u[pl.ds(a, high, stride=OTILE_X), :] = parts[a]

    lane_o = lane_of((orows, LANES))
    for f in range(fields):
        pack_s[2, f * 8 : f * 8 + 8, :] = u[f * orows : f * orows + 8, :]
        pack_s[3, f * 8 : f * 8 + 8, :] = u[(f + 1) * orows - 8 : (f + 1) * orows, :]
    ocean_copies = halo_copies(
        12,
        pack_s.at[0, pl.ds(0, orows)],
        pack_s.at[1, pl.ds(0, orows)],
        pack_s.at[2, pl.ds(0, fields * 8)],
        pack_s.at[3, pl.ds(0, fields * 8)],
        u_edge, u_corner, u_row,
    )
    for c in ocean_copies[2:4]:
        c.start()
    packed = [jnp.zeros((orows, LANES), jnp.float32) for _ in range(2)]
    for f in range(fields):
        block = u[f * orows : (f + 1) * orows, :]
        shift = f * SWEEPS
        rolled = (pltpu.roll(block, shift, 1), pltpu.roll(block, LANES - shift, 1)) if f else (block, block)
        mine = (lane_o // SWEEPS == f, (LANES - 1 - lane_o) // SWEEPS == f)
        packed = [jnp.where(mine[e], rolled[e], packed[e]) for e in range(2)]
    pack_s[0, 0:orows, :] = packed[0]
    pack_s[1, 0:orows, :] = packed[1]
    for c in ocean_copies[4:] + ocean_copies[:2]:
        c.start()

    meta_all.wait_send()
    ref = sent.at[pl.ds(0, 2 * (hn - 1))]
    whole(ref, ref, a_send, a_recv.at[0]).wait_send()
    for c in diff_copies:
        c.wait()

    has = (gx > 0, gx < nx - 1, gy > 0, gy < ny - 1)
    tail_lane = lane_of((8, LANES)) < LANES // 2
    tail_row = lax.broadcasted_iota(jnp.int32, (8, LANES), 0) < 4
    wide_lane = lane_o < LANES // 2
    row_ok = jnp.where(tail_row, has[1].astype(jnp.float32), has[0].astype(jnp.float32))
    col_ok = jnp.where(wide_lane, has[3].astype(jnp.float32), has[2].astype(jnp.float32))
    both_ok = row_ok * col_ok[0:8]
    d_tail = jnp.where(tail_row, d_row[1], d_row[0]) * row_ok
    d_side = jnp.where(wide_lane, d_edge[1], d_edge[0]) * col_ok
    d_both = (
        jnp.where(
            tail_lane,
            jnp.where(tail_row, d_corner[1, 1], d_corner[0, 1]),
            jnp.where(tail_row, d_corner[1, 0], d_corner[0, 0]),
        )
        * both_ok
    )
    d = [
        jnp.concatenate([diff[...], d_tail], axis=0),
        jnp.concatenate([d_side, d_both], axis=0),
    ]
    for c in ocean_copies:
        c.wait()
    side = [
        jnp.concatenate([u_edge[e], jnp.where(tail_row, u_corner[1, e], u_corner[0, e])], axis=0)
        for e in range(2)
    ]
    ext = orows + 8
    lane_e = lane_of((ext, LANES))
    side_ok = jnp.concatenate([col_ok, both_ok], axis=0)
    at_first, at_last = lane_e == 0, lane_e == LANES - 1
    def opened(f):
        shift = f * SWEEPS
        tail = jnp.where(tail_row, u_row[1, f * 8 : f * 8 + 8, :], u_row[0, f * 8 : f * 8 + 8, :]) * row_ok
        rolled = (
            (pltpu.roll(side[1], LANES - shift, 1), pltpu.roll(side[0], shift, 1)) if f else (side[1], side[0])
        )
        return [
            jnp.concatenate([u[f * orows : (f + 1) * orows, :], tail], axis=0),
            jnp.where(lane_e < LANES // 2, rolled[0], rolled[1]) * side_ok,
        ]

    def swept(x):
        to_right = [pltpu.roll(v, 1, 1) for v in x]
        to_left = [pltpu.roll(v, LANES - 1, 1) for v in x]
        beside = [
            jnp.where(at_first, to_right[1 - h], to_right[h])
            + jnp.where(at_last, to_left[1 - h], to_left[h])
            + pltpu.roll(x[h], 1, 0)
            + pltpu.roll(x[h], ext - 1, 0)
            for h in range(2)
        ]
        return [x[h] + d[h] * (beside[h] - 4.0 * x[h]) for h in range(2)]

    for f in range(0, fields, 2):
        pair = [opened(f), opened(f + 1)]
        for sweep in range(SWEEPS):
            pair = [swept(x) for x in pair]
        for i, x in enumerate(pair):
            out[f + i] = x[0][0:orows, :]


def local(nx, ny, flux, diffusivity, remap_bank, rec_owner, rec_source, rec_target, rec_weight):
    n = nx * ny
    fields, rows, cols = flux.shape
    orows, ocols = diffusivity.shape
    records = rec_owner.shape[0]
    cap = max(2, 2 * records // n)
    nwb = remap_bank.shape[0]
    depth = 3 * TILE_X * TILE_Y
    tiles = rows // TILE_X * (cols // TILE_Y)
    span = cap * fields
    f32, bf16 = jnp.float32, jnp.bfloat16
    v = pltpu.VMEM
    dma = pltpu.SemaphoreType.DMA
    vm = pl.BlockSpec(memory_space=pltpu.VMEM)
    flat = [x.reshape(1, records) for x in (rec_owner, rec_source, rec_target, rec_weight)]
    return pl.pallas_call(
        functools.partial(kernel, nx, ny, cap),
        out_shape=jax.ShapeDtypeStruct((fields, orows, ocols), f32),
        in_specs=[pl.BlockSpec(memory_space=pl.ANY)] * 7,
        out_specs=vm,
        scratch_shapes=[
            v((fields, rows, cols), f32),
            v((orows, ocols), f32),
            v((4, 1, records), jnp.int32),
            dma((9,)),
            v((nwb, depth, LANES), bf16),
            v((3, 2, (fields + 1) * rows, LANES), f32),
            v((tiles * fields, depth), bf16),
            v((nwb * tiles, fields, LANES), f32),
            v((n, LANES), jnp.int32),
            pltpu.SMEM((n, LANES), jnp.int32),
            v((n // 2, 2, 1, LANES), f32),
            v((n // 2, 2, 1, LANES), f32),
            v((n, span, LANES), bf16),
            v((n, span, LANES), bf16),
            v((2, 2, fields, LANES), f32),
            v((2, 2, fields, LANES), f32),
            v((2, rows, LANES), f32),
            v((2, rows, LANES), f32),
            v((2, orows, LANES), f32),
            v((2, 2, 8, LANES), f32),
            v((2, 8, LANES), f32),
            v((fields * orows + OTILE_X, LANES), f32),
            v((4, max(orows, fields * 8), LANES), f32),
            v((2, orows, LANES), f32),
            v((2, 2, 8, LANES), f32),
            v((2, fields * 8, LANES), f32),
            v((fields * orows * ocols // LANES, LANES), bf16),
            v((fields * orows * ocols // LANES, LANES), bf16),
            v((fields * orows * ocols // LANES, n * span), bf16),
            dma, dma,
            dma, dma((2,)), dma, dma,
            dma((21,)), dma((21,)),
        ],
        compiler_params=pltpu.CompilerParams(
            collective_id=0, has_side_effects=True, vmem_limit_bytes=64 * 1024 * 1024 - 128 * 1024
        ),
    )(flux, diffusivity, remap_bank.reshape(nwb, depth, LANES), *flat)


def solution(mesh):
    in_specs = (
        P(None, "gx", "gy"),
        P("gx", "gy"),
        P(),
        P(("gx", "gy")),
        P(("gx", "gy")),
        P(("gx", "gy")),
        P(("gx", "gy")),
    )
    out_specs = P(None, "gx", "gy")
    body = functools.partial(local, mesh.shape["gx"], mesh.shape["gy"])
    return jax.shard_map(body, mesh=mesh, in_specs=in_specs, out_specs=out_specs, check_vma=False)
```

```python
import functools

import jax
import jax.numpy as jnp
from jax import lax
from jax.experimental import pallas as pl
from jax.experimental.pallas import tpu as pltpu
from jax.sharding import PartitionSpec as P

TILE_X = 16
TILE_Y = 16
OTILE_X = 8
OTILE_Y = 16
SWEEPS = 4
LANES = 128
MESH = pl.DeviceIdType.MESH


def lane_of(shape):
    return lax.broadcasted_iota(jnp.int32, shape, len(shape) - 1)


def block_transpose(parts, width):
    parts = list(parts)
    block = lane_of(parts[0].shape) // width
    step = 1
    while step < len(parts):
        keep = (block & step) == 0
        for i in range(len(parts)):
            if i & step == 0:
                j = i | step
                low, high = parts[i], parts[j]
                parts[i] = jnp.where(keep, low, pltpu.roll(high, step * width, 1))
                parts[j] = jnp.where(keep, pltpu.roll(low, LANES - step * width, 1), high)
        step *= 2
    return parts


def kernel(
    nx, ny, cap,
    flux_h, diff_h, bank, own_h, src_h, tgt_h, wgt_h,
    out,
    flux, diff, recs, in_sem,
    bank_v, xs, xmat, prod, table_v, table_s, meta_s, meta_r, sent, got,
    row_s, row_r, col_s, col_r, d_edge, d_corner, d_row, u, pack_s, u_edge, u_corner, u_row, part_s, part_r, hot,
    bank_sem, table_sem, a_send, a_recv, m_send, m_recv, h_send, h_recv,
):
    n = nx * ny
    fields, rows, cols = flux.shape
    nwb = 2 * bank.shape[0]
    tiles_x, tiles_y = rows // TILE_X, cols // TILE_Y
    tiles = tiles_x * tiles_y
    orows = diff.shape[0]
    oty = diff.shape[1] // OTILE_Y
    otx = orows // OTILE_X
    span = cap * fields
    gx, gy = lax.axis_index("gx"), lax.axis_index("gy")
    me = gx * ny + gy
    up, down = lax.rem(gx + nx - 1, nx), lax.rem(gx + 1, nx)
    left, right = lax.rem(gy + ny - 1, ny), lax.rem(gy + 1, ny)

    barrier = pltpu.get_barrier_semaphore()

    hy = ny // 2
    hn = n // 2
    base = gy // hy * hy
    other = hy - base
    mine_j = gy - base
    place = gx * hy + mine_j
    j_order = [o for k in range(hy // 2 + 1) for o in sorted({hy // 2 - k, hy // 2 + k}) if o < hy]
    j_at = [mine_j if o == 0 else lax.rem(mine_j + o, hy) for o in j_order]

    def half_others(act):
        def one_row(i, c):
            x = lax.rem(gx + i, nx)
            for k, j in zip(j_order, j_at):
                if k:
                    act(x, j)
                else:
                    pl.when(i != 0)(functools.partial(act, x, j))
            return c

        lax.fori_loop(0, nx, one_row, 0)

    quarter = fields // 4
    flux_ins = [
        pltpu.make_async_copy(flux_h.at[pl.ds(i * quarter, quarter)], flux.at[pl.ds(i * quarter, quarter)], in_sem.at[5 + i])
        for i in range(4)
    ]
    ins = [
        pltpu.make_async_copy(r, recs.at[i], in_sem.at[i]) for i, r in enumerate((own_h, src_h, tgt_h, wgt_h))
    ]
    diff_in = pltpu.make_async_copy(diff_h, diff, in_sem.at[4])
    for c in flux_ins + ins + [diff_in]:
        c.start()
    bank_copies = [
        pltpu.make_async_copy(bank.at[:, i], bank_v.at[:, :, pl.ds(i * LANES, LANES)], bank_sem.at[i]) for i in range(2)
    ]

    def greet(x, y):
        pl.semaphore_signal(barrier, inc=1, device_id=(x, y), device_id_type=MESH)

    greet(gx, other + mine_j)
    for y, edge in ((left, 0), (right, hy - 1)):

        @pl.when(mine_j == edge)
        def _():
            for x in (up, gx, down):
                greet(x, y)

    half_others(lambda x, j: greet(x, base + j))
    beside_others = 3 * (mine_j == 0).astype(jnp.int32) + 3 * (mine_j == hy - 1).astype(jnp.int32)

    for c in flux_ins:
        c.wait()
    for c in bank_copies:
        c.start()
    for f in range(fields):
        for h in range(2):
            xs[0, h, f * rows : (f + 1) * rows, :] = flux[f, :, h * LANES : (h + 1) * LANES]
    lane_c = lane_of((rows, LANES))
    first = jnp.zeros((rows, LANES), jnp.float32)
    last = jnp.zeros((rows, LANES), jnp.float32)
    for f in range(fields):
        a = flux[f, :, 0:LANES]
        b = flux[f, :, cols - LANES : cols]
        first = jnp.where(lane_c == f, pltpu.roll(a, f, 1) if f else a, first)
        last = jnp.where(lane_c == f, pltpu.roll(b, f + 1, 1), last)
    col_s[0] = first
    col_s[1] = last
    for h in range(2):
        row_s[0, h] = xs[0, h, pl.ds(0, fields, stride=rows), :]
        row_s[1, h] = xs[0, h, pl.ds(rows - 1, fields, stride=rows), :]

    pl.semaphore_wait(barrier, hn + beside_others)

    def remote(a, b, k, x, y):
        return pltpu.make_async_remote_copy(
            src_ref=a, dst_ref=b, send_sem=h_send.at[k], recv_sem=h_recv.at[k],
            device_id=(x, y), device_id_type=MESH,
        )

    flux_copies = [
        remote(row_s.at[0], row_r.at[1], 0, up, gy),
        remote(row_s.at[1], row_r.at[0], 1, down, gy),
        remote(col_s.at[0], col_r.at[1], 2, gx, left),
        remote(col_s.at[1], col_r.at[0], 3, gx, right),
    ]
    for c in flux_copies:
        c.start()

    def halo_copies(base, edge0, edge1, row0, row1, edge, corner, row):
        low = pl.ds(0, 8)
        high = pl.ds(orows - 8, 8)
        return [
            remote(edge0, edge.at[1], base, gx, left),
            remote(edge1, edge.at[0], base + 1, gx, right),
            remote(row0, row.at[1], base + 2, up, gy),
            remote(row1, row.at[0], base + 3, down, gy),
            remote(edge0.at[low], corner.at[1, 1], base + 4, up, left),
            remote(edge0.at[high], corner.at[0, 1], base + 5, down, left),
            remote(edge1.at[low], corner.at[1, 0], base + 6, up, right),
            remote(edge1.at[high], corner.at[0, 0], base + 7, down, right),
        ]

    for c in ins:
        c.wait()
    records = recs.shape[2]
    owner_i = lax.broadcasted_iota(jnp.int32, (n, records), 0)
    member = recs[0] == owner_i
    lower = lax.broadcasted_iota(jnp.int32, (records, records), 0) < lane_of((records, records))
    before = jnp.dot(
        member.astype(jnp.bfloat16), lower.astype(jnp.bfloat16), preferred_element_type=jnp.float32
    )
    source, target = recs[1], recs[2]
    code = (recs[3] * tiles + lax.rem(source, tiles_y) * tiles_x + source // tiles_y).astype(jnp.float32)
    aim = (lax.rem(target, oty) * (fields * otx) + target // oty).astype(jnp.float32)
    lane = lane_of((n, LANES))
    slot_lane = lax.rem(lane, span) // fields
    field_lane = (lax.rem(lane, fields) * otx).astype(jnp.float32)
    table = jnp.zeros((n, LANES), jnp.float32)
    meta = jnp.full((n, LANES), -1.0, jnp.float32)
    for k in range(cap):
        hit = jnp.logical_and(member, before == k)
        code_k = jnp.sum(jnp.where(hit, code, 0.0), axis=1, keepdims=True)
        aim_k = jnp.sum(jnp.where(hit, aim + 1.0, 0.0), axis=1, keepdims=True) - 1.0
        table = jnp.where(lane == k, code_k, table)
        filled = jnp.where(aim_k >= 0.0, aim_k + field_lane, -1.0)
        meta = jnp.where(slot_lane == k, filled, meta)
    table_v[...] = table.astype(jnp.int32)
    table_copy = pltpu.make_async_copy(table_v, table_s, table_sem)
    table_copy.start()
    for o in range(n):
        meta_s[o // ny * hy + o % hy, o % ny // hy] = meta[o : o + 1, :]
    meta_r[place] = meta_s[place]

    def parties(kind, x, j):
        owner = x * ny + (base if kind else other) + j
        return owner, kind * hn + place, (x, base + j)

    def meta_to(x, j):
        return pltpu.make_async_remote_copy(
            src_ref=meta_s.at[x * hy + j], dst_ref=meta_r.at[place], send_sem=m_send, recv_sem=m_recv,
            device_id=(x, base + j), device_id_type=MESH,
        )

    def data_to(kind, x, j):
        owner, slot, device = parties(kind, x, j)
        return pltpu.make_async_remote_copy(
            src_ref=sent.at[owner], dst_ref=got.at[slot], send_sem=a_send, recv_sem=a_recv.at[kind],
            device_id=device, device_id_type=MESH,
        )

    half_others(lambda x, j: meta_to(x, j).start())

    per = LANES // TILE_Y
    halfx = TILE_X // per
    tile_rows = tiles_x * fields
    def spread(c):
        for h in range(2):
            for g in range(halfx):
                parts = [
                    jnp.concatenate(
                        [
                            xs[c, h, pl.ds(t * TILE_X + g * per + a, fields, stride=rows), :]
                            for t in range(tiles_x)
                        ],
                        axis=0,
                    )
                    for a in range(per)
                ]
                parts = block_transpose(parts, TILE_Y)
                at = (c * halfx + g) * LANES
                for t in range(per):
                    j = h * per + t
                    xmat[j * tile_rows : (j + 1) * tile_rows, at : at + LANES] = parts[t].astype(jnp.bfloat16)

    spread(0)

    for c in flux_copies:
        c.wait()
    row_i = lax.broadcasted_iota(jnp.int32, (rows, LANES), 0)
    for f in range(fields):
        halves = [flux[f, :, h * LANES : (h + 1) * LANES] for h in range(2)]
        ends = (
            pltpu.roll(col_r[0], LANES - f, 1) if f else col_r[0],
            pltpu.roll(col_r[1], LANES - 1 - f, 1),
        )
        to_right = [pltpu.roll(x, 1, 1) for x in halves]
        to_left = [pltpu.roll(x, LANES - 1, 1) for x in halves]
        at_first, at_last = lane_c == 0, lane_c == LANES - 1
        before_y = [jnp.where(at_first, ends[0], to_right[0]), jnp.where(at_first, to_right[0], to_right[1])]
        after_y = [jnp.where(at_last, to_left[1], to_left[0]), jnp.where(at_last, ends[1], to_left[1])]
        for h in range(2):
            x = halves[h]
            above = jnp.where(row_i == 0, row_r[0, h, f : f + 1, :], pltpu.roll(x, 1, 0))
            below = jnp.where(row_i == rows - 1, row_r[1, h, f : f + 1, :], pltpu.roll(x, rows - 1, 0))
            xs[1, h, f * rows : (f + 1) * rows, :] = (below - above) * 0.5
            xs[2, h, f * rows : (f + 1) * rows, :] = (after_y[h] - before_y[h]) * 0.5

    spread(1)
    spread(2)
    for c in bank_copies:
        c.wait()

    def products(p, c):
        got_pair = jnp.dot(xmat[...], bank_v[p], preferred_element_type=jnp.float32)
        prod[pl.ds(2 * p * tiles, tiles)] = got_pair[:, :LANES].reshape(tiles, fields, LANES)
        prod[pl.ds((2 * p + 1) * tiles, tiles)] = got_pair[:, LANES:].reshape(tiles, fields, LANES)
        return c

    lax.fori_loop(0, nwb // 2, products, 0)
    table_copy.wait()

    def record(d, s):
        return prod[jnp.clip(table_s[d, s], 0, nwb * tiles - 1)]

    def fill(d, ref, at):
        for s in range(0, cap, 2):
            pair = jnp.concatenate([record(d, s), record(d, s + 1)], axis=0)
            ref[at, s * fields : (s + 2) * fields, :] = pair.astype(jnp.bfloat16)

    for kind in range(2):

        def send_data(x, j):
            d = parties(kind, x, j)[0]
            fill(d, sent, d)
            data_to(kind, x, j).start()

        half_others(send_data)
        fill(gx * ny + (base if kind else other) + mine_j, got, kind * hn + place)

    diff_in.wait()
    diff_copies = halo_copies(
        4, diff, diff, diff.at[pl.ds(0, 8)], diff.at[pl.ds(orows - 8, 8)], d_edge, d_corner, d_row
    )
    for c in diff_copies:
        c.start()

    cells = fields * otx * oty
    shares = LANES // span
    depth = hn * span
    cell_i = lax.broadcasted_iota(jnp.int32, (cells, LANES), 0).astype(jnp.float32)
    part_lane = lane_of((1, LANES)) // span
    mine_half = gy // hy

    def whole(src_ref, dst_ref, send_sem, recv_sem):
        return pltpu.make_async_remote_copy(
            src_ref=src_ref, dst_ref=dst_ref, send_sem=send_sem, recv_sem=recv_sem,
            device_id=(gx, other + mine_j), device_id_type=MESH,
        )

    meta_all = whole(meta_s.at[pl.ds(0, hn - 1)], meta_r.at[pl.ds(0, hn - 1)], m_send, m_recv)
    meta_all.wait_recv()
    for kind in range(2):
        row = mine_half if kind else 1 - mine_half
        for b in range(depth // LANES):
            aims = meta_r[b * shares, row]
            for i in range(1, shares):
                aims = jnp.where(part_lane == i, meta_r[b * shares + i, row], aims)
            at = kind * depth + b * LANES
            hot[:, at : at + LANES] = jnp.where(cell_i == aims, 1.0, 0.0).astype(jnp.bfloat16)

    def collect(kind):
        ref = got.at[pl.ds(kind * hn, hn - 1)]
        whole(ref, ref, a_send, a_recv.at[kind]).wait_recv()
        data = got[kind * hn : (kind + 1) * hn].reshape(depth, LANES)
        return jnp.dot(hot[:, kind * depth : (kind + 1) * depth], data, preferred_element_type=jnp.float32)

    part_s[...] = collect(0).astype(jnp.bfloat16)
    cross = remote(part_s, part_r, 20, gx, other + mine_j)
    cross.start()
    total = collect(1)
    cross.wait()
    total = total + part_r[...].astype(jnp.float32)
    high = fields * otx
    parts = block_transpose([total[t * high : (t + 1) * high, :] for t in range(oty)], OTILE_Y)
    for a in range(OTILE_X):
        u[pl.ds(a, high, stride=OTILE_X), :] = parts[a]

    lane_o = lane_of((orows, LANES))
    for f in range(fields):
        pack_s[2, f * 8 : f * 8 + 8, :] = u[f * orows : f * orows + 8, :]
        pack_s[3, f * 8 : f * 8 + 8, :] = u[(f + 1) * orows - 8 : (f + 1) * orows, :]
    ocean_copies = halo_copies(
        12,
        pack_s.at[0, pl.ds(0, orows)],
        pack_s.at[1, pl.ds(0, orows)],
        pack_s.at[2, pl.ds(0, fields * 8)],
        pack_s.at[3, pl.ds(0, fields * 8)],
        u_edge, u_corner, u_row,
    )
    for c in ocean_copies[2:4]:
        c.start()
    packed = [jnp.zeros((orows, LANES), jnp.float32) for _ in range(2)]
    for f in range(fields):
        block = u[f * orows : (f + 1) * orows, :]
        shift = f * SWEEPS
        rolled = (pltpu.roll(block, shift, 1), pltpu.roll(block, LANES - shift, 1)) if f else (block, block)
        mine = (lane_o // SWEEPS == f, (LANES - 1 - lane_o) // SWEEPS == f)
        packed = [jnp.where(mine[e], rolled[e], packed[e]) for e in range(2)]
    pack_s[0, 0:orows, :] = packed[0]
    pack_s[1, 0:orows, :] = packed[1]
    for c in ocean_copies[4:] + ocean_copies[:2]:
        c.start()

    meta_all.wait_send()
    ref = sent.at[pl.ds(0, 2 * (hn - 1))]
    whole(ref, ref, a_send, a_recv.at[0]).wait_send()
    for c in diff_copies:
        c.wait()

    has = (gx > 0, gx < nx - 1, gy > 0, gy < ny - 1)
    tail_lane = lane_of((8, LANES)) < LANES // 2
    tail_row = lax.broadcasted_iota(jnp.int32, (8, LANES), 0) < 4
    wide_lane = lane_o < LANES // 2
    row_ok = jnp.where(tail_row, has[1].astype(jnp.float32), has[0].astype(jnp.float32))
    col_ok = jnp.where(wide_lane, has[3].astype(jnp.float32), has[2].astype(jnp.float32))
    both_ok = row_ok * col_ok[0:8]
    d_tail = jnp.where(tail_row, d_row[1], d_row[0]) * row_ok
    d_side = jnp.where(wide_lane, d_edge[1], d_edge[0]) * col_ok
    d_both = (
        jnp.where(
            tail_lane,
            jnp.where(tail_row, d_corner[1, 1], d_corner[0, 1]),
            jnp.where(tail_row, d_corner[1, 0], d_corner[0, 0]),
        )
        * both_ok
    )
    d = [
        jnp.concatenate([diff[...], d_tail], axis=0),
        jnp.concatenate([d_side, d_both], axis=0),
    ]
    for c in ocean_copies:
        c.wait()
    side = [
        jnp.concatenate([u_edge[e], jnp.where(tail_row, u_corner[1, e], u_corner[0, e])], axis=0)
        for e in range(2)
    ]
    ext = orows + 8
    lane_e = lane_of((ext, LANES))
    side_ok = jnp.concatenate([col_ok, both_ok], axis=0)
    at_first, at_last = lane_e == 0, lane_e == LANES - 1
    def opened(f):
        shift = f * SWEEPS
        tail = jnp.where(tail_row, u_row[1, f * 8 : f * 8 + 8, :], u_row[0, f * 8 : f * 8 + 8, :]) * row_ok
        rolled = (
            (pltpu.roll(side[1], LANES - shift, 1), pltpu.roll(side[0], shift, 1)) if f else (side[1], side[0])
        )
        return [
            jnp.concatenate([u[f * orows : (f + 1) * orows, :], tail], axis=0),
            jnp.where(lane_e < LANES // 2, rolled[0], rolled[1]) * side_ok,
        ]

    def swept(x):
        to_right = [pltpu.roll(v, 1, 1) for v in x]
        to_left = [pltpu.roll(v, LANES - 1, 1) for v in x]
        beside = [
            jnp.where(at_first, to_right[1 - h], to_right[h])
            + jnp.where(at_last, to_left[1 - h], to_left[h])
            + pltpu.roll(x[h], 1, 0)
            + pltpu.roll(x[h], ext - 1, 0)
            for h in range(2)
        ]
        return [x[h] + d[h] * (beside[h] - 4.0 * x[h]) for h in range(2)]

    for f in range(0, fields, 4):
        some = [opened(f + i) for i in range(4)]
        for sweep in range(SWEEPS):
            some = [swept(x) for x in some]
        for i, x in enumerate(some):
            out[f + i] = x[0][0:orows, :]


def local(nx, ny, flux, diffusivity, remap_bank, rec_owner, rec_source, rec_target, rec_weight):
    n = nx * ny
    fields, rows, cols = flux.shape
    orows, ocols = diffusivity.shape
    records = rec_owner.shape[0]
    cap = max(2, 2 * records // n)
    nwb = remap_bank.shape[0]
    depth = 3 * TILE_X * TILE_Y
    tiles = rows // TILE_X * (cols // TILE_Y)
    span = cap * fields
    f32, bf16 = jnp.float32, jnp.bfloat16
    v = pltpu.VMEM
    dma = pltpu.SemaphoreType.DMA
    vm = pl.BlockSpec(memory_space=pltpu.VMEM)
    flat = [x.reshape(1, records) for x in (rec_owner, rec_source, rec_target, rec_weight)]
    return pl.pallas_call(
        functools.partial(kernel, nx, ny, cap),
        out_shape=jax.ShapeDtypeStruct((fields, orows, ocols), f32),
        in_specs=[pl.BlockSpec(memory_space=pl.ANY)] * 7,
        out_specs=vm,
        scratch_shapes=[
            v((fields, rows, cols), f32),
            v((orows, ocols), f32),
            v((4, 1, records), jnp.int32),
            dma((9,)),
            v((nwb // 2, depth, 2 * LANES), bf16),
            v((3, 2, (fields + 1) * rows, LANES), f32),
            v((tiles * fields, depth), bf16),
            v((nwb * tiles, fields, LANES), f32),
            v((n, LANES), jnp.int32),
            pltpu.SMEM((n, LANES), jnp.int32),
            v((n // 2, 2, 1, LANES), f32),
            v((n // 2, 2, 1, LANES), f32),
            v((n, span, LANES), bf16),
            v((n, span, LANES), bf16),
            v((2, 2, fields, LANES), f32),
            v((2, 2, fields, LANES), f32),
            v((2, rows, LANES), f32),
            v((2, rows, LANES), f32),
            v((2, orows, LANES), f32),
            v((2, 2, 8, LANES), f32),
            v((2, 8, LANES), f32),
            v((fields * orows + OTILE_X, LANES), f32),
            v((4, max(orows, fields * 8), LANES), f32),
            v((2, orows, LANES), f32),
            v((2, 2, 8, LANES), f32),
            v((2, fields * 8, LANES), f32),
            v((fields * orows * ocols // LANES, LANES), bf16),
            v((fields * orows * ocols // LANES, LANES), bf16),
            v((fields * orows * ocols // LANES, n * span), bf16),
            dma((2,)), dma,
            dma, dma((2,)), dma, dma,
            dma((21,)), dma((21,)),
        ],
        compiler_params=pltpu.CompilerParams(
            collective_id=0, has_side_effects=True, vmem_limit_bytes=64 * 1024 * 1024 - 128 * 1024
        ),
    )(flux, diffusivity, remap_bank.reshape(nwb // 2, 2, depth, LANES), *flat)


def solution(mesh):
    in_specs = (
        P(None, "gx", "gy"),
        P("gx", "gy"),
        P(),
        P(("gx", "gy")),
        P(("gx", "gy")),
        P(("gx", "gy")),
        P(("gx", "gy")),
    )
    out_specs = P(None, "gx", "gy")
    body = functools.partial(local, mesh.shape["gx"], mesh.shape["gy"])
    return jax.shard_map(body, mesh=mesh, in_specs=in_specs, out_specs=out_specs, check_vma=False)
```

```python
import functools

import jax
import jax.numpy as jnp
from jax import lax
from jax.experimental import pallas as pl
from jax.experimental.pallas import tpu as pltpu
from jax.sharding import PartitionSpec as P

TILE_X = 16
TILE_Y = 16
OTILE_X = 8
OTILE_Y = 16
SWEEPS = 4
LANES = 128
MESH = pl.DeviceIdType.MESH


def lane_of(shape):
    return lax.broadcasted_iota(jnp.int32, shape, len(shape) - 1)


def block_transpose(parts, width):
    parts = list(parts)
    block = lane_of(parts[0].shape) // width
    step = 1
    while step < len(parts):
        keep = (block & step) == 0
        for i in range(len(parts)):
            if i & step == 0:
                j = i | step
                low, high = parts[i], parts[j]
                parts[i] = jnp.where(keep, low, pltpu.roll(high, step * width, 1))
                parts[j] = jnp.where(keep, pltpu.roll(low, LANES - step * width, 1), high)
        step *= 2
    return parts


def kernel(
    nx, ny, cap,
    flux_h, diff_h, bank, own_h, src_h, tgt_h, wgt_h,
    out,
    flux, diff, recs, in_sem,
    bank_v, xs, xmat, prod, table_v, table_s, meta_s, meta_r, sent, got,
    row_s, row_r, col_s, col_r, d_edge, d_corner, d_row, u, pack_s, u_edge, u_corner, u_row, part_s, part_r, hot,
    bank_sem, table_sem, a_send, a_recv, m_send, m_recv, h_send, h_recv,
):
    n = nx * ny
    fields, rows, cols = flux.shape
    nwb = 2 * bank.shape[0]
    tiles_x, tiles_y = rows // TILE_X, cols // TILE_Y
    tiles = tiles_x * tiles_y
    orows = diff.shape[0]
    oty = diff.shape[1] // OTILE_Y
    otx = orows // OTILE_X
    span = cap * fields
    gx, gy = lax.axis_index("gx"), lax.axis_index("gy")
    me = gx * ny + gy
    up, down = lax.rem(gx + nx - 1, nx), lax.rem(gx + 1, nx)
    left, right = lax.rem(gy + ny - 1, ny), lax.rem(gy + 1, ny)

    barrier = pltpu.get_barrier_semaphore()

    hy = ny // 2
    hn = n // 2
    base = gy // hy * hy
    other = hy - base
    mine_j = gy - base
    place = gx * hy + mine_j
    j_order = [o for k in range(hy // 2 + 1) for o in sorted({hy // 2 - k, hy // 2 + k}) if o < hy]
    j_at = [mine_j if o == 0 else lax.rem(mine_j + o, hy) for o in j_order]

    def half_others(act):
        def one_row(i, c):
            x = lax.rem(gx + i, nx)
            for k, j in zip(j_order, j_at):
                if k:
                    act(x, j)
                else:
                    pl.when(i != 0)(functools.partial(act, x, j))
            return c

        lax.fori_loop(0, nx, one_row, 0)

    pitch = rows + 8
    quarter = fields // 4
    flux_ins = [
        pltpu.make_async_copy(flux_h.at[pl.ds(i * quarter, quarter)], flux.at[pl.ds(i * quarter, quarter)], in_sem.at[5 + i])
        for i in range(4)
    ]
    ins = [
        pltpu.make_async_copy(r, recs.at[i], in_sem.at[i]) for i, r in enumerate((own_h, src_h, tgt_h, wgt_h))
    ]
    diff_in = pltpu.make_async_copy(diff_h, diff, in_sem.at[4])
    for c in flux_ins + ins + [diff_in]:
        c.start()
    bank_copies = [
        pltpu.make_async_copy(bank.at[:, i], bank_v.at[:, :, pl.ds(i * LANES, LANES)], bank_sem.at[i]) for i in range(2)
    ]

    def greet(x, y):
        pl.semaphore_signal(barrier, inc=1, device_id=(x, y), device_id_type=MESH)

    greet(gx, other + mine_j)
    for y, edge in ((left, 0), (right, hy - 1)):

        @pl.when(mine_j == edge)
        def _():
            for x in (up, gx, down):
                greet(x, y)

    half_others(lambda x, j: greet(x, base + j))
    beside_others = 3 * (mine_j == 0).astype(jnp.int32) + 3 * (mine_j == hy - 1).astype(jnp.int32)

    for c in flux_ins:
        c.wait()
    for c in bank_copies:
        c.start()
    for f in range(fields):
        for h in range(2):
            xs[0, h, f * pitch : f * pitch + rows, :] = flux[f, :, h * LANES : (h + 1) * LANES]
    lane_c = lane_of((rows, LANES))
    first = jnp.zeros((rows, LANES), jnp.float32)
    last = jnp.zeros((rows, LANES), jnp.float32)
    for f in range(fields):
        a = flux[f, :, 0:LANES]
        b = flux[f, :, cols - LANES : cols]
        first = jnp.where(lane_c == f, pltpu.roll(a, f, 1) if f else a, first)
        last = jnp.where(lane_c == f, pltpu.roll(b, f + 1, 1), last)
    col_s[0] = first
    col_s[1] = last
    for h in range(2):
        row_s[0, h] = xs[0, h, pl.ds(0, fields, stride=pitch), :]
        row_s[1, h] = xs[0, h, pl.ds(rows - 1, fields, stride=pitch), :]

    pl.semaphore_wait(barrier, hn + beside_others)

    def remote(a, b, k, x, y):
        return pltpu.make_async_remote_copy(
            src_ref=a, dst_ref=b, send_sem=h_send.at[k], recv_sem=h_recv.at[k],
            device_id=(x, y), device_id_type=MESH,
        )

    flux_copies = [
        remote(row_s.at[0], row_r.at[1], 0, up, gy),
        remote(row_s.at[1], row_r.at[0], 1, down, gy),
        remote(col_s.at[0], col_r.at[1], 2, gx, left),
        remote(col_s.at[1], col_r.at[0], 3, gx, right),
    ]
    for c in flux_copies:
        c.start()

    def halo_copies(base, edge0, edge1, row0, row1, edge, corner, row):
        low = pl.ds(0, 8)
        high = pl.ds(orows - 8, 8)
        return [
            remote(edge0, edge.at[1], base, gx, left),
            remote(edge1, edge.at[0], base + 1, gx, right),
            remote(row0, row.at[1], base + 2, up, gy),
            remote(row1, row.at[0], base + 3, down, gy),
            remote(edge0.at[low], corner.at[1, 1], base + 4, up, left),
            remote(edge0.at[high], corner.at[0, 1], base + 5, down, left),
            remote(edge1.at[low], corner.at[1, 0], base + 6, up, right),
            remote(edge1.at[high], corner.at[0, 0], base + 7, down, right),
        ]

    for c in ins:
        c.wait()
    records = recs.shape[2]
    owner_i = lax.broadcasted_iota(jnp.int32, (n, records), 0)
    member = recs[0] == owner_i
    lower = lax.broadcasted_iota(jnp.int32, (records, records), 0) < lane_of((records, records))
    before = jnp.dot(
        member.astype(jnp.bfloat16), lower.astype(jnp.bfloat16), preferred_element_type=jnp.float32
    )
    source, target = recs[1], recs[2]
    code = (recs[3] * tiles + lax.rem(source, tiles_y) * tiles_x + source // tiles_y).astype(jnp.float32)
    aim = (lax.rem(target, oty) * (fields * otx) + target // oty).astype(jnp.float32)
    lane = lane_of((n, LANES))
    slot_lane = lax.rem(lane, span) // fields
    field_lane = (lax.rem(lane, fields) * otx).astype(jnp.float32)
    table = jnp.zeros((n, LANES), jnp.float32)
    meta = jnp.full((n, LANES), -1.0, jnp.float32)
    for k in range(cap):
        hit = jnp.logical_and(member, before == k)
        code_k = jnp.sum(jnp.where(hit, code, 0.0), axis=1, keepdims=True)
        aim_k = jnp.sum(jnp.where(hit, aim + 1.0, 0.0), axis=1, keepdims=True) - 1.0
        table = jnp.where(lane == k, code_k, table)
        filled = jnp.where(aim_k >= 0.0, aim_k + field_lane, -1.0)
        meta = jnp.where(slot_lane == k, filled, meta)
    table_v[...] = table.astype(jnp.int32)
    table_copy = pltpu.make_async_copy(table_v, table_s, table_sem)
    table_copy.start()
    for o in range(n):
        meta_s[o // ny * hy + o % hy, o % ny // hy] = meta[o : o + 1, :]
    meta_r[place] = meta_s[place]

    def parties(kind, x, j):
        owner = x * ny + (base if kind else other) + j
        return owner, kind * hn + place, (x, base + j)

    def meta_to(x, j):
        return pltpu.make_async_remote_copy(
            src_ref=meta_s.at[x * hy + j], dst_ref=meta_r.at[place], send_sem=m_send, recv_sem=m_recv,
            device_id=(x, base + j), device_id_type=MESH,
        )

    def data_to(kind, x, j):
        owner, slot, device = parties(kind, x, j)
        return pltpu.make_async_remote_copy(
            src_ref=sent.at[owner], dst_ref=got.at[slot], send_sem=a_send, recv_sem=a_recv.at[kind],
            device_id=device, device_id_type=MESH,
        )

    half_others(lambda x, j: meta_to(x, j).start())

    per = LANES // TILE_Y
    halfx = TILE_X // per
    tile_rows = tiles_x * fields
    def spread(c):
        for h in range(2):
            for g in range(halfx):
                parts = [
                    jnp.concatenate(
                        [
                            xs[c, h, pl.ds(t * TILE_X + g * per + a, fields, stride=pitch), :]
                            for t in range(tiles_x)
                        ],
                        axis=0,
                    )
                    for a in range(per)
                ]
                parts = block_transpose(parts, TILE_Y)
                at = (c * halfx + g) * LANES
                for t in range(per):
                    j = h * per + t
                    xmat[j * tile_rows : (j + 1) * tile_rows, at : at + LANES] = parts[t].astype(jnp.bfloat16)

    spread(0)

    for c in flux_copies:
        c.wait()
    row_i = lax.broadcasted_iota(jnp.int32, (rows, LANES), 0)
    for f in range(fields):
        halves = [flux[f, :, h * LANES : (h + 1) * LANES] for h in range(2)]
        ends = (
            pltpu.roll(col_r[0], LANES - f, 1) if f else col_r[0],
            pltpu.roll(col_r[1], LANES - 1 - f, 1),
        )
        to_right = [pltpu.roll(x, 1, 1) for x in halves]
        to_left = [pltpu.roll(x, LANES - 1, 1) for x in halves]
        at_first, at_last = lane_c == 0, lane_c == LANES - 1
        before_y = [jnp.where(at_first, ends[0], to_right[0]), jnp.where(at_first, to_right[0], to_right[1])]
        after_y = [jnp.where(at_last, to_left[1], to_left[0]), jnp.where(at_last, ends[1], to_left[1])]
        for h in range(2):
            x = halves[h]
            above = jnp.where(row_i == 0, row_r[0, h, f : f + 1, :], pltpu.roll(x, 1, 0))
            below = jnp.where(row_i == rows - 1, row_r[1, h, f : f + 1, :], pltpu.roll(x, rows - 1, 0))
            xs[1, h, f * pitch : f * pitch + rows, :] = (below - above) * 0.5
            xs[2, h, f * pitch : f * pitch + rows, :] = (after_y[h] - before_y[h]) * 0.5

    spread(1)
    spread(2)
    for c in bank_copies:
        c.wait()

    def products(p, c):
        got_pair = jnp.dot(xmat[...], bank_v[p], preferred_element_type=jnp.float32)
        prod[pl.ds(2 * p * tiles, tiles)] = got_pair[:, :LANES].reshape(tiles, fields, LANES)
        prod[pl.ds((2 * p + 1) * tiles, tiles)] = got_pair[:, LANES:].reshape(tiles, fields, LANES)
        return c

    lax.fori_loop(0, nwb // 2, products, 0)
    table_copy.wait()

    def record(d, s):
        return prod[jnp.clip(table_s[d, s], 0, nwb * tiles - 1)]

    def fill(d, ref, at):
        for s in range(0, cap, 2):
            pair = jnp.concatenate([record(d, s), record(d, s + 1)], axis=0)
            ref[at, s * fields : (s + 2) * fields, :] = pair.astype(jnp.bfloat16)

    for kind in range(2):

        def send_data(x, j):
            d = parties(kind, x, j)[0]
            fill(d, sent, d)
            data_to(kind, x, j).start()

        half_others(send_data)
        fill(gx * ny + (base if kind else other) + mine_j, got, kind * hn + place)

    diff_in.wait()
    diff_copies = halo_copies(
        4, diff, diff, diff.at[pl.ds(0, 8)], diff.at[pl.ds(orows - 8, 8)], d_edge, d_corner, d_row
    )
    for c in diff_copies:
        c.start()

    cells = fields * otx * oty
    shares = LANES // span
    depth = hn * span
    cell_i = lax.broadcasted_iota(jnp.int32, (cells, LANES), 0).astype(jnp.float32)
    part_lane = lane_of((1, LANES)) // span
    mine_half = gy // hy

    def whole(src_ref, dst_ref, send_sem, recv_sem):
        return pltpu.make_async_remote_copy(
            src_ref=src_ref, dst_ref=dst_ref, send_sem=send_sem, recv_sem=recv_sem,
            device_id=(gx, other + mine_j), device_id_type=MESH,
        )

    meta_all = whole(meta_s.at[pl.ds(0, hn - 1)], meta_r.at[pl.ds(0, hn - 1)], m_send, m_recv)
    meta_all.wait_recv()
    for kind in range(2):
        row = mine_half if kind else 1 - mine_half
        for b in range(depth // LANES):
            aims = meta_r[b * shares, row]
            for i in range(1, shares):
                aims = jnp.where(part_lane == i, meta_r[b * shares + i, row], aims)
            at = kind * depth + b * LANES
            hot[:, at : at + LANES] = jnp.where(cell_i == aims, 1.0, 0.0).astype(jnp.bfloat16)

    def collect(kind):
        ref = got.at[pl.ds(kind * hn, hn - 1)]
        whole(ref, ref, a_send, a_recv.at[kind]).wait_recv()
        data = got[kind * hn : (kind + 1) * hn].reshape(depth, LANES)
        return jnp.dot(hot[:, kind * depth : (kind + 1) * depth], data, preferred_element_type=jnp.float32)

    part_s[...] = collect(0).astype(jnp.bfloat16)
    cross = remote(part_s, part_r, 20, gx, other + mine_j)
    cross.start()
    total = collect(1)
    cross.wait()
    total = total + part_r[...].astype(jnp.float32)
    high = fields * otx
    parts = block_transpose([total[t * high : (t + 1) * high, :] for t in range(oty)], OTILE_Y)
    for a in range(OTILE_X):
        u[pl.ds(a, high, stride=OTILE_X), :] = parts[a]

    lane_o = lane_of((orows, LANES))
    for f in range(fields):
        pack_s[2, f * 8 : f * 8 + 8, :] = u[f * orows : f * orows + 8, :]
        pack_s[3, f * 8 : f * 8 + 8, :] = u[(f + 1) * orows - 8 : (f + 1) * orows, :]
    ocean_copies = halo_copies(
        12,
        pack_s.at[0, pl.ds(0, orows)],
        pack_s.at[1, pl.ds(0, orows)],
        pack_s.at[2, pl.ds(0, fields * 8)],
        pack_s.at[3, pl.ds(0, fields * 8)],
        u_edge, u_corner, u_row,
    )
    for c in ocean_copies[2:4]:
        c.start()
    packed = [jnp.zeros((orows, LANES), jnp.float32) for _ in range(2)]
    for f in range(fields):
        block = u[f * orows : (f + 1) * orows, :]
        shift = f * SWEEPS
        rolled = (pltpu.roll(block, shift, 1), pltpu.roll(block, LANES - shift, 1)) if f else (block, block)
        mine = (lane_o // SWEEPS == f, (LANES - 1 - lane_o) // SWEEPS == f)
        packed = [jnp.where(mine[e], rolled[e], packed[e]) for e in range(2)]
    pack_s[0, 0:orows, :] = packed[0]
    pack_s[1, 0:orows, :] = packed[1]
    for c in ocean_copies[4:] + ocean_copies[:2]:
        c.start()

    meta_all.wait_send()
    ref = sent.at[pl.ds(0, 2 * (hn - 1))]
    whole(ref, ref, a_send, a_recv.at[0]).wait_send()
    for c in diff_copies:
        c.wait()

    has = (gx > 0, gx < nx - 1, gy > 0, gy < ny - 1)
    tail_lane = lane_of((8, LANES)) < LANES // 2
    tail_row = lax.broadcasted_iota(jnp.int32, (8, LANES), 0) < 4
    wide_lane = lane_o < LANES // 2
    row_ok = jnp.where(tail_row, has[1].astype(jnp.float32), has[0].astype(jnp.float32))
    col_ok = jnp.where(wide_lane, has[3].astype(jnp.float32), has[2].astype(jnp.float32))
    both_ok = row_ok * col_ok[0:8]
    d_tail = jnp.where(tail_row, d_row[1], d_row[0]) * row_ok
    d_side = jnp.where(wide_lane, d_edge[1], d_edge[0]) * col_ok
    d_both = (
        jnp.where(
            tail_lane,
            jnp.where(tail_row, d_corner[1, 1], d_corner[0, 1]),
            jnp.where(tail_row, d_corner[1, 0], d_corner[0, 0]),
        )
        * both_ok
    )
    d = [
        jnp.concatenate([diff[...], d_tail], axis=0),
        jnp.concatenate([d_side, d_both], axis=0),
    ]
    for c in ocean_copies:
        c.wait()
    side = [
        jnp.concatenate([u_edge[e], jnp.where(tail_row, u_corner[1, e], u_corner[0, e])], axis=0)
        for e in range(2)
    ]
    ext = orows + 8
    lane_e = lane_of((ext, LANES))
    side_ok = jnp.concatenate([col_ok, both_ok], axis=0)
    at_first, at_last = lane_e == 0, lane_e == LANES - 1
    def opened(f):
        shift = f * SWEEPS
        tail = jnp.where(tail_row, u_row[1, f * 8 : f * 8 + 8, :], u_row[0, f * 8 : f * 8 + 8, :]) * row_ok
        rolled = (
            (pltpu.roll(side[1], LANES - shift, 1), pltpu.roll(side[0], shift, 1)) if f else (side[1], side[0])
        )
        return [
            jnp.concatenate([u[f * orows : (f + 1) * orows, :], tail], axis=0),
            jnp.where(lane_e < LANES // 2, rolled[0], rolled[1]) * side_ok,
        ]

    def swept(x):
        to_right = [pltpu.roll(v, 1, 1) for v in x]
        to_left = [pltpu.roll(v, LANES - 1, 1) for v in x]
        beside = [
            jnp.where(at_first, to_right[1 - h], to_right[h])
            + jnp.where(at_last, to_left[1 - h], to_left[h])
            + pltpu.roll(x[h], 1, 0)
            + pltpu.roll(x[h], ext - 1, 0)
            for h in range(2)
        ]
        return [x[h] + d[h] * (beside[h] - 4.0 * x[h]) for h in range(2)]

    for f in range(0, fields, 4):
        some = [opened(f + i) for i in range(4)]
        for sweep in range(SWEEPS):
            some = [swept(x) for x in some]
        for i, x in enumerate(some):
            out[f + i] = x[0][0:orows, :]


def local(nx, ny, flux, diffusivity, remap_bank, rec_owner, rec_source, rec_target, rec_weight):
    n = nx * ny
    fields, rows, cols = flux.shape
    orows, ocols = diffusivity.shape
    records = rec_owner.shape[0]
    cap = max(2, 2 * records // n)
    nwb = remap_bank.shape[0]
    depth = 3 * TILE_X * TILE_Y
    tiles = rows // TILE_X * (cols // TILE_Y)
    span = cap * fields
    f32, bf16 = jnp.float32, jnp.bfloat16
    v = pltpu.VMEM
    dma = pltpu.SemaphoreType.DMA
    vm = pl.BlockSpec(memory_space=pltpu.VMEM)
    flat = [x.reshape(1, records) for x in (rec_owner, rec_source, rec_target, rec_weight)]
    return pl.pallas_call(
        functools.partial(kernel, nx, ny, cap),
        out_shape=jax.ShapeDtypeStruct((fields, orows, ocols), f32),
        in_specs=[pl.BlockSpec(memory_space=pl.ANY)] * 7,
        out_specs=vm,
        scratch_shapes=[
            v((fields, rows, cols), f32),
            v((orows, ocols), f32),
            v((4, 1, records), jnp.int32),
            dma((9,)),
            v((nwb // 2, depth, 2 * LANES), bf16),
            v((3, 2, (fields + 1) * (rows + 8), LANES), f32),
            v((tiles * fields, depth), bf16),
            v((nwb * tiles, fields, LANES), f32),
            v((n, LANES), jnp.int32),
            pltpu.SMEM((n, LANES), jnp.int32),
            v((n // 2, 2, 1, LANES), f32),
            v((n // 2, 2, 1, LANES), f32),
            v((n, span, LANES), bf16),
            v((n, span, LANES), bf16),
            v((2, 2, fields, LANES), f32),
            v((2, 2, fields, LANES), f32),
            v((2, rows, LANES), f32),
            v((2, rows, LANES), f32),
            v((2, orows, LANES), f32),
            v((2, 2, 8, LANES), f32),
            v((2, 8, LANES), f32),
            v((fields * orows + OTILE_X, LANES), f32),
            v((4, max(orows, fields * 8), LANES), f32),
            v((2, orows, LANES), f32),
            v((2, 2, 8, LANES), f32),
            v((2, fields * 8, LANES), f32),
            v((fields * orows * ocols // LANES, LANES), bf16),
            v((fields * orows * ocols // LANES, LANES), bf16),
            v((fields * orows * ocols // LANES, n * span), bf16),
            dma((2,)), dma,
            dma, dma((2,)), dma, dma,
            dma((21,)), dma((21,)),
        ],
        compiler_params=pltpu.CompilerParams(
            collective_id=0, has_side_effects=True, vmem_limit_bytes=64 * 1024 * 1024 - 128 * 1024
        ),
    )(flux, diffusivity, remap_bank.reshape(nwb // 2, 2, depth, LANES), *flat)


def solution(mesh):
    in_specs = (
        P(None, "gx", "gy"),
        P("gx", "gy"),
        P(),
        P(("gx", "gy")),
        P(("gx", "gy")),
        P(("gx", "gy")),
        P(("gx", "gy")),
    )
    out_specs = P(None, "gx", "gy")
    body = functools.partial(local, mesh.shape["gx"], mesh.shape["gy"])
    return jax.shard_map(body, mesh=mesh, in_specs=in_specs, out_specs=out_specs, check_vma=False)
```

```python
import functools

import jax
import jax.numpy as jnp
from jax import lax
from jax.experimental import pallas as pl
from jax.experimental.pallas import tpu as pltpu
from jax.sharding import PartitionSpec as P

TILE_X = 16
TILE_Y = 16
OTILE_X = 8
OTILE_Y = 16
SWEEPS = 4
LANES = 128
MESH = pl.DeviceIdType.MESH


def lane_of(shape):
    return lax.broadcasted_iota(jnp.int32, shape, len(shape) - 1)


def block_transpose(parts, width):
    parts = list(parts)
    block = lane_of(parts[0].shape) // width
    step = 1
    while step < len(parts):
        keep = (block & step) == 0
        for i in range(len(parts)):
            if i & step == 0:
                j = i | step
                low, high = parts[i], parts[j]
                parts[i] = jnp.where(keep, low, pltpu.roll(high, step * width, 1))
                parts[j] = jnp.where(keep, pltpu.roll(low, LANES - step * width, 1), high)
        step *= 2
    return parts


def kernel(
    nx, ny, cap,
    flux_h, diff_h, bank, own_h, src_h, tgt_h, wgt_h,
    out,
    flux, diff, recs, in_sem,
    bank_v, xs, xmat, prod, table_v, table_s, meta_s, meta_r, sent, got,
    row_s, row_r, col_s, col_r, d_edge, d_corner, d_row, u, pack_s, u_edge, u_corner, u_row, part_s, part_r, hot,
    bank_sem, table_sem, a_send, a_recv, m_send, m_recv, h_send, h_recv,
):
    n = nx * ny
    fields, rows, cols = flux.shape
    nwb = 2 * bank.shape[0]
    tiles_x, tiles_y = rows // TILE_X, cols // TILE_Y
    tiles = tiles_x * tiles_y
    orows = diff.shape[0]
    oty = diff.shape[1] // OTILE_Y
    otx = orows // OTILE_X
    span = cap * fields
    gx, gy = lax.axis_index("gx"), lax.axis_index("gy")
    me = gx * ny + gy
    up, down = lax.rem(gx + nx - 1, nx), lax.rem(gx + 1, nx)
    left, right = lax.rem(gy + ny - 1, ny), lax.rem(gy + 1, ny)

    barrier = pltpu.get_barrier_semaphore()

    hy = ny // 2
    hn = n // 2
    base = gy // hy * hy
    other = hy - base
    mine_j = gy - base
    place = gx * hy + mine_j
    j_order = [o for k in range(hy // 2 + 1) for o in sorted({hy // 2 - k, hy // 2 + k}) if o < hy]
    j_at = [mine_j if o == 0 else lax.rem(mine_j + o, hy) for o in j_order]

    def half_others(act):
        def one_row(i, c):
            x = lax.rem(gx + i, nx)
            for k, j in zip(j_order, j_at):
                if k:
                    act(x, j)
                else:
                    pl.when(i != 0)(functools.partial(act, x, j))
            return c

        lax.fori_loop(0, nx, one_row, 0)

    pitch = rows + 8
    quarter = fields // 4
    flux_ins = [
        pltpu.make_async_copy(flux_h.at[pl.ds(i * quarter, quarter)], flux.at[pl.ds(i * quarter, quarter)], in_sem.at[5 + i])
        for i in range(4)
    ]
    ins = [
        pltpu.make_async_copy(r, recs.at[i], in_sem.at[i]) for i, r in enumerate((own_h, src_h, tgt_h, wgt_h))
    ]
    diff_in = pltpu.make_async_copy(diff_h, diff, in_sem.at[4])
    for c in flux_ins + ins + [diff_in]:
        c.start()
    bank_copies = [
        pltpu.make_async_copy(bank.at[:, i], bank_v.at[:, :, pl.ds(i * LANES, LANES)], bank_sem.at[i]) for i in range(2)
    ]

    def greet(x, y):
        pl.semaphore_signal(barrier, inc=1, device_id=(x, y), device_id_type=MESH)

    greet(gx, other + mine_j)
    for y, edge in ((left, 0), (right, hy - 1)):

        @pl.when(mine_j == edge)
        def _():
            for x in (up, gx, down):
                greet(x, y)

    half_others(lambda x, j: greet(x, base + j))
    beside_others = 3 * (mine_j == 0).astype(jnp.int32) + 3 * (mine_j == hy - 1).astype(jnp.int32)

    for c in flux_ins:
        c.wait()
    for c in bank_copies:
        c.start()
    for f in range(fields):
        for h in range(2):
            xs[0, h, f * pitch : f * pitch + rows, :] = flux[f, :, h * LANES : (h + 1) * LANES]
    lane_c = lane_of((rows, LANES))
    first = jnp.zeros((rows, LANES), jnp.float32)
    last = jnp.zeros((rows, LANES), jnp.float32)
    for f in range(fields):
        a = flux[f, :, 0:LANES]
        b = flux[f, :, cols - LANES : cols]
        first = jnp.where(lane_c == f, pltpu.roll(a, f, 1) if f else a, first)
        last = jnp.where(lane_c == f, pltpu.roll(b, f + 1, 1), last)
    col_s[0] = first
    col_s[1] = last
    for h in range(2):
        row_s[0, h] = xs[0, h, pl.ds(0, fields, stride=pitch), :]
        row_s[1, h] = xs[0, h, pl.ds(rows - 1, fields, stride=pitch), :]

    pl.semaphore_wait(barrier, hn + beside_others)

    def remote(a, b, k, x, y):
        return pltpu.make_async_remote_copy(
            src_ref=a, dst_ref=b, send_sem=h_send.at[k], recv_sem=h_recv.at[k],
            device_id=(x, y), device_id_type=MESH,
        )

    flux_copies = [
        remote(row_s.at[0], row_r.at[1], 0, up, gy),
        remote(row_s.at[1], row_r.at[0], 1, down, gy),
        remote(col_s.at[0], col_r.at[1], 2, gx, left),
        remote(col_s.at[1], col_r.at[0], 3, gx, right),
    ]
    for c in flux_copies:
        c.start()

    def halo_copies(base, edge0, edge1, row0, row1, edge, corner, row):
        low = pl.ds(0, 8)
        high = pl.ds(orows - 8, 8)
        return [
            remote(edge0, edge.at[1], base, gx, left),
            remote(edge1, edge.at[0], base + 1, gx, right),
            remote(row0, row.at[1], base + 2, up, gy),
            remote(row1, row.at[0], base + 3, down, gy),
            remote(edge0.at[low], corner.at[1, 1], base + 4, up, left),
            remote(edge0.at[high], corner.at[0, 1], base + 5, down, left),
            remote(edge1.at[low], corner.at[1, 0], base + 6, up, right),
            remote(edge1.at[high], corner.at[0, 0], base + 7, down, right),
        ]

    for c in ins:
        c.wait()
    records = recs.shape[2]
    owner_i = lax.broadcasted_iota(jnp.int32, (n, records), 0)
    member = recs[0] == owner_i
    lower = lax.broadcasted_iota(jnp.int32, (records, records), 0) < lane_of((records, records))
    before = jnp.dot(
        member.astype(jnp.bfloat16), lower.astype(jnp.bfloat16), preferred_element_type=jnp.float32
    )
    source, target = recs[1], recs[2]
    code = (recs[3] * tiles + lax.rem(source, tiles_y) * tiles_x + source // tiles_y).astype(jnp.float32)
    aim = (lax.rem(target, oty) * (fields * otx) + target // oty).astype(jnp.float32)
    lane = lane_of((n, LANES))
    slot_lane = lax.rem(lane, span) // fields
    field_lane = (lax.rem(lane, fields) * otx).astype(jnp.float32)
    table = jnp.zeros((n, LANES), jnp.float32)
    meta = jnp.full((n, LANES), -1.0, jnp.float32)
    for k in range(cap):
        hit = jnp.logical_and(member, before == k)
        code_k = jnp.sum(jnp.where(hit, code, 0.0), axis=1, keepdims=True)
        aim_k = jnp.sum(jnp.where(hit, aim + 1.0, 0.0), axis=1, keepdims=True) - 1.0
        table = jnp.where(lane == k, code_k, table)
        filled = jnp.where(aim_k >= 0.0, aim_k + field_lane, -1.0)
        meta = jnp.where(slot_lane == k, filled, meta)
    table_v[...] = table.astype(jnp.int32)
    table_copy = pltpu.make_async_copy(table_v, table_s, table_sem)
    table_copy.start()
    for o in range(n):
        meta_s[o // ny * hy + o % hy, o % ny // hy] = meta[o : o + 1, :]
    meta_r[place] = meta_s[place]

    def parties(kind, x, j):
        owner = x * ny + (base if kind else other) + j
        return owner, kind * hn + place, (x, base + j)

    def meta_to(x, j):
        return pltpu.make_async_remote_copy(
            src_ref=meta_s.at[x * hy + j], dst_ref=meta_r.at[place], send_sem=m_send, recv_sem=m_recv,
            device_id=(x, base + j), device_id_type=MESH,
        )

    def data_to(kind, x, j):
        owner, slot, device = parties(kind, x, j)
        return pltpu.make_async_remote_copy(
            src_ref=sent.at[owner], dst_ref=got.at[slot], send_sem=a_send, recv_sem=a_recv.at[kind],
            device_id=device, device_id_type=MESH,
        )

    half_others(lambda x, j: meta_to(x, j).start())

    per = LANES // TILE_Y
    halfx = TILE_X // per
    tile_rows = tiles_x * fields
    def spread(c):
        for h in range(2):
            for g in range(halfx):
                parts = [
                    jnp.concatenate(
                        [
                            xs[c, h, pl.ds(t * TILE_X + g * per + a, fields, stride=pitch), :]
                            for t in range(tiles_x)
                        ],
                        axis=0,
                    )
                    for a in range(per)
                ]
                parts = block_transpose(parts, TILE_Y)
                at = (c * halfx + g) * LANES
                for t in range(per):
                    j = h * per + t
                    xmat[j * tile_rows : (j + 1) * tile_rows, at : at + LANES] = parts[t].astype(jnp.bfloat16)

    spread(0)

    for c in flux_copies:
        c.wait()
    row_i = lax.broadcasted_iota(jnp.int32, (rows, LANES), 0)
    for f in range(fields):
        halves = [flux[f, :, h * LANES : (h + 1) * LANES] for h in range(2)]
        ends = (
            pltpu.roll(col_r[0], LANES - f, 1) if f else col_r[0],
            pltpu.roll(col_r[1], LANES - 1 - f, 1),
        )
        to_right = [pltpu.roll(x, 1, 1) for x in halves]
        to_left = [pltpu.roll(x, LANES - 1, 1) for x in halves]
        at_first, at_last = lane_c == 0, lane_c == LANES - 1
        before_y = [jnp.where(at_first, ends[0], to_right[0]), jnp.where(at_first, to_right[0], to_right[1])]
        after_y = [jnp.where(at_last, to_left[1], to_left[0]), jnp.where(at_last, ends[1], to_left[1])]
        for h in range(2):
            x = halves[h]
            above = jnp.where(row_i == 0, row_r[0, h, f : f + 1, :], pltpu.roll(x, 1, 0))
            below = jnp.where(row_i == rows - 1, row_r[1, h, f : f + 1, :], pltpu.roll(x, rows - 1, 0))
            xs[1, h, f * pitch : f * pitch + rows, :] = (below - above) * 0.5
            xs[2, h, f * pitch : f * pitch + rows, :] = (after_y[h] - before_y[h]) * 0.5

    spread(1)
    spread(2)
    for c in bank_copies:
        c.wait()

    def products(p, c):
        got_pair = jnp.dot(xmat[...], bank_v[p], preferred_element_type=jnp.float32)
        prod[pl.ds(2 * p * tiles, tiles)] = got_pair[:, :LANES].reshape(tiles, fields, LANES)
        prod[pl.ds((2 * p + 1) * tiles, tiles)] = got_pair[:, LANES:].reshape(tiles, fields, LANES)
        return c

    lax.fori_loop(0, nwb // 2, products, 0, unroll=2)
    table_copy.wait()

    def record(d, s):
        return prod[jnp.clip(table_s[d, s], 0, nwb * tiles - 1)]

    def fill(d, ref, at):
        for s in range(0, cap, 2):
            pair = jnp.concatenate([record(d, s), record(d, s + 1)], axis=0)
            ref[at, s * fields : (s + 2) * fields, :] = pair.astype(jnp.bfloat16)

    for kind in range(2):

        def send_data(x, j):
            d = parties(kind, x, j)[0]
            fill(d, sent, d)
            data_to(kind, x, j).start()

        half_others(send_data)
        fill(gx * ny + (base if kind else other) + mine_j, got, kind * hn + place)

    diff_in.wait()
    diff_copies = halo_copies(
        4, diff, diff, diff.at[pl.ds(0, 8)], diff.at[pl.ds(orows - 8, 8)], d_edge, d_corner, d_row
    )
    for c in diff_copies:
        c.start()

    cells = fields * otx * oty
    shares = LANES // span
    depth = hn * span
    cell_i = lax.broadcasted_iota(jnp.int32, (cells, LANES), 0).astype(jnp.float32)
    part_lane = lane_of((1, LANES)) // span
    mine_half = gy // hy

    def whole(src_ref, dst_ref, send_sem, recv_sem):
        return pltpu.make_async_remote_copy(
            src_ref=src_ref, dst_ref=dst_ref, send_sem=send_sem, recv_sem=recv_sem,
            device_id=(gx, other + mine_j), device_id_type=MESH,
        )

    meta_all = whole(meta_s.at[pl.ds(0, hn - 1)], meta_r.at[pl.ds(0, hn - 1)], m_send, m_recv)
    meta_all.wait_recv()
    for kind in range(2):
        row = mine_half if kind else 1 - mine_half
        for b in range(depth // LANES):
            aims = meta_r[b * shares, row]
            for i in range(1, shares):
                aims = jnp.where(part_lane == i, meta_r[b * shares + i, row], aims)
            at = kind * depth + b * LANES
            hot[:, at : at + LANES] = jnp.where(cell_i == aims, 1.0, 0.0).astype(jnp.bfloat16)

    def collect(kind):
        ref = got.at[pl.ds(kind * hn, hn - 1)]
        whole(ref, ref, a_send, a_recv.at[kind]).wait_recv()
        data = got[kind * hn : (kind + 1) * hn].reshape(depth, LANES)
        return jnp.dot(hot[:, kind * depth : (kind + 1) * depth], data, preferred_element_type=jnp.float32)

    part_s[...] = collect(0).astype(jnp.bfloat16)
    cross = remote(part_s, part_r, 20, gx, other + mine_j)
    cross.start()
    total = collect(1)
    cross.wait()
    total = total + part_r[...].astype(jnp.float32)
    high = fields * otx
    parts = block_transpose([total[t * high : (t + 1) * high, :] for t in range(oty)], OTILE_Y)
    for a in range(OTILE_X):
        u[pl.ds(a, high, stride=OTILE_X), :] = parts[a]

    lane_o = lane_of((orows, LANES))
    for f in range(fields):
        pack_s[2, f * 8 : f * 8 + 8, :] = u[f * orows : f * orows + 8, :]
        pack_s[3, f * 8 : f * 8 + 8, :] = u[(f + 1) * orows - 8 : (f + 1) * orows, :]
    ocean_copies = halo_copies(
        12,
        pack_s.at[0, pl.ds(0, orows)],
        pack_s.at[1, pl.ds(0, orows)],
        pack_s.at[2, pl.ds(0, fields * 8)],
        pack_s.at[3, pl.ds(0, fields * 8)],
        u_edge, u_corner, u_row,
    )
    for c in ocean_copies[2:4]:
        c.start()
    packed = [jnp.zeros((orows, LANES), jnp.float32) for _ in range(2)]
    for f in range(fields):
        block = u[f * orows : (f + 1) * orows, :]
        shift = f * SWEEPS
        rolled = (pltpu.roll(block, shift, 1), pltpu.roll(block, LANES - shift, 1)) if f else (block, block)
        mine = (lane_o // SWEEPS == f, (LANES - 1 - lane_o) // SWEEPS == f)
        packed = [jnp.where(mine[e], rolled[e], packed[e]) for e in range(2)]
    pack_s[0, 0:orows, :] = packed[0]
    pack_s[1, 0:orows, :] = packed[1]
    for c in ocean_copies[4:] + ocean_copies[:2]:
        c.start()

    meta_all.wait_send()
    ref = sent.at[pl.ds(0, 2 * (hn - 1))]
    whole(ref, ref, a_send, a_recv.at[0]).wait_send()
    for c in diff_copies:
        c.wait()

    has = (gx > 0, gx < nx - 1, gy > 0, gy < ny - 1)
    tail_lane = lane_of((8, LANES)) < LANES // 2
    tail_row = lax.broadcasted_iota(jnp.int32, (8, LANES), 0) < 4
    wide_lane = lane_o < LANES // 2
    row_ok = jnp.where(tail_row, has[1].astype(jnp.float32), has[0].astype(jnp.float32))
    col_ok = jnp.where(wide_lane, has[3].astype(jnp.float32), has[2].astype(jnp.float32))
    both_ok = row_ok * col_ok[0:8]
    d_tail = jnp.where(tail_row, d_row[1], d_row[0]) * row_ok
    d_side = jnp.where(wide_lane, d_edge[1], d_edge[0]) * col_ok
    d_both = (
        jnp.where(
            tail_lane,
            jnp.where(tail_row, d_corner[1, 1], d_corner[0, 1]),
            jnp.where(tail_row, d_corner[1, 0], d_corner[0, 0]),
        )
        * both_ok
    )
    d = [
        jnp.concatenate([diff[...], d_tail], axis=0),
        jnp.concatenate([d_side, d_both], axis=0),
    ]
    for c in ocean_copies:
        c.wait()
    side = [
        jnp.concatenate([u_edge[e], jnp.where(tail_row, u_corner[1, e], u_corner[0, e])], axis=0)
        for e in range(2)
    ]
    ext = orows + 8
    lane_e = lane_of((ext, LANES))
    side_ok = jnp.concatenate([col_ok, both_ok], axis=0)
    at_first, at_last = lane_e == 0, lane_e == LANES - 1
    def opened(f):
        shift = f * SWEEPS
        tail = jnp.where(tail_row, u_row[1, f * 8 : f * 8 + 8, :], u_row[0, f * 8 : f * 8 + 8, :]) * row_ok
        rolled = (
            (pltpu.roll(side[1], LANES - shift, 1), pltpu.roll(side[0], shift, 1)) if f else (side[1], side[0])
        )
        return [
            jnp.concatenate([u[f * orows : (f + 1) * orows, :], tail], axis=0),
            jnp.where(lane_e < LANES // 2, rolled[0], rolled[1]) * side_ok,
        ]

    def swept(x):
        to_right = [pltpu.roll(v, 1, 1) for v in x]
        to_left = [pltpu.roll(v, LANES - 1, 1) for v in x]
        beside = [
            jnp.where(at_first, to_right[1 - h], to_right[h])
            + jnp.where(at_last, to_left[1 - h], to_left[h])
            + pltpu.roll(x[h], 1, 0)
            + pltpu.roll(x[h], ext - 1, 0)
            for h in range(2)
        ]
        return [x[h] + d[h] * (beside[h] - 4.0 * x[h]) for h in range(2)]

    for f in range(0, fields, 4):
        some = [opened(f + i) for i in range(4)]
        for sweep in range(SWEEPS):
            some = [swept(x) for x in some]
        for i, x in enumerate(some):
            out[f + i] = x[0][0:orows, :]


def local(nx, ny, flux, diffusivity, remap_bank, rec_owner, rec_source, rec_target, rec_weight):
    n = nx * ny
    fields, rows, cols = flux.shape
    orows, ocols = diffusivity.shape
    records = rec_owner.shape[0]
    cap = max(2, 2 * records // n)
    nwb = remap_bank.shape[0]
    depth = 3 * TILE_X * TILE_Y
    tiles = rows // TILE_X * (cols // TILE_Y)
    span = cap * fields
    f32, bf16 = jnp.float32, jnp.bfloat16
    v = pltpu.VMEM
    dma = pltpu.SemaphoreType.DMA
    vm = pl.BlockSpec(memory_space=pltpu.VMEM)
    flat = [x.reshape(1, records) for x in (rec_owner, rec_source, rec_target, rec_weight)]
    return pl.pallas_call(
        functools.partial(kernel, nx, ny, cap),
        out_shape=jax.ShapeDtypeStruct((fields, orows, ocols), f32),
        in_specs=[pl.BlockSpec(memory_space=pl.ANY)] * 7,
        out_specs=vm,
        scratch_shapes=[
            v((fields, rows, cols), f32),
            v((orows, ocols), f32),
            v((4, 1, records), jnp.int32),
            dma((9,)),
            v((nwb // 2, depth, 2 * LANES), bf16),
            v((3, 2, (fields + 1) * (rows + 8), LANES), f32),
            v((tiles * fields, depth), bf16),
            v((nwb * tiles, fields, LANES), f32),
            v((n, LANES), jnp.int32),
            pltpu.SMEM((n, LANES), jnp.int32),
            v((n // 2, 2, 1, LANES), f32),
            v((n // 2, 2, 1, LANES), f32),
            v((n, span, LANES), bf16),
            v((n, span, LANES), bf16),
            v((2, 2, fields, LANES), f32),
            v((2, 2, fields, LANES), f32),
            v((2, rows, LANES), f32),
            v((2, rows, LANES), f32),
            v((2, orows, LANES), f32),
            v((2, 2, 8, LANES), f32),
            v((2, 8, LANES), f32),
            v((fields * orows + OTILE_X, LANES), f32),
            v((4, max(orows, fields * 8), LANES), f32),
            v((2, orows, LANES), f32),
            v((2, 2, 8, LANES), f32),
            v((2, fields * 8, LANES), f32),
            v((fields * orows * ocols // LANES, LANES), bf16),
            v((fields * orows * ocols // LANES, LANES), bf16),
            v((fields * orows * ocols // LANES, n * span), bf16),
            dma((2,)), dma,
            dma, dma((2,)), dma, dma,
            dma((21,)), dma((21,)),
        ],
        compiler_params=pltpu.CompilerParams(
            collective_id=0, has_side_effects=True, vmem_limit_bytes=64 * 1024 * 1024 - 128 * 1024
        ),
    )(flux, diffusivity, remap_bank.reshape(nwb // 2, 2, depth, LANES), *flat)


def solution(mesh):
    in_specs = (
        P(None, "gx", "gy"),
        P("gx", "gy"),
        P(),
        P(("gx", "gy")),
        P(("gx", "gy")),
        P(("gx", "gy")),
        P(("gx", "gy")),
    )
    out_specs = P(None, "gx", "gy")
    body = functools.partial(local, mesh.shape["gx"], mesh.shape["gy"])
    return jax.shard_map(body, mesh=mesh, in_specs=in_specs, out_specs=out_specs, check_vma=False)
```
